32 devices in a mesh: wide: 8 (over y, x, core), narrow: 4 (over z).
Axes of the slice: x: 2, y: 2, z: 4, core: 2. Of those that a mesh axis runs over, the one named last changes fastest.
Arguments:
- patches: bfloat16 [16384, 768], P(('wide', 'narrow')), may hold values from -6 to 6
- patch_rows: int32 [16384], P(('wide', 'narrow')), may hold values from 0 to 255
- patch_cols: int32 [16384], P(('wide', 'narrow')), may hold values from 0 to 255
- input_ids: int32 [8192], P(('wide', 'narrow')), may hold values from 0 to 50303
- target_ids: int32 [8192], P(('wide', 'narrow')), may hold values from 0 to 50303
- target_lengths: int32 [8], P('wide'), may hold values from 1 to 1024, 5120 in all
- loss_mask: int32 [8, 1024], P('wide'), may hold values 0 or 1
- master_slabs: float32 [192, 768, 128], P(('wide', 'narrow')), may hold values from -0.21875 to 0.21875
- left_stats: float32 [192, 768, 768], P(('wide', 'narrow'))
- left_roots: float32 [192, 768, 768], P(('wide', 'narrow'))
- right_stats: float32 [192, 128, 128], P(('wide', 'narrow'))
- right_roots: float32 [192, 128, 128], P(('wide', 'narrow'))
- block_slot: int32 [192], replicated, may hold values from 0 to 191, each once
- vocab_table: float32 [50304, 768], P('wide', 'narrow'), may hold values from -6 to 6
- vocab_first: float32 [50304, 768], P('wide', 'narrow'), may hold values from -3.8146973e-06 to 3.8146973e-06
- vocab_second: float32 [50304, 768], P('wide', 'narrow'), may hold values from 3.5626664e-13 to 1.4250666e-12
- small_params: float32 [520, 768], replicated
- small_first: float32 [520, 768], replicated, may hold values from -1.9073486e-05 to 1.9073486e-05
- small_second: float32 [520, 768], replicated, may hold values from 3.5626664e-12 to 1.4250666e-11
- step_count: int32 [], replicated, may hold values from 2 to 20
Outputs:
- loss_sum: float32 [], replicated
- count_total: float32 [], replicated
- master_new: float32 [192, 768, 128], P(('wide', 'narrow'))
- weights_low: bfloat16 [192, 768, 128], P(('wide', 'narrow'))
- slab_grads: float32 [192, 768, 128], P(('wide', 'narrow'))
- left_new: float32 [192, 768, 768], P(('wide', 'narrow'))
- right_new: float32 [192, 128, 128], P(('wide', 'narrow'))
- vocab_new: float32 [50304, 768], P('wide', 'narrow')
- vocab_low: bfloat16 [50304, 768], P('wide', 'narrow')
- vocab_first_new: float32 [50304, 768], P('wide', 'narrow')
- vocab_second_new: float32 [50304, 768], P('wide', 'narrow')
- small_new: float32 [520, 768], replicated
- small_first_new: float32 [520, 768], replicated
- small_second_new: float32 [520, 768], replicated
- grad_norm: float32 [], replicated
The draws below stay inside these ranges and needn't reach their ends.
Inputs may be any that keep to these rules, and one draw needn't show every extreme that they name: `block_slot`: each slot once; its first 174 entries place the blocks, slot s lies on device s // 6 in wide-major order. `target_lengths`: the longest target fills all 1024 slots.
All inputs are finite; a program needn't handle non-finite values. No bound on the sum of `target_lengths` or of `loss_mask` on one device may be relied on, other than what follows from the above.
Results may differ from the reference program's by a relative error of at most 0.0089.
Values may be sent and summed in bfloat16 or wider, within the bound.
No kernel may reach another device: no remote copies, remote signals or barrier semaphores. Data moves between devices by JAX's collectives and lax.ppermute only.
A program may use at most 576 MiB of HBM per device.

```python
import math
import jax
import jax.numpy as jnp
import numpy as np
from jax import lax

D = 768
HEADS = 12
HEAD_DIM = 64
FF = 2048
VOCAB = 50304
POS = 256
PATCHES = 2048
TGT = 1024
SCREENS = 8
COLS = 22272
BW = 128
BLOCKS = 174
SLOTS = 192
SMALL_ROWS = 520
NPARAMS = 56137728


def noisy_identity(key, extent, lowest, highest_level):
    levels = jax.random.uniform(jax.random.fold_in(key, 11), (SLOTS, 1, 1), jnp.float32, lowest, highest_level)
    noises = jax.random.normal(jax.random.fold_in(key, 12), (SLOTS, extent, extent), jnp.float32) * (0.25 / extent ** 0.5)
    return levels * (jnp.eye(extent, dtype=jnp.float32)[None] + noises + jnp.swapaxes(noises, 1, 2))


def draw_left_stats(key, part):
    baseline = 0.0004 * BW / NPARAMS
    return noisy_identity(jax.random.fold_in(key, 1), D, baseline, 4.0 * baseline)


def draw_left_roots(key, part):
    baseline = (0.0004 * BW / NPARAMS) ** (-0.25)
    return noisy_identity(jax.random.fold_in(key, 2), D, 0.7 * baseline, baseline)


def draw_right_stats(key, part):
    baseline = 0.0004 * D / NPARAMS
    return noisy_identity(jax.random.fold_in(key, 3), BW, baseline, 4.0 * baseline)


def draw_right_roots(key, part):
    baseline = (0.0004 * D / NPARAMS) ** (-0.25)
    return noisy_identity(jax.random.fold_in(key, 4), BW, 0.7 * baseline, baseline)


def draw_small_params(key, part):
    tables = 0.25 * jax.random.normal(jax.random.fold_in(key, 5), (2 * POS, D), jnp.float32)
    gain_rows = 1.0 + 0.1 * jax.random.normal(jax.random.fold_in(key, 6), (7, D), jnp.float32)
    bias_row = 0.25 * jax.random.normal(jax.random.fold_in(key, 7), (1, D), jnp.float32)
    return jnp.concatenate([tables, gain_rows, bias_row], axis=0)


def with_ends(entries, own_key, low, top_value):
    shape = entries.shape
    place = [jax.random.randint(jax.random.fold_in(own_key, axis), (), 0, shape[axis]) for axis in range(len(shape))]
    entries = entries.at[tuple(place)].set(low)
    longest = shape.index(max(shape))
    place[longest] = (place[longest] + 1) % shape[longest]
    return entries.at[tuple(place)].set(top_value)


def level_of(rng, dims, cuts, low, top_value):
    def one(dim, parts):
        steps = jax.random.uniform(jax.random.fold_in(jax.random.fold_in(rng, 6), dim), (parts,), jnp.float32, low / len(cuts), top_value / len(cuts))
        return jnp.repeat(jnp.exp(steps), dims[dim] // parts).reshape((-1,) + (1,) * (len(dims) - dim - 1))

    loudness = one(*cuts[0])
    for cut in cuts[1:]:
        loudness = loudness * one(*cut)
    return loudness


def cumulative_ranks(amount, skew):
    portions = [(1 << 20) // math.isqrt(grade ** skew) + 1 for grade in range(1, amount + 1)]
    spread = 1 + sum(portions) // (1 << 30)
    return np.cumsum(np.array([max(1, weight // spread) for weight in portions]))


def ranked(rng, shape, count, skew):
    grid = cumulative_ranks(count, skew)
    ticket = jax.random.randint(jax.random.fold_in(rng, 1), shape, 0, int(grid[count - 1]))
    standing = jnp.searchsorted(jnp.asarray(grid, jnp.int32), ticket, side="right")
    return jax.random.permutation(jax.random.fold_in(rng, 2), count)[standing].astype(jnp.int32)


def profile(number_of, total, reach, skew):
    weights = [(1 << 20) // math.isqrt(rank ** skew) + 1 for rank in range(2, number_of + 1)]
    spare, given = total - reach - (number_of - 1), [1] * (number_of - 1)
    while spare > 0:
        movable = [i for i in range(number_of - 1) if given[i] < reach]
        mass, left = sum([weights[i] for i in movable]), spare
        for i in movable:
            extra = min(reach - given[i], max(1, left * weights[i] // mass), spare)
            given[i] = given[i] + extra
            spare = spare - extra
    return np.array([reach] + given)


def ragged_sizes(key, number_of, total, reach, lean):
    if number_of == 2:
        one = jax.random.randint(key, (), max(1, total - reach), min(reach, total - 1) + 1)
        return jnp.stack([one, total - one])
    sizes = jnp.asarray(profile(number_of, total, reach, lean), jnp.int32)
    couples = (number_of - 1) // 2
    donor, sink = sizes[1:1 + 2 * couples:2], sizes[2:2 + 2 * couples:2]
    room = jnp.minimum(donor - 1, reach - sink)
    passed = jax.random.randint(jax.random.fold_in(key, 1), (couples,), 0, 1 << 20) % (room + 1)
    sizes = sizes.at[1:1 + 2 * couples:2].set(donor - passed).at[2:2 + 2 * couples:2].set(sink + passed)
    return sizes[jax.random.permutation(jax.random.fold_in(key, 2), number_of)]


def noise(rng, dims, deviation, limit, split=(), held_as=jnp.bfloat16):
    loudness = level_of(rng, dims, split, -0.22, 0.18) if split else 1.0
    drawn = jax.random.normal(rng, dims, jnp.float32) * deviation * loudness
    return jnp.minimum(jnp.maximum(drawn, -limit), limit).astype(held_as)


def setup_inputs(seed: int = 0) -> dict:
    arg_keys = jax.random.split(jax.random.key(seed), 21)
    return {
        "patches": noise(arg_keys[0], (SCREENS * PATCHES, D), 1.0, 6.0, ((0, 32),)),
        "patch_rows": with_ends(jax.random.randint(arg_keys[1], (SCREENS * PATCHES,), 0, POS), jax.random.fold_in(arg_keys[1], 1), 0, POS - 1).astype(jnp.int32),
        "patch_cols": with_ends(jax.random.randint(arg_keys[2], (SCREENS * PATCHES,), 0, POS), jax.random.fold_in(arg_keys[2], 1), 0, POS - 1).astype(jnp.int32),
        "input_ids": with_ends(ranked(arg_keys[3], (SCREENS * TGT,), VOCAB, 2), jax.random.fold_in(arg_keys[3], 3), 0, VOCAB - 1).astype(jnp.int32),
        "target_ids": with_ends(ranked(arg_keys[4], (SCREENS * TGT,), VOCAB, 2), jax.random.fold_in(arg_keys[4], 3), 0, VOCAB - 1).astype(jnp.int32),
        "target_lengths": ragged_sizes(arg_keys[5], SCREENS, SCREENS * TGT * 5 // 8, TGT, 2).astype(jnp.int32),
        "loss_mask": with_ends((jax.random.randint(arg_keys[6], (SCREENS, TGT), 0, 4) < 3).astype(jnp.int32), jax.random.fold_in(arg_keys[6], 1), 0, 1),
        "master_slabs": noise(arg_keys[7], (SLOTS, D, BW), D ** -0.5, 0.21875, ((0, 32),), jnp.float32),
        "left_stats": draw_left_stats(jax.random.fold_in(arg_keys[20], 71), 0),
        "left_roots": draw_left_roots(jax.random.fold_in(arg_keys[20], 71), 0),
        "right_stats": draw_right_stats(jax.random.fold_in(arg_keys[20], 71), 0),
        "right_roots": draw_right_roots(jax.random.fold_in(arg_keys[20], 71), 0),
        "block_slot": jax.random.permutation(arg_keys[12], SLOTS).astype(jnp.int32),
        "vocab_table": noise(arg_keys[13], (VOCAB, D), 1.0, 6.0, ((0, 8), (1, 4)), jnp.float32),
        "vocab_first": noise(arg_keys[14], (VOCAB, D), (0.0022 / NPARAMS ** 0.5), 3.814697265625e-06, ((0, 8), (1, 4)), jnp.float32),
        "vocab_second": jnp.clip(jnp.exp(math.log(1.4250665534773499e-12) - 1.3862944 * jax.random.uniform(arg_keys[15], (VOCAB, D), jnp.float32) ** level_of(arg_keys[15], (VOCAB, D), ((0, 8), (1, 4)), -0.2, 0.2)), 3.5626663836933747e-13, 1.4250665534773499e-12),
        "small_params": draw_small_params(jax.random.fold_in(arg_keys[20], 71), 0),
        "small_first": noise(arg_keys[17], (SMALL_ROWS, D), (0.01 / NPARAMS ** 0.5), 1.9073486328125e-05, (), jnp.float32),
        "small_second": jnp.clip(jnp.exp(jax.random.uniform(arg_keys[18], (SMALL_ROWS, D), jnp.float32, math.log(3.5626664379034834e-12), math.log(1.4250665751613933e-11))), 3.5626664379034834e-12, 1.4250665751613933e-11),
        "step_count": jax.random.randint(arg_keys[19], (), 2, 21).astype(jnp.int32),
    }


@jax.custom_vjp
def low(v):
    return lax.optimization_barrier(v.astype(jnp.bfloat16)).astype(jnp.float32)

@jax.custom_vjp
def low_back(v):
    return v

def low_keep(v):
    return (low(v), None)

def low_pass(kept, grad):
    return (grad,)

def back_keep(v):
    return (v, None)

def back_low(kept, grad):
    return (low(grad),)
low.defvjp(low_keep, low_pass)
low_back.defvjp(back_keep, back_low)
highest = lax.Precision.HIGHEST
attn_scale = 0.125
norm_eps = 1e-06
clip_limit = 0.02
stat_decay = 0.5
rate_shampoo = 0.02
rate_adam = 0.5
beta_first = 0.9
beta_second = 0.95
adam_eps = 1e-08
weight_decay = 0.01

def matmul(left, right):
    return jnp.dot(left, right, precision=highest)

def matrix_part(weights, number):
    extents = [D, 3 * D, D, 2 * FF, FF, 3 * D, D, D, 2 * D, D, 2 * FF, FF]
    offset = sum(extents[:number])
    return weights[:, offset:offset + extents[number]]

def rms_norm(values, gain_vec):
    return values * lax.rsqrt(lax.optimization_barrier(jnp.mean(values * values, axis=-1, keepdims=True)) + norm_eps) * gain_vec

def split_heads(values):
    return values.reshape(values.shape[0], HEADS, HEAD_DIM)

def attention(queries, keys_in, values_in, allowed):
    scores = low_back(jnp.einsum('qhd,khd->hqk', split_heads(queries), split_heads(keys_in), precision=highest) * attn_scale)
    scores = jnp.where(allowed[None], scores, -1000000000.0)
    probs_low = low(jax.nn.softmax(scores, axis=-1))
    mixed = jnp.einsum('hqk,khd->qhd', probs_low, split_heads(values_in), precision=highest)
    return mixed.reshape(queries.shape[0], D)

def gated_unit(gate_up):
    return jax.nn.gelu(gate_up[:, :FF], approximate=True) * gate_up[:, FF:]

def feed_forward(stream, gain_vec, w_in, w_back):
    gate_up = low_back(matmul(low(rms_norm(stream, gain_vec)), w_in))
    hidden = low(gated_unit(gate_up))
    return low_back(matmul(hidden, w_back.T))

def encode(weights, small_params, patches, rows_ids, cols_ids):
    gain_rows = small_params[2 * POS:]
    stream_zero = low_back(matmul(patches, matrix_part(weights, 0))) + gain_rows[7] + small_params[rows_ids] + small_params[POS + cols_ids]
    mix_rows = low(low_back(matmul(low(rms_norm(stream_zero, gain_rows[0])), matrix_part(weights, 1))))
    open_mask = jnp.ones((PATCHES, PATCHES), bool)
    mixed_rows = low(low_back(attention(mix_rows[:, :D], mix_rows[:, D:2 * D], mix_rows[:, 2 * D:], open_mask)))
    stream_one = stream_zero + low_back(matmul(mixed_rows, matrix_part(weights, 2)))
    stream_two = stream_one + feed_forward(stream_one, gain_rows[1], matrix_part(weights, 3), matrix_part(weights, 4))
    return rms_norm(stream_two, gain_rows[2])

def decode(weights, embed_table, small_params, encoded, in_ids):
    gain_rows = small_params[2 * POS:]
    stream_zero = embed_table[in_ids]
    mix_rows = low(low_back(matmul(low(rms_norm(stream_zero, gain_rows[3])), matrix_part(weights, 5))))
    causal = jnp.tril(jnp.ones((TGT, TGT), bool))
    mixed_rows = low(low_back(attention(mix_rows[:, :D], mix_rows[:, D:2 * D], mix_rows[:, 2 * D:], causal)))
    stream_one = stream_zero + low_back(matmul(mixed_rows, matrix_part(weights, 6)))
    query_rows = low(low_back(matmul(low(rms_norm(stream_one, gain_rows[4])), matrix_part(weights, 7))))
    pair_rows = low(low_back(matmul(low(encoded), matrix_part(weights, 8))))
    open_mask = jnp.ones((TGT, PATCHES), bool)
    mixed_rows = low(low_back(attention(query_rows, pair_rows[:, :D], pair_rows[:, D:], open_mask)))
    stream_two = stream_one + low_back(matmul(mixed_rows, matrix_part(weights, 9)))
    stream_three = stream_two + feed_forward(stream_two, gain_rows[5], matrix_part(weights, 10), matrix_part(weights, 11))
    return rms_norm(stream_three, gain_rows[6]) * D ** (-0.5)

def screen_loss(weights, embed_table, small_params, screen_item):
    patches, rows_ids, cols_ids, in_ids, tgt_ids, counted = screen_item
    encoded = encode(weights, small_params, patches, rows_ids, cols_ids)
    final_normed = decode(weights, embed_table, small_params, encoded, in_ids)
    logits = low_back(matmul(low(final_normed), embed_table.T))
    log_total = jax.nn.logsumexp(logits, axis=-1)
    target = jnp.take_along_axis(logits, tgt_ids[:, None], axis=1)[:, 0]
    return jnp.sum(counted * (log_total - target))

def adamw(param, moment, second, grad, step_count):
    moment = beta_first * moment + (1 - beta_first) * grad
    second = beta_second * second + (1 - beta_second) * grad * grad
    steps = step_count.astype(jnp.float32)
    m_hat = moment / (1 - jnp.power(beta_first, steps))
    v_hat = second / (1 - jnp.power(beta_second, steps))
    return (param - rate_adam * (m_hat / (jnp.sqrt(v_hat) + adam_eps) + weight_decay * param), moment, second)

def shampoo(slot_item):
    grad, left_stat, left_root, right_stat, right_root, master = slot_item
    left_next = stat_decay * left_stat + (1 - stat_decay) * matmul(grad, grad.T)
    right_next = stat_decay * right_stat + (1 - stat_decay) * matmul(grad.T, grad)
    precond = matmul(matmul(left_root, grad), right_root)
    scale_back = lax.rsqrt(jnp.mean(precond * precond) + norm_eps)
    return (left_next, right_next, master - rate_shampoo * precond * scale_back)

def reference(patches, patch_rows, patch_cols, input_ids, target_ids, target_lengths, loss_mask, master_slabs, left_stats, left_roots, right_stats, right_roots, block_slot, vocab_table, vocab_first, vocab_second, small_params, small_first, small_second, step_count):
    slot_ids = block_slot[:BLOCKS].astype(jnp.int32)
    weights = low(master_slabs)[slot_ids].transpose(1, 0, 2).reshape(D, COLS)
    embed_table = low(vocab_table)
    counted = ((jnp.arange(TGT)[None, :] < target_lengths[:, None]) & (loss_mask == 1)).astype(jnp.float32)
    tokens_counted = jnp.maximum(jnp.sum(counted), 1.0)
    screen_data = (patches.astype(jnp.float32).reshape(SCREENS, PATCHES, D), patch_rows.reshape(SCREENS, PATCHES), patch_cols.reshape(SCREENS, PATCHES), input_ids.reshape(SCREENS, TGT), target_ids.reshape(SCREENS, TGT), counted)

    def total_loss(weights, embed_table, small_params):

        def add_screen(running, screen_item):
            return (running + jax.checkpoint(screen_loss)(weights, embed_table, small_params, screen_item), None)
        summed, _ = lax.scan(add_screen, jnp.zeros((), jnp.float32), screen_data)
        return (summed / tokens_counted, summed)
    loss_mean, pullback, loss_sum = jax.vjp(total_loss, weights, embed_table, small_params, has_aux=True)
    grad_w, grad_e, grad_s = pullback(jnp.ones((), jnp.float32))
    grad_norm = jnp.sqrt(jnp.sum(grad_w * grad_w) + jnp.sum(grad_e * grad_e) + jnp.sum(grad_s * grad_s))
    factor = jnp.minimum(1.0, clip_limit / (grad_norm + 1e-06))
    grad_blocks = grad_w.reshape(D, BLOCKS, BW).transpose(1, 0, 2) * factor
    slab_grads = jnp.zeros((SLOTS, D, BW), grad_blocks.dtype).at[slot_ids].set(grad_blocks)
    left_new, right_new, master_new = lax.map(shampoo, (slab_grads, left_stats, left_roots, right_stats, right_roots, master_slabs))
    vocab_new, vocab_first_new, vocab_second_new = adamw(vocab_table, vocab_first, vocab_second, grad_e * factor, step_count)
    small_new, small_first_new, small_second_new = adamw(small_params, small_first, small_second, grad_s * factor, step_count)
    return (loss_sum, tokens_counted, master_new, master_new.astype(jnp.bfloat16), slab_grads, left_new, right_new, vocab_new, vocab_new.astype(jnp.bfloat16), vocab_first_new, vocab_second_new, small_new, small_first_new, small_second_new, grad_norm)
```

```python
import jax
import jax.numpy as jnp
from jax import lax
from jax.experimental import pallas as pl
from jax.experimental.pallas import tpu as pltpu
from jax.sharding import PartitionSpec as P

HEAD_DIM = 64
D = 768
attn_scale = 0.125
KERNEL_VMEM = 56 * 1024 * 1024


def dot_nt(left, right):
    return lax.dot_general(
        left, right, (((1,), (1,)), ((), ())), preferred_element_type=jnp.float32
    )


def dot_nn(left, right):
    return lax.dot_general(
        left, right, (((1,), (0,)), ((), ())), preferred_element_type=jnp.float32
    )


def dot_tn(left, right):
    return lax.dot_general(
        left, right, (((0,), (0,)), ((), ())), preferred_element_type=jnp.float32
    )


def attend_kernel(masked, row_step, *refs):
    if masked:
        query_pos, key_pos, q_ref, k_ref, v_ref, out_ref, lse_ref = refs
    else:
        q_ref, k_ref, v_ref, out_ref, lse_ref = refs
    keys = k_ref[...]
    values = v_ref[...]
    key_lane = lax.broadcasted_iota(jnp.int32, values.shape, 1) // HEAD_DIM
    lane = lax.broadcasted_iota(jnp.int32, (row_step, 128), 1) // HEAD_DIM
    one = jnp.ones((), values.dtype)
    sides = [jnp.where(key_lane == side, values, one) for side in range(2)]
    for start in range(0, q_ref.shape[0], row_step):
        rows = pl.ds(start, row_step)
        queries = q_ref[rows, :]
        mixed, totals = [], []
        for side in range(2):
            half = jnp.where(lane == side, queries, jnp.zeros((), queries.dtype)) * attn_scale
            scores = dot_nt(half.astype(jnp.bfloat16), keys)
            if masked:
                scores = jnp.where(key_pos[...] <= query_pos[rows, :], scores, -1000000000.0)
            top = jnp.max(scores, axis=1, keepdims=True)
            exponent = jnp.exp(scores - top).astype(jnp.bfloat16)
            both = dot_nn(exponent, sides[side])
            other = (1 - side) * HEAD_DIM
            summed = both[:, other : other + 1]
            mixed.append(both / summed)
            totals.append(top + jnp.log(summed))
        out_ref[rows, :] = jnp.where(lane == 0, mixed[0], mixed[1]).astype(out_ref.dtype)
        lse_ref[rows, :] = jnp.where(lane == 0, totals[0], totals[1])


def attend(queries, keys_values, positions):
    rows, keys = queries.shape[0], keys_values.shape[0]
    pairs = D // 128
    row_step = min(rows, 256)
    extra, extra_specs = (), []
    if positions is not None:
        query_pos, key_pos = positions
        extra = (query_pos.reshape(rows, 1), key_pos.reshape(1, keys))
        extra_specs = [
            pl.BlockSpec((rows, 1), lambda j: (0, 0)),
            pl.BlockSpec((1, keys), lambda j: (0, 0)),
        ]
    return pl.pallas_call(
        lambda *refs: attend_kernel(positions is not None, row_step, *refs),
        grid=(pairs,),
        in_specs=extra_specs
        + [
            pl.BlockSpec((rows, 128), lambda j: (0, j)),
            pl.BlockSpec((keys, 128), lambda j: (0, j)),
            pl.BlockSpec((keys, 128), lambda j: (0, j + pairs)),
        ],
        out_specs=[
            pl.BlockSpec((rows, 128), lambda j: (0, j)),
            pl.BlockSpec((rows, 128), lambda j: (0, j)),
        ],
        out_shape=[
            jax.ShapeDtypeStruct((rows, D), jnp.bfloat16),
            jax.ShapeDtypeStruct((rows, D), jnp.float32),
        ],
        compiler_params=pltpu.CompilerParams(vmem_limit_bytes=KERNEL_VMEM),
        cost_estimate=pl.CostEstimate(
            flops=16 * rows * keys * D,
            bytes_accessed=4 * keys * D + 8 * rows * D,
            transcendentals=rows * keys * 12,
        ),
    )(*extra, queries, keys_values, keys_values)


def attend_back_kernel(masked, key_step, *refs):
    if masked:
        query_pos, key_pos, q_ref, k_ref, v_ref, out_ref, lse_ref, grad_ref, dq_ref, dk_ref, dv_ref = refs
    else:
        q_ref, k_ref, v_ref, out_ref, lse_ref, grad_ref, dq_ref, dk_ref, dv_ref = refs
    queries = q_ref[...]
    grads = grad_ref[...]
    lane = lax.broadcasted_iota(jnp.int32, queries.shape, 1) // HEAD_DIM
    zero = jnp.zeros((), queries.dtype)
    totals = lse_ref[...].T
    weighted = (grads.astype(jnp.float32) * out_ref[...].astype(jnp.float32)).T
    halves, grad_halves, total_rows, delta_rows, grad_queries = [], [], [], [], []
    for side in range(2):
        halves.append((jnp.where(lane == side, queries, zero) * attn_scale).astype(jnp.bfloat16))
        grad_halves.append(jnp.where(lane == side, grads, zero))
        total_rows.append(totals[side * HEAD_DIM : side * HEAD_DIM + 1, :])
        delta_rows.append(
            jnp.sum(weighted[side * HEAD_DIM : (side + 1) * HEAD_DIM, :], axis=0, keepdims=True)
        )
        grad_queries.append(jnp.zeros(queries.shape, jnp.float32))
    for start in range(0, k_ref.shape[0], key_step):
        rows = pl.ds(start, key_step)
        keys = k_ref[rows, :]
        values = v_ref[rows, :]
        grad_keys = jnp.zeros(keys.shape, jnp.float32)
        grad_values = jnp.zeros(keys.shape, jnp.float32)
        for side in range(2):
            scores = dot_nt(keys, halves[side])
            probs = jnp.exp(scores - total_rows[side])
            if masked:
                probs = jnp.where(key_pos[rows, :] <= query_pos[...], probs, 0.0)
            grad_probs = dot_nt(values, grad_halves[side])
            grad_scores = (probs * (grad_probs - delta_rows[side])).astype(jnp.bfloat16)
            grad_values += dot_nn(probs.astype(jnp.bfloat16), grad_halves[side])
            grad_keys += dot_nn(grad_scores, halves[side])
            grad_queries[side] += dot_tn(grad_scores, keys)
        dk_ref[rows, :] = grad_keys.astype(dk_ref.dtype)
        dv_ref[rows, :] = grad_values.astype(dv_ref.dtype)
    dq_ref[...] = (jnp.where(lane == 0, grad_queries[0], grad_queries[1]) * attn_scale).astype(
        dq_ref.dtype
    )


def attend_back(queries, keys_values, positions, mixed_rows, log_total, grad_mixed):
    rows, keys = queries.shape[0], keys_values.shape[0]
    pairs = D // 128
    key_step = min(keys, 512)
    extra, extra_specs = (), []
    if positions is not None:
        query_pos, key_pos = positions
        extra = (query_pos.reshape(1, rows), key_pos.reshape(keys, 1))
        extra_specs = [
            pl.BlockSpec((1, rows), lambda j: (0, 0)),
            pl.BlockSpec((keys, 1), lambda j: (0, 0)),
        ]
    row_spec = pl.BlockSpec((rows, 128), lambda j: (0, j))
    key_spec = pl.BlockSpec((keys, 128), lambda j: (0, j))
    value_spec = pl.BlockSpec((keys, 128), lambda j: (0, j + pairs))
    return pl.pallas_call(
        lambda *refs: attend_back_kernel(positions is not None, key_step, *refs),
        grid=(pairs,),
        in_specs=extra_specs + [row_spec, key_spec, value_spec, row_spec, row_spec, row_spec],
        out_specs=[row_spec, key_spec, key_spec],
        out_shape=[
            jax.ShapeDtypeStruct((rows, D), jnp.bfloat16),
            jax.ShapeDtypeStruct((keys, D), jnp.bfloat16),
            jax.ShapeDtypeStruct((keys, D), jnp.bfloat16),
        ],
        compiler_params=pltpu.CompilerParams(vmem_limit_bytes=KERNEL_VMEM),
        cost_estimate=pl.CostEstimate(
            flops=40 * rows * keys * D,
            bytes_accessed=8 * keys * D + 12 * rows * D,
            transcendentals=rows * keys * 12,
        ),
    )(*extra, queries, keys_values, keys_values, mixed_rows, log_total, grad_mixed)


def head_kernel(vocab, tile, used_ref, rows_ref, table_ref, mixed_ref, exp_ref, stats_ref, logits_ref):
    step = pl.program_id(0)
    padded = table_ref.shape[1]
    shape = (rows_ref.shape[0], 128)
    lane = lax.broadcasted_iota(jnp.int32, shape, 1)

    @pl.when(used_ref[step] == 0)
    def _():
        mixed_ref[...] = jnp.zeros(mixed_ref.shape, mixed_ref.dtype)
        exp_ref[...] = jnp.zeros(exp_ref.shape, exp_ref.dtype)
        stats_ref[...] = jnp.where(lane == 1, 1.0, 0.0)

    @pl.when(used_ref[step] != 0)
    def _():
        rows = rows_ref[...]
        top = jnp.full((rows.shape[0], 1), -jnp.inf, jnp.float32)
        for start in range(0, padded, tile):
            logits = dot_nn(rows, table_ref[:, start : start + tile])
            if start + tile > vocab:
                column = start + lax.broadcasted_iota(jnp.int32, logits.shape, 1)
                logits = jnp.where(column < vocab, logits, -jnp.inf)
            logits_ref[:, start : start + tile] = logits
            top = jnp.maximum(top, jnp.max(logits, axis=1, keepdims=True))
        summed = jnp.zeros((rows.shape[0], 1), jnp.float32)
        mixed = jnp.zeros(mixed_ref.shape, jnp.float32)
        for start in range(0, padded, tile):
            exponent = jnp.exp(logits_ref[:, start : start + tile] - top)
            summed += jnp.sum(exponent, axis=1, keepdims=True)
            low = exponent.astype(jnp.bfloat16)
            exp_ref[:, start : start + tile] = low
            mixed += dot_nt(low, table_ref[:, start : start + tile])
        mixed_ref[...] = mixed
        stats_ref[...] = jnp.where(lane == 0, top, summed)


def head_forward(rows_all, table, used, vocab, block_rows, tile):
    rows, padded = rows_all.shape[0], table.shape[1]
    return pl.pallas_call(
        lambda *refs: head_kernel(vocab, tile, *refs),
        grid_spec=pltpu.PrefetchScalarGridSpec(
            num_scalar_prefetch=1,
            grid=(rows // block_rows,),
            in_specs=[
                pl.BlockSpec((block_rows, D), lambda i, used: (i, 0)),
                pl.BlockSpec((D, padded), lambda i, used: (0, 0), pipeline_mode=pl.Buffered(1)),
            ],
            out_specs=[
                pl.BlockSpec((block_rows, D), lambda i, used: (i, 0)),
                pl.BlockSpec((block_rows, padded), lambda i, used: (i, 0)),
                pl.BlockSpec((block_rows, 128), lambda i, used: (i, 0)),
            ],
            scratch_shapes=[pltpu.VMEM((block_rows, padded), jnp.float32)],
        ),
        out_shape=[
            jax.ShapeDtypeStruct((rows, D), jnp.float32),
            jax.ShapeDtypeStruct((rows, padded), jnp.bfloat16),
            jax.ShapeDtypeStruct((rows, 128), jnp.float32),
        ],
        compiler_params=pltpu.CompilerParams(vmem_limit_bytes=KERNEL_VMEM),
        cost_estimate=pl.CostEstimate(
            flops=4 * rows * padded * D,
            bytes_accessed=2 * rows * padded + 2 * padded * D,
            transcendentals=rows * padded,
        ),
    )(used, rows_all, table)


def table_grad_kernel(tile, used_ref, rows_ref, exp_ref, info_ref, grad_ref, total_ref):
    step = pl.program_id(0)

    @pl.when(step == 0)
    def _():
        total_ref[...] = jnp.zeros(total_ref.shape, total_ref.dtype)

    @pl.when(used_ref[step] != 0)
    def _():
        rows = rows_ref[...]
        scale = info_ref[:, 0:1]
        weight = info_ref[:, 1:2]
        target = info_ref[:, 2:3].astype(jnp.int32)
        for start in range(0, exp_ref.shape[1], tile):
            column = start + lax.broadcasted_iota(jnp.int32, (exp_ref.shape[0], tile), 1)
            probs = exp_ref[:, start : start + tile].astype(jnp.float32) * scale
            hits = jnp.where(column == target, weight, 0.0)
            grad_logits = (probs - hits).astype(jnp.bfloat16)
            total_ref[:, start : start + tile] += dot_tn(rows, grad_logits)

    @pl.when(step == pl.num_programs(0) - 1)
    def _():
        grad_ref[...] = total_ref[...].astype(grad_ref.dtype)


def table_grad(rows_all, exps, info, used, block_rows, tile):
    rows, padded = exps.shape
    return pl.pallas_call(
        lambda *refs: table_grad_kernel(tile, *refs),
        grid_spec=pltpu.PrefetchScalarGridSpec(
            num_scalar_prefetch=1,
            grid=(rows // block_rows,),
            in_specs=[
                pl.BlockSpec((block_rows, D), lambda i, used: (i, 0)),
                pl.BlockSpec((block_rows, padded), lambda i, used: (i, 0)),
                pl.BlockSpec((block_rows, 128), lambda i, used: (i, 0)),
            ],
            out_specs=pl.BlockSpec((D, padded), lambda i, used: (0, 0), pipeline_mode=pl.Buffered(1)),
            scratch_shapes=[pltpu.VMEM((D, padded), jnp.float32)],
        ),
        out_shape=jax.ShapeDtypeStruct((D, padded), jnp.bfloat16),
        compiler_params=pltpu.CompilerParams(vmem_limit_bytes=KERNEL_VMEM),
        cost_estimate=pl.CostEstimate(
            flops=2 * rows * padded * D,
            bytes_accessed=2 * rows * padded + 2 * padded * D,
            transcendentals=0,
        ),
    )(used, rows_all, exps, info)


FF = 2048
POS = 256
TGT = 1024
BW = 128
BLOCKS = 174
EXTENTS = [D, 3 * D, D, 2 * FF, FF, 3 * D, D, D, 2 * D, D, 2 * FF, FF]
GATHERS = [[0, 1], [2, 3, 4], [5, 6, 7, 8], [9, 10, 11]]
SMALL_ROWS = 2 * POS + 8

norm_eps = 1e-06
clip_limit = 0.02
stat_decay = 0.5
rate_shampoo = 0.02
rate_adam = 0.5
beta_first = 0.9
beta_second = 0.95
adam_eps = 1e-08
weight_decay = 0.01
BOTH = ("wide", "narrow")


def rms_norm(values, gain_vec):
    return (
        values * lax.rsqrt(jnp.mean(values * values, axis=-1, keepdims=True) + norm_eps) * gain_vec
    )


def norm_back(values, gain_vec, grad_out):
    _, pullback = jax.vjp(rms_norm, values, gain_vec)
    return pullback(grad_out)


def low(values):
    return values.astype(jnp.bfloat16)


def gated_unit(gate_up):
    return jax.nn.gelu(gate_up[:, :FF], approximate=True) * gate_up[:, FF:]


def swap(values, bit):
    count = lax.axis_size("wide")
    return lax.ppermute(values, "wide", [(w, w ^ bit) for w in range(count)])


def shift(values, step):
    count = lax.axis_size("narrow")
    return lax.ppermute(values, "narrow", [(i, (i + step) % count) for i in range(count)])


def wide_bits():
    return lax.axis_size("wide").bit_length() - 1


def bit_value(level):
    return (lax.axis_index("wide") >> level) & 1


def gather_wide(values, order):
    bits = wide_bits()
    whole = values.reshape((1,) * bits + values.shape)
    for level in order:
        axis = bits - 1 - level
        other = swap(whole, 1 << level)
        mine_last = bit_value(level) == 1
        whole = jnp.where(
            mine_last,
            jnp.concatenate([other, whole], axis=axis),
            jnp.concatenate([whole, other], axis=axis),
        )
    return whole.reshape((1 << bits,) + values.shape)


def scatter_wide(values, order):
    bits = wide_bits()
    rest = values.shape[1:]
    whole = values.reshape((2,) * bits + rest)
    for level in order:
        axis = bits - 1 - level
        bit = bit_value(level)
        mine = lax.dynamic_index_in_dim(whole, bit, axis, keepdims=True)
        theirs = lax.dynamic_index_in_dim(whole, 1 - bit, axis, keepdims=True)
        got = swap(low(theirs), 1 << level)
        whole = low(mine.astype(jnp.float32) + got.astype(jnp.float32))
    return whole.reshape(rest)


def split_orders():
    upper = list(range(1, wide_bits()))
    return upper, upper[::-1]


def gather_wide_fast(values):
    first, second = split_orders()
    half = values.shape[-1] // 2
    return jnp.concatenate(
        [gather_wide(values[..., :half], first + [0]), gather_wide(values[..., half:], second + [0])],
        axis=-1,
    )


def scatter_wide_fast(values):
    first, second = split_orders()
    half = values.shape[-1] // 2
    return jnp.concatenate(
        [scatter_wide(values[..., :half], [0] + first), scatter_wide(values[..., half:], [0] + second)],
        axis=-1,
    )


def group_offsets():
    offsets, bit = [0], lax.axis_size("narrow") // 2
    while bit:
        offsets = offsets + [o ^ bit for o in offsets]
        bit //= 2
    return offsets


def gather_group(rows):
    bit = lax.axis_size("narrow") // 2
    while bit:
        rows = jnp.concatenate([rows, swap(rows, bit)], axis=0)
        bit //= 2
    return rows


def return_group(grads):
    bit = 1
    while bit < lax.axis_size("narrow"):
        half = grads.shape[0] // 2
        got = swap(low(grads[half:]), bit)
        grads = grads[:half].astype(jnp.float32) + got.astype(jnp.float32)
        bit *= 2
    return low(grads)


def feed_forward(stream, gain_vec, w_in, w_back):
    normed = low(rms_norm(stream, gain_vec))
    gate_up = dot_nn(normed, w_in)
    hidden = low(gated_unit(gate_up))
    return (dot_nt(hidden, w_back), (normed, gate_up, hidden))


def feed_back(stream, gain_vec, w_in, w_back, kept_state, grad_out):
    normed, gate_up, hidden = kept_state
    grad_low = low(grad_out)
    grad_w_back = low(dot_tn(grad_low, hidden))
    _, pullback = jax.vjp(gated_unit, gate_up)
    grad_gate_up = low(pullback(dot_nn(grad_low, w_back))[0])
    grad_w_in = low(dot_tn(normed, grad_gate_up))
    grad_stream, grad_gain = norm_back(stream, gain_vec, dot_nt(grad_gate_up, w_in))
    return (grad_stream, grad_gain, grad_w_in, grad_w_back)


def attention_back(queries, keys_values, positions, mixed_rows, log_total, w_out, grad_out):
    grad_low = low(grad_out)
    grad_w_out = low(dot_tn(mixed_rows, grad_low))
    grad_mixed = low(dot_nt(grad_low, w_out))
    grad_query, grad_key, grad_value = attend_back(
        queries, keys_values, positions, mixed_rows, log_total, grad_mixed
    )
    grad_pair = return_group(jnp.concatenate([grad_key, grad_value], axis=1))
    return (grad_w_out, grad_query, grad_pair)


def own_shards(columns):
    return lax.psum_scatter(columns, BOTH, scatter_dimension=0, tiled=True)


def adamw(param, moment, second, grad, step_count):
    moment = beta_first * moment + (1 - beta_first) * grad
    second = beta_second * second + (1 - beta_second) * grad * grad
    steps = step_count.astype(jnp.float32)
    m_hat = moment / (1 - jnp.power(beta_first, steps))
    v_hat = second / (1 - jnp.power(beta_second, steps))
    return (
        param - rate_adam * (m_hat / (jnp.sqrt(v_hat) + adam_eps) + weight_decay * param),
        moment,
        second,
    )


def shards(
    patches,
    patch_rows,
    patch_cols,
    input_ids,
    target_ids,
    target_lengths,
    loss_mask,
    master_slabs,
    left_stats,
    left_roots,
    right_stats,
    right_roots,
    block_slot,
    vocab_table,
    vocab_first,
    vocab_second,
    small_params,
    small_first,
    small_second,
    step_count,
):
    wide_count = lax.axis_size("wide")
    narrow_count = lax.axis_size("narrow")
    devices = wide_count * narrow_count
    screen_sets = wide_count // narrow_count
    wide_pos = lax.axis_index("wide")
    narrow_pos = lax.axis_index("narrow")
    member = wide_pos % narrow_count
    slot_total = block_slot.shape[0]
    own_count = master_slabs.shape[0]
    piece = D // devices
    slot_ids = block_slot[:BLOCKS]
    enc_rows, dec_rows = patches.shape[0], input_ids.shape[0]
    vocab_rows, features = vocab_table.shape

    block_of_slot = (slot_ids[:, None] == jnp.arange(slot_total)[None, :]).astype(jnp.bfloat16)
    pieces = low(master_slabs).reshape(own_count, devices, piece, BW).transpose(1, 0, 2, 3)
    pieces = lax.all_to_all(pieces, BOTH, 0, 0).reshape(slot_total, piece * BW)
    ordered = low(dot_nn(block_of_slot, pieces)).reshape(BLOCKS, piece, BW)
    row_shard = ordered.transpose(1, 0, 2).reshape(piece, BLOCKS * BW)
    weights = [None] * len(EXTENTS)
    for numbers in GATHERS:
        begin = sum(EXTENTS[: numbers[0]])
        size = sum(EXTENTS[n] for n in numbers)
        group = lax.all_gather(row_shard[:, begin : begin + size], BOTH, axis=0, tiled=True)
        for n in numbers:
            offset = sum(EXTENTS[:n]) - begin
            weights[n] = group[:, offset : offset + EXTENTS[n]]

    exchange = []
    for w in range(wide_count):
        for n in range(narrow_count):
            base = w // narrow_count * narrow_count
            exchange.append((w * narrow_count + n, (base + n) * narrow_count + w % narrow_count))
    patches = lax.ppermute(patches, BOTH, exchange)
    whole_ids = lax.ppermute(
        jnp.concatenate([patch_rows, patch_cols, input_ids, target_ids]), BOTH, exchange
    )
    rows_ids, cols_ids = whole_ids[:enc_rows], whole_ids[enc_rows : 2 * enc_rows]
    token_ids = whole_ids[2 * enc_rows :].reshape(2, dec_rows)
    layer_tokens = lax.all_gather(token_ids, "wide", axis=0)
    layer_targets = layer_tokens[:, 1].reshape(-1)
    every_input = lax.all_gather(layer_tokens, "narrow", axis=1)
    screens_info = lax.all_gather(
        jnp.concatenate([target_lengths[:, None], loss_mask], axis=1), "wide", axis=0, tiled=True
    )
    counted = (
        (jnp.arange(TGT)[None, :] < screens_info[:, :1]) & (screens_info[:, 1:] == 1)
    ).astype(jnp.float32)
    tokens_counted = jnp.maximum(jnp.sum(counted), 1.0)
    row_counted = lax.dynamic_index_in_dim(
        counted.reshape(screen_sets, narrow_count, TGT), narrow_pos, 1, keepdims=False
    ).reshape(-1)
    own_counted = lax.dynamic_slice_in_dim(row_counted, wide_pos * dec_rows, dec_rows)

    padded = -(-vocab_rows // 256) * 256
    table_low = low(vocab_table)
    columns = jnp.arange(vocab_rows)
    vocab_start = wide_pos * vocab_rows
    flat_inputs = every_input[:, :, 0].reshape(-1) - vocab_start
    flat_targets = every_input[:, :, 1].reshape(-1) - vocab_start

    def looked_up(ids):
        onehot = (ids[:, None] == columns[None, :]).astype(jnp.bfloat16)
        found = low(dot_nn(onehot, table_low)).reshape(wide_count, narrow_count * dec_rows, features)
        found = scatter_wide(found, list(range(wide_bits())))
        found = lax.all_to_all(found.reshape(narrow_count, dec_rows, features), "narrow", 0, 0)
        return found.transpose(1, 0, 2).reshape(dec_rows, D)

    stream_dec = looked_up(flat_inputs).astype(jnp.float32)
    target_rows = looked_up(flat_targets).astype(jnp.float32)
    table_parts = [jnp.pad(table_low.T, ((0, 0), (0, padded - vocab_rows)))]
    for _ in range(narrow_count - 1):
        table_parts.append(shift(table_parts[-1], -1))
    table = jnp.concatenate(table_parts, axis=0)

    gain_rows = small_params[2 * POS :]
    picked = jnp.concatenate(
        [
            rows_ids[:, None] == jnp.arange(POS)[None, :],
            cols_ids[:, None] == jnp.arange(POS)[None, :],
        ],
        axis=1,
    ).astype(jnp.bfloat16)
    tables = small_params[: 2 * POS]
    tables_high = low(tables)
    tables_rest = low(tables - tables_high.astype(jnp.float32))
    enc_zero = (
        dot_nn(patches, weights[0])
        + gain_rows[7]
        + dot_nn(picked, tables_high)
        + dot_nn(picked, tables_rest)
    )
    enc_normed = low(rms_norm(enc_zero, gain_rows[0]))
    enc_mix = low(dot_nn(enc_normed, weights[1]))
    enc_keys = gather_group(enc_mix[:, D:])
    enc_mixed, enc_total = attend(enc_mix[:, :D], enc_keys, None)
    enc_one = enc_zero + dot_nn(enc_mixed, weights[2])
    branch, enc_ffn = feed_forward(enc_one, gain_rows[1], weights[3], weights[4])
    enc_two = enc_one + branch
    encoded = low(rms_norm(enc_two, gain_rows[2]))

    query_pos = (member * dec_rows + jnp.arange(dec_rows)).astype(jnp.int32)
    key_pos = jnp.concatenate(
        [(member ^ offset) * dec_rows + jnp.arange(dec_rows) for offset in group_offsets()]
    ).astype(jnp.int32)
    causal = (query_pos, key_pos)
    dec_zero = stream_dec
    dec_normed = low(rms_norm(dec_zero, gain_rows[3]))
    dec_mix = low(dot_nn(dec_normed, weights[5]))
    self_keys = gather_group(dec_mix[:, D:])
    self_mixed, self_total = attend(dec_mix[:, :D], self_keys, causal)
    dec_one = dec_zero + dot_nn(self_mixed, weights[6])
    cross_normed = low(rms_norm(dec_one, gain_rows[4]))
    cross_query = low(dot_nn(cross_normed, weights[7]))
    cross_keys = gather_group(low(dot_nn(encoded, weights[8])))
    cross_mixed, cross_total = attend(cross_query, cross_keys, None)
    dec_two = dec_one + dot_nn(cross_mixed, weights[9])
    branch, dec_ffn = feed_forward(dec_two, gain_rows[5], weights[10], weights[11])
    dec_three = dec_two + branch
    final = low(rms_norm(dec_three, gain_rows[6]) * D ** (-0.5))

    rotated = lax.dynamic_slice_in_dim(
        jnp.concatenate([final, final], axis=1), narrow_pos * features, D, axis=1
    )
    rows_all = gather_wide_fast(rotated).reshape(-1, D)
    total_rows = rows_all.shape[0]
    block_rows = 256
    used = jnp.any(row_counted.reshape(-1, block_rows) != 0, axis=1).astype(jnp.int32)
    tile = padded // 5 if padded % 640 == 0 else 256
    mixed, exps, stats = head_forward(rows_all, table, used, vocab_rows, block_rows, tile)
    top_part, summed_part = stats[:, 0], stats[:, 1]
    stats_all = lax.all_gather(jnp.stack([top_part, summed_part]), "wide", axis=0)
    top_logit = jnp.max(stats_all[:, 0], axis=0)
    summed = jnp.sum(stats_all[:, 1] * jnp.exp(stats_all[:, 0] - top_logit), axis=0)
    log_total = top_logit + jnp.log(summed)
    row_weight = row_counted / tokens_counted
    scale = row_weight * jnp.exp(top_part - log_total)
    grad_rows = (mixed * scale[:, None]).reshape(wide_count, dec_rows, D)
    grad_back = scatter_wide_fast(grad_rows).astype(jnp.float32)
    grad_back = lax.dynamic_slice_in_dim(
        jnp.concatenate([grad_back, grad_back], axis=1), (D - narrow_pos * features) % D, D, axis=1
    )
    own_weight = own_counted / tokens_counted
    grad_final = grad_back - own_weight[:, None] * target_rows
    target_logit = jnp.sum(final.astype(jnp.float32) * target_rows, axis=1)
    own_total = lax.dynamic_slice_in_dim(log_total, wide_pos * dec_rows, dec_rows)
    loss_local = jnp.sum(own_counted * (own_total - target_logit))
    target_cols = (layer_targets - vocab_start).astype(jnp.float32)
    info = jnp.concatenate(
        [
            jnp.stack([scale, row_weight, target_cols], axis=1),
            jnp.zeros((total_rows, 125), jnp.float32),
        ],
        axis=1,
    )
    grad_table = table_grad(rows_all, exps, info, used, block_rows, tile)
    grad_parts = grad_table.reshape(narrow_count, features, padded)
    moving = grad_parts[narrow_count - 1]
    for k in range(narrow_count - 2, -1, -1):
        moving = grad_parts[k].astype(jnp.float32) + shift(low(moving), 1).astype(jnp.float32)
    head_grad = moving[:, :vocab_rows].T

    grad_three, gain_final = norm_back(dec_three, gain_rows[6], grad_final * D ** (-0.5))
    grad_two, gain_dffn, grad_in, grad_out = feed_back(
        dec_two, gain_rows[5], weights[10], weights[11], dec_ffn, grad_three
    )
    shard_dffn = own_shards(jnp.concatenate([grad_in, grad_out], axis=1))
    grad_two = grad_two + grad_three
    grad_cout, grad_query, grad_pair = attention_back(
        cross_query, cross_keys, None, cross_mixed, cross_total, weights[9], grad_two
    )
    grad_cq = low(dot_tn(cross_normed, grad_query))
    grad_one, gain_cross = norm_back(dec_one, gain_rows[4], dot_nt(grad_query, weights[7]))
    grad_one = grad_one + grad_two
    grad_ckv = low(dot_tn(encoded, grad_pair))
    grad_encoded = dot_nt(grad_pair, weights[8])
    grad_so, grad_query, grad_pair = attention_back(
        dec_mix[:, :D], self_keys, causal, self_mixed, self_total, weights[6], grad_one
    )
    grad_mix = jnp.concatenate([grad_query, grad_pair], axis=1)
    grad_sqkv = low(dot_tn(dec_normed, grad_mix))
    shard_dattn = own_shards(
        jnp.concatenate([grad_sqkv, grad_so, grad_cq, grad_ckv, grad_cout], axis=1)
    )
    grad_zero, gain_self = norm_back(dec_zero, gain_rows[3], dot_nt(grad_mix, weights[5]))
    grad_tokens = low(grad_zero + grad_one)

    sent = grad_tokens.reshape(dec_rows, narrow_count, features).transpose(1, 0, 2)
    sent = lax.all_to_all(sent, "narrow", 0, 0).reshape(narrow_count * dec_rows, features)
    sent = gather_wide(sent, list(range(wide_bits()))[::-1]).reshape(-1, features)
    onehot = (flat_inputs[:, None] == columns[None, :]).astype(jnp.bfloat16)
    vocab_grad = head_grad + dot_tn(onehot, sent)

    grad_two, gain_efinal = norm_back(enc_two, gain_rows[2], grad_encoded)
    grad_one, gain_effn, grad_in, grad_out = feed_back(
        enc_one, gain_rows[1], weights[3], weights[4], enc_ffn, grad_two
    )
    shard_effn = own_shards(jnp.concatenate([grad_in, grad_out], axis=1))
    grad_one = grad_one + grad_two
    grad_eo, grad_query, grad_pair = attention_back(
        enc_mix[:, :D], enc_keys, None, enc_mixed, enc_total, weights[2], grad_one
    )
    grad_mix = jnp.concatenate([grad_query, grad_pair], axis=1)
    grad_eqkv = low(dot_tn(enc_normed, grad_mix))
    grad_zero, gain_eattn = norm_back(enc_zero, gain_rows[0], dot_nt(grad_mix, weights[1]))
    grad_zero = grad_zero + grad_one
    grad_patch = low(dot_tn(patches, low(grad_zero)))
    grad_tables = dot_tn(low(grad_zero), picked)
    gains = [gain_eattn, gain_effn, gain_efinal, gain_self, gain_cross, gain_dffn, gain_final]
    grad_small = low(
        jnp.concatenate(
            [grad_tables, jnp.stack(gains + [jnp.sum(grad_zero, axis=0)], axis=1)], axis=1
        )
    )
    filler = jnp.zeros((D, -SMALL_ROWS % BW), jnp.bfloat16)
    shard_eattn = own_shards(
        jnp.concatenate([grad_patch, grad_eqkv, grad_eo, grad_small, filler], axis=1)
    )

    projection = shard_eattn[:, : 5 * D]
    small_shard = shard_eattn[:, 5 * D : 5 * D + SMALL_ROWS].astype(jnp.float32)
    grads = jnp.concatenate([projection, shard_effn, shard_dattn, shard_dffn], axis=1)
    partial_square = (
        jnp.sum(jnp.square(grads.astype(jnp.float32)))
        + jnp.sum(vocab_grad * vocab_grad)
        + jnp.sum(small_shard * small_shard)
    )
    scalars = jnp.where(
        jnp.arange(SMALL_ROWS)[None, :] == 0,
        partial_square,
        jnp.where(jnp.arange(SMALL_ROWS)[None, :] == 1, loss_local, 0.0),
    )
    shared = lax.all_gather(
        jnp.concatenate([small_shard, scalars], axis=0), BOTH, axis=0
    )
    small_grad = shared[:, :piece].reshape(D, SMALL_ROWS).T
    total_square = jnp.sum(shared[:, piece, 0])
    loss_sum = jnp.sum(shared[:, piece, 1])
    slotted = grads.reshape(piece, BLOCKS, BW).transpose(1, 0, 2).reshape(BLOCKS, piece * BW)
    slotted = low(dot_tn(block_of_slot, slotted)).reshape(devices, own_count, piece, BW)
    slab = lax.all_to_all(slotted, BOTH, 0, 0).transpose(1, 0, 2, 3).reshape(own_count, D, BW)

    grad_norm = jnp.sqrt(total_square)
    factor = jnp.minimum(1.0, clip_limit / (grad_norm + 1e-06))
    kept = (1 - stat_decay) * factor * factor
    slab_grad = slab.astype(jnp.float32) * factor
    left_new = stat_decay * left_stats + kept * jnp.einsum(
        "sik,sjk->sij", slab, slab, preferred_element_type=jnp.float32
    )
    right_new = stat_decay * right_stats + kept * jnp.einsum(
        "ski,skj->sij", slab, slab, preferred_element_type=jnp.float32
    )
    rooted = jnp.einsum("sij,sjk->sik", low(left_roots), slab, preferred_element_type=jnp.float32)
    precond = factor * jnp.einsum(
        "sij,sjk->sik", rooted, right_roots, precision=lax.Precision.HIGHEST
    )
    scale_back = lax.rsqrt(jnp.mean(precond * precond, axis=(1, 2), keepdims=True) + norm_eps)
    master_new = master_slabs - rate_shampoo * precond * scale_back
    vocab_new, vocab_first_new, vocab_second_new = adamw(
        vocab_table, vocab_first, vocab_second, vocab_grad * factor, step_count
    )
    small_new, small_first_new, small_second_new = adamw(
        small_params, small_first, small_second, small_grad * factor, step_count
    )
    return (
        loss_sum,
        tokens_counted,
        master_new,
        master_new.astype(jnp.bfloat16),
        slab_grad,
        left_new,
        right_new,
        vocab_new,
        vocab_new.astype(jnp.bfloat16),
        vocab_first_new,
        vocab_second_new,
        small_new,
        small_first_new,
        small_second_new,
        grad_norm,
    )


def solution(mesh):
    in_specs = (
        P(("wide", "narrow"), None),
        P(("wide", "narrow")),
        P(("wide", "narrow")),
        P(("wide", "narrow")),
        P(("wide", "narrow")),
        P("wide"),
        P("wide", None),
        P(("wide", "narrow"), None, None),
        P(("wide", "narrow"), None, None),
        P(("wide", "narrow"), None, None),
        P(("wide", "narrow"), None, None),
        P(("wide", "narrow"), None, None),
        P(),
        P("wide", "narrow"),
        P("wide", "narrow"),
        P("wide", "narrow"),
        P(),
        P(),
        P(),
        P(),
    )
    out_specs = (
        P(),
        P(),
        P(("wide", "narrow"), None, None),
        P(("wide", "narrow"), None, None),
        P(("wide", "narrow"), None, None),
        P(("wide", "narrow"), None, None),
        P(("wide", "narrow"), None, None),
        P("wide", "narrow"),
        P("wide", "narrow"),
        P("wide", "narrow"),
        P("wide", "narrow"),
        P(),
        P(),
        P(),
        P(),
    )
    return jax.shard_map(shards, mesh=mesh, in_specs=in_specs, out_specs=out_specs, check_vma=False)
```

```python
import jax
import jax.numpy as jnp
from jax import lax
from jax.experimental import pallas as pl
from jax.experimental.pallas import tpu as pltpu
from jax.sharding import PartitionSpec as P

HEAD_DIM = 64
D = 768
attn_scale = 0.125
KERNEL_VMEM = 56 * 1024 * 1024


def dot_nt(left, right):
    return lax.dot_general(
        left, right, (((1,), (1,)), ((), ())), preferred_element_type=jnp.float32
    )


def dot_nn(left, right):
    return lax.dot_general(
        left, right, (((1,), (0,)), ((), ())), preferred_element_type=jnp.float32
    )


def dot_tn(left, right):
    return lax.dot_general(
        left, right, (((0,), (0,)), ((), ())), preferred_element_type=jnp.float32
    )


def attend_kernel(masked, row_step, *refs):
    if masked:
        query_pos, key_pos, q_ref, k_ref, v_ref, out_ref, lse_ref = refs
    else:
        q_ref, k_ref, v_ref, out_ref, lse_ref = refs
    keys = k_ref[...]
    values = v_ref[...]
    key_lane = lax.broadcasted_iota(jnp.int32, values.shape, 1) // HEAD_DIM
    lane = lax.broadcasted_iota(jnp.int32, (row_step, 128), 1) // HEAD_DIM
    one = jnp.ones((), values.dtype)
    sides = [jnp.where(key_lane == side, values, one) for side in range(2)]
    for start in range(0, q_ref.shape[0], row_step):
        rows = pl.ds(start, row_step)
        queries = q_ref[rows, :]
        mixed, totals = [], []
        for side in range(2):
            half = jnp.where(lane == side, queries, jnp.zeros((), queries.dtype)) * attn_scale
            scores = dot_nt(half.astype(jnp.bfloat16), keys)
            if masked:
                scores = jnp.where(key_pos[...] <= query_pos[rows, :], scores, -1000000000.0)
            top = jnp.max(scores, axis=1, keepdims=True)
            exponent = jnp.exp(scores - top).astype(jnp.bfloat16)
            both = dot_nn(exponent, sides[side])
            other = (1 - side) * HEAD_DIM
            summed = both[:, other : other + 1]
            mixed.append(both / summed)
            totals.append(top + jnp.log(summed))
        out_ref[rows, :] = jnp.where(lane == 0, mixed[0], mixed[1]).astype(out_ref.dtype)
        lse_ref[rows, :] = jnp.where(lane == 0, totals[0], totals[1])


def attend(queries, keys_values, positions):
    rows, keys = queries.shape[0], keys_values.shape[0]
    pairs = D // 128
    row_step = min(rows, 256)
    extra, extra_specs = (), []
    if positions is not None:
        query_pos, key_pos = positions
        extra = (query_pos.reshape(rows, 1), key_pos.reshape(1, keys))
        extra_specs = [
            pl.BlockSpec((rows, 1), lambda j: (0, 0)),
            pl.BlockSpec((1, keys), lambda j: (0, 0)),
        ]
    return pl.pallas_call(
        lambda *refs: attend_kernel(positions is not None, row_step, *refs),
        grid=(pairs,),
        in_specs=extra_specs
        + [
            pl.BlockSpec((rows, 128), lambda j: (0, j)),
            pl.BlockSpec((keys, 128), lambda j: (0, j)),
            pl.BlockSpec((keys, 128), lambda j: (0, j + pairs)),
        ],
        out_specs=[
            pl.BlockSpec((rows, 128), lambda j: (0, j)),
            pl.BlockSpec((rows, 128), lambda j: (0, j)),
        ],
        out_shape=[
            jax.ShapeDtypeStruct((rows, D), jnp.bfloat16),
            jax.ShapeDtypeStruct((rows, D), jnp.float32),
        ],
        compiler_params=pltpu.CompilerParams(vmem_limit_bytes=KERNEL_VMEM),
        cost_estimate=pl.CostEstimate(
            flops=16 * rows * keys * D,
            bytes_accessed=4 * keys * D + 8 * rows * D,
            transcendentals=rows * keys * 12,
        ),
    )(*extra, queries, keys_values, keys_values)


def attend_back_kernel(masked, key_step, *refs):
    if masked:
        query_pos, key_pos, q_ref, k_ref, v_ref, out_ref, lse_ref, grad_ref, dq_ref, dk_ref, dv_ref = refs
    else:
        q_ref, k_ref, v_ref, out_ref, lse_ref, grad_ref, dq_ref, dk_ref, dv_ref = refs
    queries = q_ref[...]
    grads = grad_ref[...]
    lane = lax.broadcasted_iota(jnp.int32, queries.shape, 1) // HEAD_DIM
    zero = jnp.zeros((), queries.dtype)
    totals = lse_ref[...].T
    weighted = (grads.astype(jnp.float32) * out_ref[...].astype(jnp.float32)).T
    halves, grad_halves, total_rows, delta_rows, grad_queries = [], [], [], [], []
    for side in range(2):
        halves.append((jnp.where(lane == side, queries, zero) * attn_scale).astype(jnp.bfloat16))
        grad_halves.append(jnp.where(lane == side, grads, zero))
        total_rows.append(totals[side * HEAD_DIM : side * HEAD_DIM + 1, :])
        delta_rows.append(
            jnp.sum(weighted[side * HEAD_DIM : (side + 1) * HEAD_DIM, :], axis=0, keepdims=True)
        )
        grad_queries.append(jnp.zeros(queries.shape, jnp.float32))
    for start in range(0, k_ref.shape[0], key_step):
        rows = pl.ds(start, key_step)
        keys = k_ref[rows, :]
        values = v_ref[rows, :]
        grad_keys = jnp.zeros(keys.shape, jnp.float32)
        grad_values = jnp.zeros(keys.shape, jnp.float32)
        for side in range(2):
            scores = dot_nt(keys, halves[side])
            probs = jnp.exp(scores - total_rows[side])
            if masked:
                probs = jnp.where(key_pos[rows, :] <= query_pos[...], probs, 0.0)
            grad_probs = dot_nt(values, grad_halves[side])
            grad_scores = (probs * (grad_probs - delta_rows[side])).astype(jnp.bfloat16)
            grad_values += dot_nn(probs.astype(jnp.bfloat16), grad_halves[side])
            grad_keys += dot_nn(grad_scores, halves[side])
            grad_queries[side] += dot_tn(grad_scores, keys)
        dk_ref[rows, :] = grad_keys.astype(dk_ref.dtype)
        dv_ref[rows, :] = grad_values.astype(dv_ref.dtype)
    dq_ref[...] = (jnp.where(lane == 0, grad_queries[0], grad_queries[1]) * attn_scale).astype(
        dq_ref.dtype
    )


def attend_back(queries, keys_values, positions, mixed_rows, log_total, grad_mixed):
    rows, keys = queries.shape[0], keys_values.shape[0]
    pairs = D // 128
    key_step = min(keys, 512)
    extra, extra_specs = (), []
    if positions is not None:
        query_pos, key_pos = positions
        extra = (query_pos.reshape(1, rows), key_pos.reshape(keys, 1))
        extra_specs = [
            pl.BlockSpec((1, rows), lambda j: (0, 0)),
            pl.BlockSpec((keys, 1), lambda j: (0, 0)),
        ]
    row_spec = pl.BlockSpec((rows, 128), lambda j: (0, j))
    key_spec = pl.BlockSpec((keys, 128), lambda j: (0, j))
    value_spec = pl.BlockSpec((keys, 128), lambda j: (0, j + pairs))
    return pl.pallas_call(
        lambda *refs: attend_back_kernel(positions is not None, key_step, *refs),
        grid=(pairs,),
        in_specs=extra_specs + [row_spec, key_spec, value_spec, row_spec, row_spec, row_spec],
        out_specs=[row_spec, key_spec, key_spec],
        out_shape=[
            jax.ShapeDtypeStruct((rows, D), jnp.bfloat16),
            jax.ShapeDtypeStruct((keys, D), jnp.bfloat16),
            jax.ShapeDtypeStruct((keys, D), jnp.bfloat16),
        ],
        compiler_params=pltpu.CompilerParams(vmem_limit_bytes=KERNEL_VMEM),
        cost_estimate=pl.CostEstimate(
            flops=40 * rows * keys * D,
            bytes_accessed=8 * keys * D + 12 * rows * D,
            transcendentals=rows * keys * 12,
        ),
    )(*extra, queries, keys_values, keys_values, mixed_rows, log_total, grad_mixed)


def head_kernel(vocab, tile, parts, used_ref, rows_ref, *refs):
    part_refs, refs = refs[:parts], refs[parts:]
    mixed_ref, exp_ref, stats_ref, logits_ref, table_ref, arrived = refs
    step = pl.program_id(0)
    padded = table_ref.shape[1]
    shape = (rows_ref.shape[0], 128)
    lane = lax.broadcasted_iota(jnp.int32, shape, 1)

    @pl.when(step == 0)
    def _():
        height = D // parts
        copies = [
            pltpu.make_async_copy(
                part, table_ref.at[pl.ds(k * height, height), :], arrived.at[k]
            )
            for k, part in enumerate(part_refs)
        ]
        for copy in copies:
            copy.start()
        for copy in copies:
            copy.wait()

    @pl.when(used_ref[step] == 0)
    def _():
        mixed_ref[...] = jnp.zeros(mixed_ref.shape, mixed_ref.dtype)
        exp_ref[...] = jnp.zeros(exp_ref.shape, exp_ref.dtype)
        stats_ref[...] = jnp.where(lane == 1, 1.0, 0.0)

    @pl.when(used_ref[step] != 0)
    def _():
        rows = rows_ref[...]
        top = jnp.full((rows.shape[0], 1), -jnp.inf, jnp.float32)
        for start in range(0, padded, tile):
            logits = dot_nn(rows, table_ref[:, start : start + tile])
            if start + tile > vocab:
                column = start + lax.broadcasted_iota(jnp.int32, logits.shape, 1)
                logits = jnp.where(column < vocab, logits, -jnp.inf)
            logits_ref[:, start : start + tile] = logits
            top = jnp.maximum(top, jnp.max(logits, axis=1, keepdims=True))
        summed = jnp.zeros((rows.shape[0], 1), jnp.float32)
        mixed = jnp.zeros(mixed_ref.shape, jnp.float32)
        for start in range(0, padded, tile):
            exponent = jnp.exp(logits_ref[:, start : start + tile] - top)
            summed += jnp.sum(exponent, axis=1, keepdims=True)
            lowered = exponent.astype(jnp.bfloat16)
            exp_ref[:, start : start + tile] = lowered
            mixed += dot_nt(lowered, table_ref[:, start : start + tile])
        mixed_ref[...] = mixed
        stats_ref[...] = jnp.where(lane == 0, top, summed)


def head_forward(rows_all, table_parts, used, vocab, block_rows, tile):
    rows, padded, parts = rows_all.shape[0], table_parts[0].shape[1], len(table_parts)
    return pl.pallas_call(
        lambda *refs: head_kernel(vocab, tile, parts, *refs),
        grid_spec=pltpu.PrefetchScalarGridSpec(
            num_scalar_prefetch=1,
            grid=(rows // block_rows,),
            in_specs=[pl.BlockSpec((block_rows, D), lambda i, used: (i, 0))]
            + [pl.BlockSpec(memory_space=pl.ANY)] * parts,
            out_specs=[
                pl.BlockSpec((block_rows, D), lambda i, used: (i, 0)),
                pl.BlockSpec((block_rows, padded), lambda i, used: (i, 0)),
                pl.BlockSpec((block_rows, 128), lambda i, used: (i, 0)),
            ],
            scratch_shapes=[
                pltpu.VMEM((block_rows, padded), jnp.float32),
                pltpu.VMEM((D, padded), jnp.bfloat16),
                pltpu.SemaphoreType.DMA((parts,)),
            ],
        ),
        out_shape=[
            jax.ShapeDtypeStruct((rows, D), jnp.float32),
            jax.ShapeDtypeStruct((rows, padded), jnp.bfloat16),
            jax.ShapeDtypeStruct((rows, 128), jnp.float32),
        ],
        compiler_params=pltpu.CompilerParams(vmem_limit_bytes=KERNEL_VMEM),
        cost_estimate=pl.CostEstimate(
            flops=4 * rows * padded * D,
            bytes_accessed=2 * rows * padded + 2 * padded * D,
            transcendentals=rows * padded,
        ),
    )(used, rows_all, *table_parts)


def table_grad_kernel(tile, used_ref, rows_ref, exp_ref, info_ref, grad_ref, total_ref):
    step = pl.program_id(0)

    @pl.when(step == 0)
    def _():
        total_ref[...] = jnp.zeros(total_ref.shape, total_ref.dtype)

    @pl.when(used_ref[step] != 0)
    def _():
        rows = rows_ref[...]
        scale = info_ref[:, 0:1]
        weight = info_ref[:, 1:2]
        target = info_ref[:, 2:3].astype(jnp.int32)
        for start in range(0, exp_ref.shape[1], tile):
            column = start + lax.broadcasted_iota(jnp.int32, (exp_ref.shape[0], tile), 1)
            probs = exp_ref[:, start : start + tile].astype(jnp.float32) * scale
            hits = jnp.where(column == target, weight, 0.0)
            grad_logits = (probs - hits).astype(jnp.bfloat16)
            total_ref[:, start : start + tile] += dot_tn(rows, grad_logits)

    @pl.when(step == pl.num_programs(0) - 1)
    def _():
        grad_ref[...] = total_ref[...].astype(grad_ref.dtype)


def table_grad(rows_all, exps, info, used, block_rows, tile):
    rows, padded = exps.shape
    return pl.pallas_call(
        lambda *refs: table_grad_kernel(tile, *refs),
        grid_spec=pltpu.PrefetchScalarGridSpec(
            num_scalar_prefetch=1,
            grid=(rows // block_rows,),
            in_specs=[
                pl.BlockSpec((block_rows, D), lambda i, used: (i, 0)),
                pl.BlockSpec((block_rows, padded), lambda i, used: (i, 0)),
                pl.BlockSpec((block_rows, 128), lambda i, used: (i, 0)),
            ],
            out_specs=pl.BlockSpec((D, padded), lambda i, used: (0, 0), pipeline_mode=pl.Buffered(1)),
            scratch_shapes=[pltpu.VMEM((D, padded), jnp.float32)],
        ),
        out_shape=jax.ShapeDtypeStruct((D, padded), jnp.bfloat16),
        compiler_params=pltpu.CompilerParams(vmem_limit_bytes=KERNEL_VMEM),
        cost_estimate=pl.CostEstimate(
            flops=2 * rows * padded * D,
            bytes_accessed=2 * rows * padded + 2 * padded * D,
            transcendentals=0,
        ),
    )(used, rows_all, exps, info)


FF = 2048
POS = 256
TGT = 1024
BW = 128
BLOCKS = 174
EXTENTS = [D, 3 * D, D, 2 * FF, FF, 3 * D, D, D, 2 * D, D, 2 * FF, FF]
GATHERS = [[0, 1], [5, 6, 7, 8], [9, 10, 11]]
PERMUTED = [2, 3, 4]
SMALL_ROWS = 2 * POS + 8

norm_eps = 1e-06
clip_limit = 0.02
stat_decay = 0.5
rate_shampoo = 0.02
rate_adam = 0.5
beta_first = 0.9
beta_second = 0.95
adam_eps = 1e-08
weight_decay = 0.01
BOTH = ("wide", "narrow")


def rms_norm(values, gain_vec):
    return (
        values * lax.rsqrt(jnp.mean(values * values, axis=-1, keepdims=True) + norm_eps) * gain_vec
    )


def norm_back(values, gain_vec, grad_out):
    _, pullback = jax.vjp(rms_norm, values, gain_vec)
    return pullback(grad_out)


def low(values):
    return values.astype(jnp.bfloat16)


def gated_unit(gate_up):
    return jax.nn.gelu(gate_up[:, :FF], approximate=True) * gate_up[:, FF:]


def swap(values, bit):
    count = lax.axis_size("wide")
    return lax.ppermute(values, "wide", [(w, w ^ bit) for w in range(count)])


def shift(values, step):
    count = lax.axis_size("narrow")
    return lax.ppermute(values, "narrow", [(i, (i + step) % count) for i in range(count)])


def wide_bits():
    return lax.axis_size("wide").bit_length() - 1


def bit_value(level):
    return (lax.axis_index("wide") >> level) & 1


def gather_wide(values, order):
    bits = wide_bits()
    whole = join_wide(values.reshape((1,) * bits + values.shape), order)
    return whole.reshape((1 << bits,) + values.shape)


def split_orders():
    upper = list(range(1, wide_bits()))
    return upper, upper[::-1]


def gather_wide_fast(values):
    first, second = split_orders()
    half = values.shape[-1] // 2
    return jnp.concatenate(
        [gather_wide(values[..., :half], first + [0]), gather_wide(values[..., half:], second + [0])],
        axis=-1,
    )


def tie(*values):
    return lax.optimization_barrier(values)


def from_narrow(rows):
    count = lax.axis_size("narrow")
    ahead = [rows] + [shift(rows, -step) for step in range(1, count)]
    start = (count - lax.axis_index("narrow")) % count
    return lax.dynamic_slice_in_dim(jnp.stack(ahead + ahead), start, count, axis=0)


def join(whole, other, level):
    axis = wide_bits() - 1 - level
    return jnp.where(
        bit_value(level) == 1,
        jnp.concatenate([other, whole], axis=axis),
        jnp.concatenate([whole, other], axis=axis),
    )


def join_wide(whole, order):
    for level in order:
        whole = join(whole, swap(whole, 1 << level), level)
    return whole


class Flow:
    def __init__(self, stages):
        self.stages, self.result, self.values = stages, None, None
        self.pull(None)

    def pull(self, values):
        try:
            self.values = self.stages.send(values)
        except StopIteration as end:
            self.result, self.values = end.value, None

    def drain(self):
        while self.values is not None:
            self.pull(self.values)
        return self.result


def step(main, *flows):
    for _ in range(2):
        live = [flow for flow in flows if flow.values is not None]
        main, values = lax.optimization_barrier((main, [flow.values for flow in live]))
        for flow, tied in zip(live, values):
            flow.pull(tied)
    return main


def scatter_flow(factors, extra=None):
    bits = wide_bits()
    count = lax.axis_size("narrow")
    here = lax.axis_index("narrow")
    pairs = 1 << (bits - 1)
    low_bit = bit_value(0)

    def products(side, got):
        results, offset = [], 0
        for left, right in factors:
            split = left.reshape(left.shape[0], pairs, 2, -1)
            chosen = lax.dynamic_index_in_dim(split, side, 2, keepdims=False)
            result = dot_tn(chosen.reshape(left.shape[0], -1), right)
            if got is not None:
                result = result + got[:, offset : offset + right.shape[1]].astype(jnp.float32)
            if extra is not None and extra[0] == offset:
                split = extra[1].reshape(pairs, 2, -1, right.shape[1])
                chosen = lax.dynamic_index_in_dim(split, side, 1, keepdims=False)
                result = result + chosen.reshape(result.shape)
            offset += right.shape[1]
            results.append(low(result))
        return jnp.concatenate(results, axis=1)

    yield []
    (sent,) = yield [products(1 - low_bit, None)]
    (got,) = yield [swap(sent, 1)]
    mine = products(low_bit, got)
    middle = mine.shape[1] // 256 * 128
    orders = split_orders()
    wholes = [
        part.reshape((2,) * (bits - 1) + (-1, part.shape[1]))
        for part in (mine[:, :middle], mine[:, middle:])
    ]
    for number in range(bits - 1):
        levels = [order[number] for order in orders]
        theirs = [
            lax.dynamic_index_in_dim(whole, 1 - bit_value(level), bits - 1 - level, keepdims=True)
            for whole, level in zip(wholes, levels)
        ]
        tied = yield wholes + theirs
        wholes, theirs = tied[:2], tied[2:]
        got = yield [swap(part, 1 << level) for part, level in zip(theirs, levels)]
        wholes = [
            low(
                lax.dynamic_index_in_dim(
                    whole, bit_value(level), bits - 1 - level, keepdims=True
                ).astype(jnp.float32)
                + part.astype(jnp.float32)
            )
            for whole, part, level in zip(wholes, got, levels)
        ]
    rows = jnp.concatenate([whole.reshape(count, -1, whole.shape[-1]) for whole in wholes], axis=-1)
    pieces = [
        lax.dynamic_index_in_dim(rows, (here + k) % count, 0, keepdims=False) for k in range(count)
    ]
    pieces = yield pieces
    got = yield [shift(pieces[k], k) for k in range(1, count)]
    total = pieces[0].astype(jnp.float32)
    for piece in got:
        total = total + piece.astype(jnp.float32)
    return low(total)


def ring_flow(parts):
    moving = parts[-1]
    yield []
    for part in parts[-2::-1]:
        (moving,) = yield [low(moving)]
        (moving,) = yield [shift(moving, 1)]
        moving = part.astype(jnp.float32) + moving.astype(jnp.float32)
    return moving


def table_flow(own):
    parts = [own]
    yield []
    for _ in range(lax.axis_size("narrow") - 1):
        (moving,) = yield [parts[-1]]
        (moving,) = yield [shift(moving, -1)]
        parts.append(moving)
    return parts


def keys_flow(rows):
    bit = lax.axis_size("narrow") // 2
    yield []
    while bit:
        (rows,) = yield [rows]
        rows, other = yield [rows, swap(rows, bit)]
        rows = jnp.concatenate([rows, other], axis=0)
        bit //= 2
    return rows


def return_flow(parts):
    bit = 1
    yield []
    while bit < lax.axis_size("narrow"):
        half = parts[0].shape[0] // 2
        sent = yield [part[half:] for part in parts]
        got = yield [swap(other, bit) for other in sent]
        parts = [
            low(part[:half].astype(jnp.float32) + other.astype(jnp.float32))
            for part, other in zip(parts, got)
        ]
        bit *= 2
    return jnp.concatenate(parts, axis=1)


def gather_flow(rows):
    bits = wide_bits()
    count = lax.axis_size("narrow")
    columns = rows.shape[1]
    middle = columns // 2
    yield []
    (rows,) = yield [rows]
    ahead = yield [rows] + [shift(rows, -k) for k in range(1, count)]
    start = (count - lax.axis_index("narrow")) % count
    stacked = lax.dynamic_slice_in_dim(jnp.stack(ahead + ahead), start, count, axis=0)
    stacked = stacked.reshape((1,) * bits + stacked.shape)
    parts = [stacked[..., :middle], stacked[..., middle:]]
    orders = split_orders()
    for number in range(bits - 1):
        parts = yield parts
        tied = yield parts + [swap(part, 1 << o[number]) for part, o in zip(parts, orders)]
        parts = [join(tied[k], tied[k + 2], orders[k][number]) for k in range(2)]
    (whole,) = yield [jnp.concatenate(parts, axis=-1)]
    whole, other = yield [whole, swap(whole, 1)]
    return join(whole, other, 0).reshape(-1, columns)


def group_offsets():
    offsets, bit = [0], lax.axis_size("narrow") // 2
    while bit:
        offsets = offsets + [o ^ bit for o in offsets]
        bit //= 2
    return offsets


def feed_forward(stream, gain_vec, w_in, w_back):
    normed = low(rms_norm(stream, gain_vec))
    gate_up = dot_nn(normed, w_in)
    hidden = low(gated_unit(gate_up))
    return (dot_nt(hidden, w_back), (normed, gate_up, hidden))


def adamw(param, moment, second, grad, step_count):
    moment = beta_first * moment + (1 - beta_first) * grad
    second = beta_second * second + (1 - beta_second) * grad * grad
    steps = step_count.astype(jnp.float32)
    m_hat = moment / (1 - jnp.power(beta_first, steps))
    v_hat = second / (1 - jnp.power(beta_second, steps))
    return (
        param - rate_adam * (m_hat / (jnp.sqrt(v_hat) + adam_eps) + weight_decay * param),
        moment,
        second,
    )


def shards(
    patches,
    patch_rows,
    patch_cols,
    input_ids,
    target_ids,
    target_lengths,
    loss_mask,
    master_slabs,
    left_stats,
    left_roots,
    right_stats,
    right_roots,
    block_slot,
    vocab_table,
    vocab_first,
    vocab_second,
    small_params,
    small_first,
    small_second,
    step_count,
):
    wide_count = lax.axis_size("wide")
    narrow_count = lax.axis_size("narrow")
    devices = wide_count * narrow_count
    screen_sets = wide_count // narrow_count
    wide_pos = lax.axis_index("wide")
    narrow_pos = lax.axis_index("narrow")
    member = wide_pos % narrow_count
    slot_total = block_slot.shape[0]
    own_count = master_slabs.shape[0]
    piece = D // devices
    slot_ids = block_slot[:BLOCKS]
    enc_rows, dec_rows = patches.shape[0], input_ids.shape[0]
    vocab_rows, features = vocab_table.shape

    block_of_slot = (slot_ids[:, None] == jnp.arange(slot_total)[None, :]).astype(jnp.bfloat16)
    pieces = low(master_slabs).reshape(own_count, devices, piece, BW).transpose(1, 0, 2, 3)
    pieces = lax.all_to_all(pieces, BOTH, 0, 0)

    exchange = []
    for w in range(wide_count):
        for n in range(narrow_count):
            base = w // narrow_count * narrow_count
            exchange.append((w * narrow_count + n, (base + n) * narrow_count + w % narrow_count))
    whole_ids = lax.ppermute(
        jnp.concatenate([patch_rows, patch_cols, input_ids, target_ids]), BOTH, exchange
    )
    rows_ids, cols_ids = whole_ids[:enc_rows], whole_ids[enc_rows : 2 * enc_rows]
    token_ids = whole_ids[2 * enc_rows :].reshape(2, dec_rows)
    layer_tokens = lax.all_gather(token_ids, "wide", axis=0)
    layer_targets = layer_tokens[:, 1].reshape(-1)
    every_input = lax.all_gather(layer_tokens, "narrow", axis=1)
    screens_info = lax.all_gather(
        jnp.concatenate([target_lengths[:, None], loss_mask], axis=1), "wide", axis=0, tiled=True
    )
    pieces, patches, every_input, screens_info = tie(pieces, patches, every_input, screens_info)
    patches = lax.ppermute(patches, BOTH, exchange)
    counted = (
        (jnp.arange(TGT)[None, :] < screens_info[:, :1]) & (screens_info[:, 1:] == 1)
    ).astype(jnp.float32)
    tokens_counted = jnp.maximum(jnp.sum(counted), 1.0)
    row_counted = lax.dynamic_index_in_dim(
        counted.reshape(screen_sets, narrow_count, TGT), narrow_pos, 1, keepdims=False
    ).reshape(-1)
    own_counted = lax.dynamic_slice_in_dim(row_counted, wide_pos * dec_rows, dec_rows)

    ordered = low(dot_nn(block_of_slot, pieces.reshape(slot_total, piece * BW)))
    row_shard = ordered.reshape(BLOCKS, piece, BW).transpose(1, 0, 2).reshape(piece, BLOCKS * BW)
    weights = [None] * len(EXTENTS)

    def shard_of(numbers):
        begin = sum(EXTENTS[: numbers[0]])
        return row_shard[:, begin : begin + sum(EXTENTS[n] for n in numbers)]

    def take(numbers, group):
        offset = 0
        for n in numbers:
            weights[n] = group[:, offset : offset + EXTENTS[n]]
            offset += EXTENTS[n]

    for numbers in GATHERS:
        take(numbers, lax.all_gather(shard_of(numbers), BOTH, axis=0, tiled=True))
    flow_weights = Flow(gather_flow(shard_of(PERMUTED)))

    padded = -(-vocab_rows // 256) * 256
    table_low = low(vocab_table)
    columns = jnp.arange(vocab_rows)
    vocab_start = wide_pos * vocab_rows
    flat_inputs = every_input[:, :, 0].reshape(-1) - vocab_start
    flat_targets = every_input[:, :, 1].reshape(-1) - vocab_start

    def looked_up(ids):
        onehot = (ids[:, None] == columns[None, :]).astype(jnp.bfloat16)
        found = low(dot_nn(onehot, table_low))
        return found.reshape(wide_count, narrow_count * dec_rows, features)

    def delivered(found):
        found = low(jnp.sum(found.astype(jnp.float32), axis=0))
        found = lax.all_to_all(found.reshape(narrow_count, dec_rows, features), "narrow", 0, 0)
        return found.transpose(1, 0, 2).reshape(dec_rows, D).astype(jnp.float32)

    flat_inputs = step(flat_inputs, flow_weights)
    found_inputs = looked_up(flat_inputs)
    found_inputs = step(found_inputs, flow_weights)
    found_inputs = lax.all_to_all(found_inputs, "wide", 0, 0)
    flow_table = Flow(table_flow(jnp.pad(table_low.T, ((0, 0), (0, padded - vocab_rows)))))

    gain_rows = small_params[2 * POS :]
    picked = jnp.concatenate(
        [
            rows_ids[:, None] == jnp.arange(POS)[None, :],
            cols_ids[:, None] == jnp.arange(POS)[None, :],
        ],
        axis=1,
    ).astype(jnp.bfloat16)
    tables = small_params[: 2 * POS]
    tables_high = low(tables)
    tables_rest = low(tables - tables_high.astype(jnp.float32))
    enc_zero = (
        dot_nn(patches, weights[0])
        + gain_rows[7]
        + dot_nn(picked, tables_high)
        + dot_nn(picked, tables_rest)
    )
    enc_zero = step(enc_zero, flow_weights)
    enc_normed = low(rms_norm(enc_zero, gain_rows[0]))
    enc_mix = low(dot_nn(enc_normed, weights[1]))
    enc_query = enc_mix[:, :D]
    flow_keys = Flow(keys_flow(enc_mix[:, D:]))
    enc_query, flat_targets = step((enc_query, flat_targets), flow_keys, flow_table)
    found_targets = looked_up(flat_targets)
    enc_query, found_targets = step((enc_query, found_targets), flow_keys, flow_weights)
    found_targets = lax.all_to_all(found_targets, "wide", 0, 0)
    enc_query = step(enc_query, flow_keys)
    enc_keys = flow_keys.drain()
    enc_mixed, enc_total = attend(enc_query, enc_keys, None)
    enc_mixed, found_inputs = step((enc_mixed, found_inputs), flow_weights)
    take(PERMUTED, flow_weights.drain())
    dec_zero = delivered(found_inputs)
    enc_one = enc_zero + dot_nn(enc_mixed, weights[2])
    enc_fnormed = low(rms_norm(enc_one, gain_rows[1]))
    enc_gate = dot_nn(enc_fnormed, weights[3])
    enc_hidden = low(gated_unit(enc_gate))
    enc_ffn = (enc_fnormed, enc_gate, enc_hidden)

    query_pos = (member * dec_rows + jnp.arange(dec_rows)).astype(jnp.int32)
    key_pos = jnp.concatenate(
        [(member ^ offset) * dec_rows + jnp.arange(dec_rows) for offset in group_offsets()]
    ).astype(jnp.int32)
    causal = (query_pos, key_pos)
    dec_normed = low(rms_norm(dec_zero, gain_rows[3]))
    dec_mix = low(dot_nn(dec_normed, weights[5]))
    flow_keys = Flow(keys_flow(dec_mix[:, D:]))
    enc_hidden, found_targets = step((enc_hidden, found_targets), flow_keys, flow_table)
    enc_two = enc_one + dot_nt(enc_hidden, weights[4])
    encoded = low(rms_norm(enc_two, gain_rows[2]))
    flow_cross = Flow(keys_flow(low(dot_nn(encoded, weights[8]))))
    dec_query = dec_mix[:, :D]
    dec_query, found_targets = step((dec_query, found_targets), flow_keys, flow_cross)
    target_rows = delivered(found_targets)
    dec_query = step(dec_query, flow_keys)
    self_keys = flow_keys.drain()
    self_mixed, self_total = attend(dec_query, self_keys, causal)
    dec_one = dec_zero + dot_nn(self_mixed, weights[6])
    cross_normed = low(rms_norm(dec_one, gain_rows[4]))
    cross_query = low(dot_nn(cross_normed, weights[7]))
    cross_query, target_rows = step((cross_query, target_rows), flow_cross)
    cross_query = step(cross_query, flow_cross, flow_table)
    cross_keys = flow_cross.drain()
    cross_mixed, cross_total = attend(cross_query, cross_keys, None)
    dec_two = dec_one + dot_nn(cross_mixed, weights[9])
    branch, dec_ffn = feed_forward(dec_two, gain_rows[5], weights[10], weights[11])
    dec_three = dec_two + branch
    final = low(rms_norm(dec_three, gain_rows[6]) * D ** (-0.5))
    table_parts = flow_table.drain()

    rotated = lax.dynamic_slice_in_dim(
        jnp.concatenate([final, final], axis=1), narrow_pos * features, D, axis=1
    )
    rows_all = gather_wide_fast(rotated).reshape(-1, D)
    total_rows = rows_all.shape[0]
    block_rows = 256
    used = jnp.any(row_counted.reshape(-1, block_rows) != 0, axis=1).astype(jnp.int32)
    tile = padded // 5 if padded % 640 == 0 else 256
    mixed, exps, stats = head_forward(
        rows_all, table_parts, used, vocab_rows, block_rows, tile
    )
    top_part, summed_part = stats[:, 0], stats[:, 1]
    stats_all = lax.all_gather(jnp.stack([top_part, summed_part]), "wide", axis=0)
    top_logit = jnp.max(stats_all[:, 0], axis=0)
    summed = jnp.sum(stats_all[:, 1] * jnp.exp(stats_all[:, 0] - top_logit), axis=0)
    log_total = top_logit + jnp.log(summed)
    row_weight = row_counted / tokens_counted
    scale = row_weight * jnp.exp(top_part - log_total)
    grad_rows = low(mixed * scale[:, None]).reshape(wide_count, dec_rows, D)
    grad_rows = lax.all_to_all(grad_rows, "wide", 0, 0)
    own_weight = own_counted / tokens_counted
    target_logit = jnp.sum(final.astype(jnp.float32) * target_rows, axis=1)
    own_total = lax.dynamic_slice_in_dim(log_total, wide_pos * dec_rows, dec_rows)
    loss_local = jnp.sum(own_counted * (own_total - target_logit))
    target_cols = (layer_targets - vocab_start).astype(jnp.float32)
    info = jnp.concatenate(
        [
            jnp.stack([scale, row_weight, target_cols], axis=1),
            jnp.zeros((total_rows, 125), jnp.float32),
        ],
        axis=1,
    )
    grad_table = table_grad(rows_all, exps, info, used, block_rows, tile)
    grad_parts = grad_table.reshape(narrow_count, features, padded)
    ring = Flow(ring_flow([grad_parts[k] for k in range(narrow_count)]))
    grad_rows = step(grad_rows, ring)
    grad_back = jnp.sum(grad_rows.astype(jnp.float32), axis=0)
    grad_back = lax.dynamic_slice_in_dim(
        jnp.concatenate([grad_back, grad_back], axis=1), (D - narrow_pos * features) % D, D, axis=1
    )
    grad_final = grad_back - own_weight[:, None] * target_rows

    grad_three, gain_final = norm_back(dec_three, gain_rows[6], grad_final * D ** (-0.5))
    low_three = low(grad_three)
    _, pullback = jax.vjp(gated_unit, dec_ffn[1])
    grad_gate = low(pullback(dot_nn(low_three, weights[11]))[0])
    flow_dffn = Flow(scatter_flow([(dec_ffn[0], grad_gate), (low_three, dec_ffn[2])]))
    grad_gate = step(grad_gate, flow_dffn)
    grad_two, gain_dffn = norm_back(dec_two, gain_rows[5], dot_nt(grad_gate, weights[10]))
    grad_two = grad_two + grad_three
    low_two = low(grad_two)
    grad_mixed = low(dot_nt(low_two, weights[9]))
    grad_mixed = step(grad_mixed, flow_dffn)
    grad_cq, grad_key, grad_value = attend_back(
        cross_query, cross_keys, None, cross_mixed, cross_total, grad_mixed
    )
    flow_cross = Flow(return_flow([grad_key, grad_value]))
    grad_cq = step(grad_cq, flow_cross)
    grad_one, gain_cross = norm_back(dec_one, gain_rows[4], dot_nt(grad_cq, weights[7]))
    grad_one = grad_one + grad_two
    low_one = low(grad_one)
    grad_mixed = low(dot_nt(low_one, weights[6]))
    grad_mixed = step(grad_mixed, flow_cross)
    grad_sq, grad_key, grad_value = attend_back(
        dec_mix[:, :D], self_keys, causal, self_mixed, self_total, grad_mixed
    )
    flow_self = Flow(return_flow([grad_key, grad_value]))
    grad_sq = step(grad_sq, flow_self, flow_dffn)
    grad_sq = step(grad_sq, flow_self, ring)
    grad_sq = step(grad_sq, flow_cross)
    grad_ckv = flow_cross.drain()

    grad_two, gain_efinal = norm_back(enc_two, gain_rows[2], dot_nt(grad_ckv, weights[8]))
    low_etwo = low(grad_two)
    _, pullback = jax.vjp(gated_unit, enc_ffn[1])
    grad_gate = low(pullback(dot_nn(low_etwo, weights[4]))[0])
    grad_gate = step(grad_gate, flow_self, flow_dffn)
    grad_smix = jnp.concatenate([grad_sq, flow_self.drain()], axis=1)
    grad_zero, gain_self = norm_back(dec_zero, gain_rows[3], dot_nt(grad_smix, weights[5]))
    grad_tokens = low(grad_zero + grad_one)
    sent = grad_tokens.reshape(dec_rows, narrow_count, features).transpose(1, 0, 2)
    sent = lax.all_to_all(sent, "narrow", 0, 0).reshape(narrow_count * dec_rows, features)
    sent = lax.all_gather(sent, "wide", axis=0, tiled=True)
    flow_dattn = Flow(
        scatter_flow(
            [
                (dec_normed, grad_smix),
                (self_mixed, low_one),
                (cross_normed, grad_cq),
                (encoded, grad_ckv),
                (cross_mixed, low_two),
            ]
        )
    )
    flow_effn = Flow(scatter_flow([(enc_ffn[0], grad_gate), (low_etwo, enc_ffn[2])]))
    grad_gate = step(grad_gate, flow_dattn, flow_effn)
    grad_one, gain_effn = norm_back(enc_one, gain_rows[1], dot_nt(grad_gate, weights[3]))
    grad_one = grad_one + grad_two
    low_eone = low(grad_one)
    grad_mixed = low(dot_nt(low_eone, weights[2]))
    grad_mixed = step(grad_mixed, flow_dattn, flow_effn)
    grad_mixed = step(grad_mixed, flow_dffn, ring)
    grad_eq, grad_key, grad_value = attend_back(
        enc_mix[:, :D], enc_keys, None, enc_mixed, enc_total, grad_mixed
    )
    flow_enc = Flow(return_flow([grad_key, grad_value]))
    grad_eq = step(grad_eq, flow_enc)
    grad_eq = step(grad_eq, flow_enc)
    grad_eq, sent = step((grad_eq, sent), flow_dattn, flow_effn)
    onehot = (flat_inputs[:, None] == columns[None, :]).astype(jnp.bfloat16)
    looked_grad = dot_tn(onehot, sent)
    grad_eq, looked_grad = step((grad_eq, looked_grad), flow_enc)
    grad_eq = step(grad_eq, flow_dattn, flow_effn)
    grad_emix = jnp.concatenate([grad_eq, flow_enc.drain()], axis=1)
    grad_zero, gain_eattn = norm_back(enc_zero, gain_rows[0], dot_nt(grad_emix, weights[1]))
    grad_zero = grad_zero + grad_one
    low_zero = low(grad_zero)
    gains = [gain_eattn, gain_effn, gain_efinal, gain_self, gain_cross, gain_dffn, gain_final]
    width = -(-SMALL_ROWS // BW) * BW
    gains = jnp.pad(jnp.stack(gains, axis=1), ((0, 0), (2 * POS, width - 2 * POS - 7)))
    marks = (jnp.arange(width) == SMALL_ROWS - 1).astype(jnp.bfloat16)
    small_factor = marks[None, :] + jnp.pad(picked, ((0, 0), (0, width - 2 * POS)))
    flow_eattn = Flow(
        scatter_flow(
            [
                (patches, low_zero),
                (enc_normed, grad_emix),
                (enc_mixed, low_eone),
                (low_zero, small_factor),
            ],
            (5 * D, gains),
        )
    )
    looked_grad = step(looked_grad, flow_eattn)
    head_grad = ring.drain()[:, :vocab_rows].T
    vocab_grad = head_grad + looked_grad
    vocab_square = jnp.sum(vocab_grad * vocab_grad)
    vocab_square = step(vocab_square, flow_eattn)
    vocab_square = step(vocab_square, flow_dattn, flow_effn)
    vocab_square = step(vocab_square, flow_eattn)
    shard_dffn, shard_dattn = flow_dffn.drain(), flow_dattn.drain()
    shard_effn, shard_eattn = flow_effn.drain(), flow_eattn.drain()

    projection = shard_eattn[:, : 5 * D]
    small_shard = shard_eattn[:, 5 * D : 5 * D + SMALL_ROWS].astype(jnp.float32)
    grads = jnp.concatenate([projection, shard_effn, shard_dattn, shard_dffn], axis=1)
    partial_square = (
        jnp.sum(jnp.square(grads.astype(jnp.float32)))
        + vocab_square
        + jnp.sum(small_shard * small_shard)
    )
    scalars = jnp.where(
        jnp.arange(SMALL_ROWS)[None, :] == 0,
        partial_square,
        jnp.where(jnp.arange(SMALL_ROWS)[None, :] == 1, loss_local, 0.0),
    )
    slotted = grads.reshape(piece, BLOCKS, BW).transpose(1, 0, 2).reshape(BLOCKS, piece * BW)
    slotted = low(dot_tn(block_of_slot, slotted)).reshape(devices, own_count, piece, BW)
    small_shard, scalars, slotted = tie(small_shard, scalars, slotted)
    slab = lax.all_to_all(slotted, BOTH, 0, 0).transpose(1, 0, 2, 3).reshape(own_count, D, BW)
    shared = from_narrow(jnp.concatenate([small_shard, scalars], axis=0))
    shared = join_wide(shared.reshape((1,) * wide_bits() + shared.shape), split_orders()[0] + [0])
    shared = shared.reshape(devices, piece + 1, SMALL_ROWS)
    small_grad = shared[:, :piece].reshape(D, SMALL_ROWS).T
    total_square = jnp.sum(shared[:, piece, 0])
    loss_sum = jnp.sum(shared[:, piece, 1])

    grad_norm = jnp.sqrt(total_square)
    factor = jnp.minimum(1.0, clip_limit / (grad_norm + 1e-06))
    kept = (1 - stat_decay) * factor * factor
    slab_grad = slab.astype(jnp.float32) * factor
    left_new = stat_decay * left_stats + kept * jnp.einsum(
        "sik,sjk->sij", slab, slab, preferred_element_type=jnp.float32
    )
    right_new = stat_decay * right_stats + kept * jnp.einsum(
        "ski,skj->sij", slab, slab, preferred_element_type=jnp.float32
    )
    rooted = jnp.einsum("sij,sjk->sik", low(left_roots), slab, preferred_element_type=jnp.float32)
    precond = factor * jnp.einsum(
        "sij,sjk->sik", rooted, right_roots, precision=lax.Precision.HIGHEST
    )
    scale_back = lax.rsqrt(jnp.mean(precond * precond, axis=(1, 2), keepdims=True) + norm_eps)
    master_new = master_slabs - rate_shampoo * precond * scale_back
    vocab_new, vocab_first_new, vocab_second_new = adamw(
        vocab_table, vocab_first, vocab_second, vocab_grad * factor, step_count
    )
    small_new, small_first_new, small_second_new = adamw(
        small_params, small_first, small_second, small_grad * factor, step_count
    )
    return (
        loss_sum,
        tokens_counted,
        master_new,
        master_new.astype(jnp.bfloat16),
        slab_grad,
        left_new,
        right_new,
        vocab_new,
        vocab_new.astype(jnp.bfloat16),
        vocab_first_new,
        vocab_second_new,
        small_new,
        small_first_new,
        small_second_new,
        grad_norm,
    )


def solution(mesh):
    in_specs = (
        P(("wide", "narrow"), None),
        P(("wide", "narrow")),
        P(("wide", "narrow")),
        P(("wide", "narrow")),
        P(("wide", "narrow")),
        P("wide"),
        P("wide", None),
        P(("wide", "narrow"), None, None),
        P(("wide", "narrow"), None, None),
        P(("wide", "narrow"), None, None),
        P(("wide", "narrow"), None, None),
        P(("wide", "narrow"), None, None),
        P(),
        P("wide", "narrow"),
        P("wide", "narrow"),
        P("wide", "narrow"),
        P(),
        P(),
        P(),
        P(),
    )
    out_specs = (
        P(),
        P(),
        P(("wide", "narrow"), None, None),
        P(("wide", "narrow"), None, None),
        P(("wide", "narrow"), None, None),
        P(("wide", "narrow"), None, None),
        P(("wide", "narrow"), None, None),
        P("wide", "narrow"),
        P("wide", "narrow"),
        P("wide", "narrow"),
        P("wide", "narrow"),
        P(),
        P(),
        P(),
        P(),
    )
    return jax.shard_map(shards, mesh=mesh, in_specs=in_specs, out_specs=out_specs, check_vma=False)
```

```python
import jax
import jax.numpy as jnp
from jax import lax
from jax.experimental import pallas as pl
from jax.experimental.pallas import tpu as pltpu
from jax.sharding import PartitionSpec as P

HEAD_DIM = 64
D = 768
attn_scale = 0.125
KERNEL_VMEM = 56 * 1024 * 1024
SMALL_COST = pl.CostEstimate(flops=1 << 20, bytes_accessed=1 << 20, transcendentals=0)


def dot_nt(left, right):
    return lax.dot_general(
        left, right, (((1,), (1,)), ((), ())), preferred_element_type=jnp.float32
    )


def dot_nn(left, right):
    return lax.dot_general(
        left, right, (((1,), (0,)), ((), ())), preferred_element_type=jnp.float32
    )


def dot_tn(left, right):
    return lax.dot_general(
        left, right, (((0,), (0,)), ((), ())), preferred_element_type=jnp.float32
    )


def attend_kernel(masked, row_step, *refs):
    if masked:
        query_pos, key_pos, q_ref, k_ref, v_ref, out_ref, lse_ref = refs
    else:
        q_ref, k_ref, v_ref, out_ref, lse_ref = refs
    keys = k_ref[...]
    values = v_ref[...]
    key_lane = lax.broadcasted_iota(jnp.int32, values.shape, 1) // HEAD_DIM
    lane = lax.broadcasted_iota(jnp.int32, (row_step, 128), 1) // HEAD_DIM
    one = jnp.ones((), values.dtype)
    sides = [jnp.where(key_lane == side, values, one) for side in range(2)]
    for start in range(0, q_ref.shape[0], row_step):
        rows = pl.ds(start, row_step)
        queries = q_ref[rows, :]
        mixed, totals = [], []
        for side in range(2):
            half = jnp.where(lane == side, queries, jnp.zeros((), queries.dtype)) * attn_scale
            scores = dot_nt(half.astype(jnp.bfloat16), keys)
            if masked:
                scores = jnp.where(key_pos[...] <= query_pos[rows, :], scores, -1000000000.0)
            top = jnp.max(scores, axis=1, keepdims=True)
            exponent = jnp.exp(scores - top).astype(jnp.bfloat16)
            both = dot_nn(exponent, sides[side])
            other = (1 - side) * HEAD_DIM
            summed = both[:, other : other + 1]
            mixed.append(both / summed)
            totals.append(top + jnp.log(summed))
        out_ref[rows, :] = jnp.where(lane == 0, mixed[0], mixed[1]).astype(out_ref.dtype)
        lse_ref[rows, :] = jnp.where(lane == 0, totals[0], totals[1])


def attend(queries, keys_values, positions):
    rows, keys = queries.shape[0], keys_values.shape[0]
    pairs = D // 128
    row_step = min(rows, 256)
    extra, extra_specs = (), []
    if positions is not None:
        query_pos, key_pos = positions
        extra = (query_pos.reshape(rows, 1), key_pos.reshape(1, keys))
        extra_specs = [
            pl.BlockSpec((rows, 1), lambda j: (0, 0)),
            pl.BlockSpec((1, keys), lambda j: (0, 0)),
        ]
    return pl.pallas_call(
        lambda *refs: attend_kernel(positions is not None, row_step, *refs),
        grid=(pairs,),
        in_specs=extra_specs
        + [
            pl.BlockSpec((rows, 128), lambda j: (0, j)),
            pl.BlockSpec((keys, 128), lambda j: (0, j)),
            pl.BlockSpec((keys, 128), lambda j: (0, j + pairs)),
        ],
        out_specs=[
            pl.BlockSpec((rows, 128), lambda j: (0, j)),
            pl.BlockSpec((rows, 128), lambda j: (0, j)),
        ],
        out_shape=[
            jax.ShapeDtypeStruct((rows, D), jnp.bfloat16),
            jax.ShapeDtypeStruct((rows, D), jnp.float32),
        ],
        compiler_params=pltpu.CompilerParams(vmem_limit_bytes=KERNEL_VMEM),
        cost_estimate=SMALL_COST,
    )(*extra, queries, keys_values, keys_values)


def attend_back_kernel(masked, key_step, *refs):
    if masked:
        query_pos, key_pos, q_ref, k_ref, v_ref, out_ref, lse_ref, grad_ref, dq_ref, dk_ref, dv_ref = refs
    else:
        q_ref, k_ref, v_ref, out_ref, lse_ref, grad_ref, dq_ref, dk_ref, dv_ref = refs
    queries = q_ref[...]
    grads = grad_ref[...]
    lane = lax.broadcasted_iota(jnp.int32, queries.shape, 1) // HEAD_DIM
    zero = jnp.zeros((), queries.dtype)
    totals = lse_ref[...].T
    weighted = (grads.astype(jnp.float32) * out_ref[...].astype(jnp.float32)).T
    halves, grad_halves, total_rows, delta_rows, grad_queries = [], [], [], [], []
    for side in range(2):
        halves.append((jnp.where(lane == side, queries, zero) * attn_scale).astype(jnp.bfloat16))
        grad_halves.append(jnp.where(lane == side, grads, zero))
        total_rows.append(totals[side * HEAD_DIM : side * HEAD_DIM + 1, :])
        delta_rows.append(
            jnp.sum(weighted[side * HEAD_DIM : (side + 1) * HEAD_DIM, :], axis=0, keepdims=True)
        )
        grad_queries.append(jnp.zeros(queries.shape, jnp.float32))
    for start in range(0, k_ref.shape[0], key_step):
        rows = pl.ds(start, key_step)
        keys = k_ref[rows, :]
        values = v_ref[rows, :]
        grad_keys = jnp.zeros(keys.shape, jnp.float32)
        grad_values = jnp.zeros(keys.shape, jnp.float32)
        for side in range(2):
            scores = dot_nt(keys, halves[side])
            probs = jnp.exp(scores - total_rows[side])
            if masked:
                probs = jnp.where(key_pos[rows, :] <= query_pos[...], probs, 0.0)
            grad_probs = dot_nt(values, grad_halves[side])
            grad_scores = (probs * (grad_probs - delta_rows[side])).astype(jnp.bfloat16)
            grad_values += dot_nn(probs.astype(jnp.bfloat16), grad_halves[side])
            grad_keys += dot_nn(grad_scores, halves[side])
            grad_queries[side] += dot_tn(grad_scores, keys)
        dk_ref[rows, :] = grad_keys.astype(dk_ref.dtype)
        dv_ref[rows, :] = grad_values.astype(dv_ref.dtype)
    dq_ref[...] = (jnp.where(lane == 0, grad_queries[0], grad_queries[1]) * attn_scale).astype(
        dq_ref.dtype
    )


def attend_back(queries, keys_values, positions, mixed_rows, log_total, grad_mixed):
    rows, keys = queries.shape[0], keys_values.shape[0]
    pairs = D // 128
    key_step = min(keys, 512)
    extra, extra_specs = (), []
    if positions is not None:
        query_pos, key_pos = positions
        extra = (query_pos.reshape(1, rows), key_pos.reshape(keys, 1))
        extra_specs = [
            pl.BlockSpec((1, rows), lambda j: (0, 0)),
            pl.BlockSpec((keys, 1), lambda j: (0, 0)),
        ]
    row_spec = pl.BlockSpec((rows, 128), lambda j: (0, j))
    key_spec = pl.BlockSpec((keys, 128), lambda j: (0, j))
    value_spec = pl.BlockSpec((keys, 128), lambda j: (0, j + pairs))
    return pl.pallas_call(
        lambda *refs: attend_back_kernel(positions is not None, key_step, *refs),
        grid=(pairs,),
        in_specs=extra_specs + [row_spec, key_spec, value_spec, row_spec, row_spec, row_spec],
        out_specs=[row_spec, key_spec, key_spec],
        out_shape=[
            jax.ShapeDtypeStruct((rows, D), jnp.bfloat16),
            jax.ShapeDtypeStruct((keys, D), jnp.bfloat16),
            jax.ShapeDtypeStruct((keys, D), jnp.bfloat16),
        ],
        compiler_params=pltpu.CompilerParams(vmem_limit_bytes=KERNEL_VMEM),
        cost_estimate=SMALL_COST,
    )(*extra, queries, keys_values, keys_values, mixed_rows, log_total, grad_mixed)


def head_kernel(vocab, tile, used_ref, rows_ref, table_ref, mixed_ref, exp_ref, stats_ref, logits_ref):
    step = pl.program_id(0)
    padded = table_ref.shape[1]
    shape = (rows_ref.shape[0], 128)
    lane = lax.broadcasted_iota(jnp.int32, shape, 1)

    @pl.when(used_ref[step] == 0)
    def _():
        mixed_ref[...] = jnp.zeros(mixed_ref.shape, mixed_ref.dtype)
        exp_ref[...] = jnp.zeros(exp_ref.shape, exp_ref.dtype)
        stats_ref[...] = jnp.where(lane == 1, 1.0, 0.0)

    @pl.when(used_ref[step] != 0)
    def _():
        rows = rows_ref[...]
        top = jnp.full((rows.shape[0], 1), -jnp.inf, jnp.float32)
        for start in range(0, padded, tile):
            logits = dot_nn(rows, table_ref[:, start : start + tile])
            if start + tile > vocab:
                column = start + lax.broadcasted_iota(jnp.int32, logits.shape, 1)
                logits = jnp.where(column < vocab, logits, -jnp.inf)
            logits_ref[:, start : start + tile] = logits
            top = jnp.maximum(top, jnp.max(logits, axis=1, keepdims=True))
        summed = jnp.zeros((rows.shape[0], 1), jnp.float32)
        mixed = jnp.zeros(mixed_ref.shape, jnp.float32)
        for start in range(0, padded, tile):
            exponent = jnp.exp(logits_ref[:, start : start + tile] - top)
            summed += jnp.sum(exponent, axis=1, keepdims=True)
            low = exponent.astype(jnp.bfloat16)
            exp_ref[:, start : start + tile] = low
            mixed += dot_nt(low, table_ref[:, start : start + tile])
        mixed_ref[...] = mixed
        stats_ref[...] = jnp.where(lane == 0, top, summed)


def head_forward(rows_all, table, used, vocab, block_rows, tile):
    rows, padded = rows_all.shape[0], table.shape[1]
    return pl.pallas_call(
        lambda *refs: head_kernel(vocab, tile, *refs),
        grid_spec=pltpu.PrefetchScalarGridSpec(
            num_scalar_prefetch=1,
            grid=(rows // block_rows,),
            in_specs=[
                pl.BlockSpec((block_rows, D), lambda i, used: (i, 0)),
                pl.BlockSpec((D, padded), lambda i, used: (0, 0), pipeline_mode=pl.Buffered(1)),
            ],
            out_specs=[
                pl.BlockSpec((block_rows, D), lambda i, used: (i, 0)),
                pl.BlockSpec((block_rows, padded), lambda i, used: (i, 0)),
                pl.BlockSpec((block_rows, 128), lambda i, used: (i, 0)),
            ],
            scratch_shapes=[pltpu.VMEM((block_rows, padded), jnp.float32)],
        ),
        out_shape=[
            jax.ShapeDtypeStruct((rows, D), jnp.float32),
            jax.ShapeDtypeStruct((rows, padded), jnp.bfloat16),
            jax.ShapeDtypeStruct((rows, 128), jnp.float32),
        ],
        compiler_params=pltpu.CompilerParams(vmem_limit_bytes=KERNEL_VMEM),
        cost_estimate=SMALL_COST,
    )(used, rows_all, table)


def table_grad_kernel(tile, used_ref, rows_ref, exp_ref, info_ref, grad_ref, total_ref):
    step = pl.program_id(0)

    @pl.when(step == 0)
    def _():
        total_ref[...] = jnp.zeros(total_ref.shape, total_ref.dtype)

    @pl.when(used_ref[step] != 0)
    def _():
        rows = rows_ref[...]
        scale = info_ref[:, 0:1]
        weight = info_ref[:, 1:2]
        target = info_ref[:, 2:3].astype(jnp.int32)
        for start in range(0, exp_ref.shape[1], tile):
            column = start + lax.broadcasted_iota(jnp.int32, (exp_ref.shape[0], tile), 1)
            probs = exp_ref[:, start : start + tile].astype(jnp.float32) * scale
            hits = jnp.where(column == target, weight, 0.0)
            grad_logits = (probs - hits).astype(jnp.bfloat16)
            total_ref[:, start : start + tile] += dot_tn(rows, grad_logits)

    @pl.when(step == pl.num_programs(0) - 1)
    def _():
        grad_ref[...] = total_ref[...].astype(grad_ref.dtype)


def table_grad(rows_all, exps, info, used, block_rows, tile):
    rows, padded = exps.shape
    return pl.pallas_call(
        lambda *refs: table_grad_kernel(tile, *refs),
        grid_spec=pltpu.PrefetchScalarGridSpec(
            num_scalar_prefetch=1,
            grid=(rows // block_rows,),
            in_specs=[
                pl.BlockSpec((block_rows, D), lambda i, used: (i, 0)),
                pl.BlockSpec((block_rows, padded), lambda i, used: (i, 0)),
                pl.BlockSpec((block_rows, 128), lambda i, used: (i, 0)),
            ],
            out_specs=pl.BlockSpec((D, padded), lambda i, used: (0, 0), pipeline_mode=pl.Buffered(1)),
            scratch_shapes=[pltpu.VMEM((D, padded), jnp.float32)],
        ),
        out_shape=jax.ShapeDtypeStruct((D, padded), jnp.bfloat16),
        compiler_params=pltpu.CompilerParams(vmem_limit_bytes=KERNEL_VMEM),
        cost_estimate=SMALL_COST,
    )(used, rows_all, exps, info)


FF = 2048
POS = 256
TGT = 1024
BW = 128
BLOCKS = 174
EXTENTS = [D, 3 * D, D, 2 * FF, FF, 3 * D, D, D, 2 * D, D, 2 * FF, FF]
GATHERS = [[0, 1], [5, 6, 7, 8], [9, 10, 11]]
PERMUTED = [2, 3, 4]
SMALL_ROWS = 2 * POS + 8

norm_eps = 1e-06
clip_limit = 0.02
stat_decay = 0.5
rate_shampoo = 0.02
rate_adam = 0.5
beta_first = 0.9
beta_second = 0.95
adam_eps = 1e-08
weight_decay = 0.01
BOTH = ("wide", "narrow")


def rms_norm(values, gain_vec):
    return (
        values * lax.rsqrt(jnp.mean(values * values, axis=-1, keepdims=True) + norm_eps) * gain_vec
    )


def norm_back(values, gain_vec, grad_out):
    _, pullback = jax.vjp(rms_norm, values, gain_vec)
    return pullback(grad_out)


def low(values):
    return values.astype(jnp.bfloat16)


def gated_unit(gate_up):
    return jax.nn.gelu(gate_up[:, :FF], approximate=True) * gate_up[:, FF:]


def swap(values, bit):
    count = lax.axis_size("wide")
    return lax.ppermute(values, "wide", [(w, w ^ bit) for w in range(count)])


def shift(values, step):
    count = lax.axis_size("narrow")
    return lax.ppermute(values, "narrow", [(i, (i + step) % count) for i in range(count)])


def wide_bits():
    return lax.axis_size("wide").bit_length() - 1


def bit_value(level):
    return (lax.axis_index("wide") >> level) & 1


def gather_wide(values, order):
    bits = wide_bits()
    whole = join_wide(values.reshape((1,) * bits + values.shape), order)
    return whole.reshape((1 << bits,) + values.shape)


def split_orders():
    upper = list(range(1, wide_bits()))
    return upper, upper[::-1]


def gather_wide_fast(values):
    first, second = split_orders()
    half = values.shape[-1] // 2
    return jnp.concatenate(
        [gather_wide(values[..., :half], first + [0]), gather_wide(values[..., half:], second + [0])],
        axis=-1,
    )


def tie(*values):
    return lax.optimization_barrier(values)


def from_narrow(rows):
    count = lax.axis_size("narrow")
    ahead = [rows] + [shift(rows, -step) for step in range(1, count)]
    start = (count - lax.axis_index("narrow")) % count
    return lax.dynamic_slice_in_dim(jnp.stack(ahead + ahead), start, count, axis=0)


def join(whole, other, level):
    axis = wide_bits() - 1 - level
    return jnp.where(
        bit_value(level) == 1,
        jnp.concatenate([other, whole], axis=axis),
        jnp.concatenate([whole, other], axis=axis),
    )


def join_wide(whole, order):
    for level in order:
        whole = join(whole, swap(whole, 1 << level), level)
    return whole


class Flow:
    def __init__(self, stages):
        self.stages, self.result, self.values = stages, None, None
        self.pull(None)

    def pull(self, values):
        try:
            self.values = self.stages.send(values)
        except StopIteration as end:
            self.result, self.values = end.value, None

    def drain(self):
        while self.values is not None:
            self.pull(self.values)
        return self.result


def step(main, *flows):
    for _ in range(2):
        live = [flow for flow in flows if flow.values is not None]
        main, values = lax.optimization_barrier((main, [flow.values for flow in live]))
        for flow, tied in zip(live, values):
            flow.pull(tied)
    return main


def scatter_flow(factors, extra=None):
    bits = wide_bits()
    count = lax.axis_size("narrow")
    here = lax.axis_index("narrow")
    pairs = 1 << (bits - 1)
    low_bit = bit_value(0)

    def products(side, got):
        results, offset = [], 0
        for left, right in factors:
            split = left.reshape(left.shape[0], pairs, 2, -1)
            chosen = lax.dynamic_index_in_dim(split, side, 2, keepdims=False)
            result = dot_tn(chosen.reshape(left.shape[0], -1), right)
            if got is not None:
                result = result + got[:, offset : offset + right.shape[1]].astype(jnp.float32)
            if extra is not None and extra[0] == offset:
                split = extra[1].reshape(pairs, 2, -1, right.shape[1])
                chosen = lax.dynamic_index_in_dim(split, side, 1, keepdims=False)
                result = result + chosen.reshape(result.shape)
            offset += right.shape[1]
            results.append(low(result))
        return jnp.concatenate(results, axis=1)

    yield []
    (sent,) = yield [products(1 - low_bit, None)]
    (got,) = yield [swap(sent, 1)]
    mine = products(low_bit, got)
    middle = mine.shape[1] // 256 * 128
    orders = split_orders()
    wholes = [
        part.reshape((2,) * (bits - 1) + (-1, part.shape[1]))
        for part in (mine[:, :middle], mine[:, middle:])
    ]
    for number in range(bits - 1):
        levels = [order[number] for order in orders]
        theirs = [
            lax.dynamic_index_in_dim(whole, 1 - bit_value(level), bits - 1 - level, keepdims=True)
            for whole, level in zip(wholes, levels)
        ]
        tied = yield wholes + theirs
        wholes, theirs = tied[:2], tied[2:]
        got = yield [swap(part, 1 << level) for part, level in zip(theirs, levels)]
        wholes = [
            low(
                lax.dynamic_index_in_dim(
                    whole, bit_value(level), bits - 1 - level, keepdims=True
                ).astype(jnp.float32)
                + part.astype(jnp.float32)
            )
            for whole, part, level in zip(wholes, got, levels)
        ]
    rows = jnp.concatenate([whole.reshape(count, -1, whole.shape[-1]) for whole in wholes], axis=-1)
    pieces = [
        lax.dynamic_index_in_dim(rows, (here + k) % count, 0, keepdims=False) for k in range(count)
    ]
    pieces = yield pieces
    got = yield [shift(pieces[k], k) for k in range(1, count)]
    total = pieces[0].astype(jnp.float32)
    for piece in got:
        total = total + piece.astype(jnp.float32)
    return low(total)


def ring_flow(parts):
    moving = parts[-1]
    yield []
    for part in parts[-2::-1]:
        (moving,) = yield [low(moving)]
        (moving,) = yield [shift(moving, 1)]
        moving = part.astype(jnp.float32) + moving.astype(jnp.float32)
    return moving


def table_flow(own):
    parts = [own]
    yield []
    for _ in range(lax.axis_size("narrow") - 1):
        (moving,) = yield [parts[-1]]
        (moving,) = yield [shift(moving, -1)]
        parts.append(moving)
    return parts


def keys_flow(rows):
    bit = lax.axis_size("narrow") // 2
    yield []
    while bit:
        (rows,) = yield [rows]
        rows, other = yield [rows, swap(rows, bit)]
        rows = jnp.concatenate([rows, other], axis=0)
        bit //= 2
    return rows


def return_flow(parts):
    bit = 1
    yield []
    while bit < lax.axis_size("narrow"):
        half = parts[0].shape[0] // 2
        sent = yield [part[half:] for part in parts]
        got = yield [swap(other, bit) for other in sent]
        parts = [
            low(part[:half].astype(jnp.float32) + other.astype(jnp.float32))
            for part, other in zip(parts, got)
        ]
        bit *= 2
    return jnp.concatenate(parts, axis=1)


def gather_flow(rows):
    bits = wide_bits()
    count = lax.axis_size("narrow")
    columns = rows.shape[1]
    middle = columns // 2
    yield []
    (rows,) = yield [rows]
    ahead = yield [rows] + [shift(rows, -k) for k in range(1, count)]
    start = (count - lax.axis_index("narrow")) % count
    stacked = lax.dynamic_slice_in_dim(jnp.stack(ahead + ahead), start, count, axis=0)
    stacked = stacked.reshape((1,) * bits + stacked.shape)
    parts = [stacked[..., :middle], stacked[..., middle:]]
    orders = split_orders()
    for number in range(bits - 1):
        parts = yield parts
        tied = yield parts + [swap(part, 1 << o[number]) for part, o in zip(parts, orders)]
        parts = [join(tied[k], tied[k + 2], orders[k][number]) for k in range(2)]
    (whole,) = yield [jnp.concatenate(parts, axis=-1)]
    whole, other = yield [whole, swap(whole, 1)]
    return join(whole, other, 0).reshape(-1, columns)


def group_offsets():
    offsets, bit = [0], lax.axis_size("narrow") // 2
    while bit:
        offsets = offsets + [o ^ bit for o in offsets]
        bit //= 2
    return offsets


def feed_forward(stream, gain_vec, w_in, w_back):
    normed = low(rms_norm(stream, gain_vec))
    gate_up = dot_nn(normed, w_in)
    hidden = low(gated_unit(gate_up))
    return (dot_nt(hidden, w_back), (normed, gate_up, hidden))


def adamw(param, moment, second, grad, step_count):
    moment = beta_first * moment + (1 - beta_first) * grad
    second = beta_second * second + (1 - beta_second) * grad * grad
    steps = step_count.astype(jnp.float32)
    m_hat = moment / (1 - jnp.power(beta_first, steps))
    v_hat = second / (1 - jnp.power(beta_second, steps))
    return (
        param - rate_adam * (m_hat / (jnp.sqrt(v_hat) + adam_eps) + weight_decay * param),
        moment,
        second,
    )


def shards(
    patches,
    patch_rows,
    patch_cols,
    input_ids,
    target_ids,
    target_lengths,
    loss_mask,
    master_slabs,
    left_stats,
    left_roots,
    right_stats,
    right_roots,
    block_slot,
    vocab_table,
    vocab_first,
    vocab_second,
    small_params,
    small_first,
    small_second,
    step_count,
):
    wide_count = lax.axis_size("wide")
    narrow_count = lax.axis_size("narrow")
    devices = wide_count * narrow_count
    screen_sets = wide_count // narrow_count
    wide_pos = lax.axis_index("wide")
    narrow_pos = lax.axis_index("narrow")
    member = wide_pos % narrow_count
    slot_total = block_slot.shape[0]
    own_count = master_slabs.shape[0]
    piece = D // devices
    slot_ids = block_slot[:BLOCKS]
    enc_rows, dec_rows = patches.shape[0], input_ids.shape[0]
    vocab_rows, features = vocab_table.shape

    block_of_slot = (slot_ids[:, None] == jnp.arange(slot_total)[None, :]).astype(jnp.bfloat16)
    pieces = low(master_slabs).reshape(own_count, devices, piece, BW).transpose(1, 0, 2, 3)
    pieces = lax.all_to_all(pieces, BOTH, 0, 0)

    exchange = []
    for w in range(wide_count):
        for n in range(narrow_count):
            base = w // narrow_count * narrow_count
            exchange.append((w * narrow_count + n, (base + n) * narrow_count + w % narrow_count))
    whole_ids = lax.ppermute(
        jnp.concatenate([patch_rows, patch_cols, input_ids, target_ids]), BOTH, exchange
    )
    rows_ids, cols_ids = whole_ids[:enc_rows], whole_ids[enc_rows : 2 * enc_rows]
    token_ids = whole_ids[2 * enc_rows :].reshape(2, dec_rows)
    every_token = from_narrow(token_ids)
    every_token = every_token.reshape((1,) * wide_bits() + every_token.shape)
    every_token = join_wide(every_token, split_orders()[0] + [0])
    every_token = every_token.reshape(wide_count, narrow_count, 2, dec_rows)
    pieces, patches, every_token = tie(pieces, patches, every_token)
    layer_tokens = lax.dynamic_index_in_dim(every_token, narrow_pos, 1, keepdims=False)
    layer_targets = layer_tokens[:, 1].reshape(-1)
    patches = lax.ppermute(patches, BOTH, exchange)
    ordered = low(dot_nn(block_of_slot, pieces.reshape(slot_total, piece * BW)))
    row_shard = ordered.reshape(BLOCKS, piece, BW).transpose(1, 0, 2).reshape(piece, BLOCKS * BW)
    weights = [None] * len(EXTENTS)

    def shard_of(numbers):
        begin = sum(EXTENTS[: numbers[0]])
        return row_shard[:, begin : begin + sum(EXTENTS[n] for n in numbers)]

    def take(numbers, group):
        offset = 0
        for n in numbers:
            weights[n] = group[:, offset : offset + EXTENTS[n]]
            offset += EXTENTS[n]

    for numbers in GATHERS:
        take(numbers, lax.all_gather(shard_of(numbers), BOTH, axis=0, tiled=True))
    flow_weights = Flow(gather_flow(shard_of(PERMUTED)))

    padded = -(-vocab_rows // 256) * 256
    table_low = low(vocab_table)
    columns = jnp.arange(vocab_rows)
    vocab_start = wide_pos * vocab_rows
    flat_inputs = every_token[:, :, 0].reshape(-1) - vocab_start
    flat_targets = every_token[:, :, 1].reshape(-1) - vocab_start

    def looked_up(ids):
        onehot = (ids[:, None] == columns[None, :]).astype(jnp.bfloat16)
        found = low(dot_nn(onehot, table_low))
        return found.reshape(wide_count, narrow_count * dec_rows, features)

    def delivered(found):
        found = low(jnp.sum(found.astype(jnp.float32), axis=0))
        found = lax.all_to_all(found.reshape(narrow_count, dec_rows, features), "narrow", 0, 0)
        return found.transpose(1, 0, 2).reshape(dec_rows, D).astype(jnp.float32)

    flat_inputs = step(flat_inputs, flow_weights)
    found_inputs = looked_up(flat_inputs)
    found_inputs = step(found_inputs, flow_weights)
    found_inputs = lax.all_to_all(found_inputs, "wide", 0, 0)
    flow_table = Flow(table_flow(jnp.pad(table_low.T, ((0, 0), (0, padded - vocab_rows)))))

    gain_rows = small_params[2 * POS :]
    picked = jnp.concatenate(
        [
            rows_ids[:, None] == jnp.arange(POS)[None, :],
            cols_ids[:, None] == jnp.arange(POS)[None, :],
        ],
        axis=1,
    ).astype(jnp.bfloat16)
    tables = small_params[: 2 * POS]
    tables_high = low(tables)
    tables_rest = low(tables - tables_high.astype(jnp.float32))
    enc_zero = (
        dot_nn(patches, weights[0])
        + gain_rows[7]
        + dot_nn(picked, tables_high)
        + dot_nn(picked, tables_rest)
    )
    enc_zero = step(enc_zero, flow_weights)
    enc_normed = low(rms_norm(enc_zero, gain_rows[0]))
    enc_mix = low(dot_nn(enc_normed, weights[1]))
    enc_query = enc_mix[:, :D]
    flow_keys = Flow(keys_flow(enc_mix[:, D:]))
    enc_query, flat_targets, found_inputs = step(
        (enc_query, flat_targets, found_inputs), flow_keys, flow_table
    )
    found_targets = looked_up(flat_targets)
    dec_zero = delivered(found_inputs)
    enc_query, found_targets, dec_zero = step(
        (enc_query, found_targets, dec_zero), flow_keys, flow_weights, flow_table
    )
    found_targets = lax.all_to_all(found_targets, "wide", 0, 0)
    enc_query = step(enc_query, flow_keys)
    enc_keys = flow_keys.drain()
    enc_mixed, enc_total = attend(enc_query, enc_keys, None)
    enc_mixed = step(enc_mixed, flow_weights)
    take(PERMUTED, flow_weights.drain())
    enc_mixed, target_lengths, loss_mask = tie(enc_mixed, target_lengths, loss_mask)
    screens_info = lax.all_gather(
        jnp.concatenate([target_lengths[:, None], loss_mask], axis=1), "wide", axis=0, tiled=True
    )
    counted = (
        (jnp.arange(TGT)[None, :] < screens_info[:, :1]) & (screens_info[:, 1:] == 1)
    ).astype(jnp.float32)
    tokens_counted = jnp.maximum(jnp.sum(counted), 1.0)
    row_counted = lax.dynamic_index_in_dim(
        counted.reshape(screen_sets, narrow_count, TGT), narrow_pos, 1, keepdims=False
    ).reshape(-1)
    own_counted = lax.dynamic_slice_in_dim(row_counted, wide_pos * dec_rows, dec_rows)

    enc_one = enc_zero + dot_nn(enc_mixed, weights[2])
    enc_fnormed = low(rms_norm(enc_one, gain_rows[1]))
    enc_gate = dot_nn(enc_fnormed, weights[3])
    enc_hidden = low(gated_unit(enc_gate))
    enc_ffn = (enc_fnormed, enc_gate, enc_hidden)

    query_pos = (member * dec_rows + jnp.arange(dec_rows)).astype(jnp.int32)
    key_pos = jnp.concatenate(
        [(member ^ offset) * dec_rows + jnp.arange(dec_rows) for offset in group_offsets()]
    ).astype(jnp.int32)
    causal = (query_pos, key_pos)
    dec_normed = low(rms_norm(dec_zero, gain_rows[3]))
    dec_mix = low(dot_nn(dec_normed, weights[5]))
    flow_keys = Flow(keys_flow(dec_mix[:, D:]))
    enc_hidden, found_targets = step((enc_hidden, found_targets), flow_keys, flow_table)
    enc_two = enc_one + dot_nt(enc_hidden, weights[4])
    encoded = low(rms_norm(enc_two, gain_rows[2]))
    flow_cross = Flow(keys_flow(low(dot_nn(encoded, weights[8]))))
    dec_query = dec_mix[:, :D]
    dec_query, found_targets = step((dec_query, found_targets), flow_keys, flow_cross)
    target_rows = delivered(found_targets)
    dec_query = step(dec_query, flow_keys)
    self_keys = flow_keys.drain()
    self_mixed, self_total = attend(dec_query, self_keys, causal)
    dec_one = dec_zero + dot_nn(self_mixed, weights[6])
    cross_normed = low(rms_norm(dec_one, gain_rows[4]))
    cross_query = low(dot_nn(cross_normed, weights[7]))
    cross_query, target_rows = step((cross_query, target_rows), flow_cross)
    cross_query = step(cross_query, flow_cross)
    cross_keys = flow_cross.drain()
    cross_mixed, cross_total = attend(cross_query, cross_keys, None)
    dec_two = dec_one + dot_nn(cross_mixed, weights[9])
    branch, dec_ffn = feed_forward(dec_two, gain_rows[5], weights[10], weights[11])
    dec_three = dec_two + branch
    final = low(rms_norm(dec_three, gain_rows[6]) * D ** (-0.5))
    table = jnp.concatenate(flow_table.drain(), axis=0)

    rotated = lax.dynamic_slice_in_dim(
        jnp.concatenate([final, final], axis=1), narrow_pos * features, D, axis=1
    )
    rows_all = gather_wide_fast(rotated).reshape(-1, D)
    total_rows = rows_all.shape[0]
    block_rows = 256
    used = jnp.any(row_counted.reshape(-1, block_rows) != 0, axis=1).astype(jnp.int32)
    tile = padded // 5 if padded % 640 == 0 else 256
    mixed, exps, stats = head_forward(rows_all, table, used, vocab_rows, block_rows, tile)
    top_part, summed_part = stats[:, 0], stats[:, 1]
    stats_all = lax.all_gather(jnp.stack([top_part, summed_part]), "wide", axis=0)
    top_logit = jnp.max(stats_all[:, 0], axis=0)
    summed = jnp.sum(stats_all[:, 1] * jnp.exp(stats_all[:, 0] - top_logit), axis=0)
    log_total = top_logit + jnp.log(summed)
    row_weight = row_counted / tokens_counted
    scale = row_weight * jnp.exp(top_part - log_total)
    grad_rows = low(mixed * scale[:, None]).reshape(wide_count, dec_rows, D)
    grad_rows = lax.all_to_all(grad_rows, "wide", 0, 0)
    own_weight = own_counted / tokens_counted
    target_logit = jnp.sum(final.astype(jnp.float32) * target_rows, axis=1)
    own_total = lax.dynamic_slice_in_dim(log_total, wide_pos * dec_rows, dec_rows)
    loss_local = jnp.sum(own_counted * (own_total - target_logit))
    target_cols = (layer_targets - vocab_start).astype(jnp.float32)
    info = jnp.concatenate(
        [
            jnp.stack([scale, row_weight, target_cols], axis=1),
            jnp.zeros((total_rows, 125), jnp.float32),
        ],
        axis=1,
    )
    grad_table = table_grad(rows_all, exps, info, used, block_rows, tile)
    grad_parts = grad_table.reshape(narrow_count, features, padded)
    ring = Flow(ring_flow([grad_parts[k] for k in range(narrow_count)]))
    grad_rows = step(grad_rows, ring)
    grad_back = jnp.sum(grad_rows.astype(jnp.float32), axis=0)
    grad_back = lax.dynamic_slice_in_dim(
        jnp.concatenate([grad_back, grad_back], axis=1), (D - narrow_pos * features) % D, D, axis=1
    )
    grad_final = grad_back - own_weight[:, None] * target_rows

    grad_three, gain_final = norm_back(dec_three, gain_rows[6], grad_final * D ** (-0.5))
    low_three = low(grad_three)
    _, pullback = jax.vjp(gated_unit, dec_ffn[1])
    grad_gate = low(pullback(dot_nn(low_three, weights[11]))[0])
    flow_dffn = Flow(scatter_flow([(dec_ffn[0], grad_gate), (low_three, dec_ffn[2])]))
    grad_gate = step(grad_gate, flow_dffn)
    grad_two, gain_dffn = norm_back(dec_two, gain_rows[5], dot_nt(grad_gate, weights[10]))
    grad_two = grad_two + grad_three
    low_two = low(grad_two)
    grad_mixed = low(dot_nt(low_two, weights[9]))
    grad_mixed = step(grad_mixed, flow_dffn)
    grad_cq, grad_key, grad_value = attend_back(
        cross_query, cross_keys, None, cross_mixed, cross_total, grad_mixed
    )
    flow_cross = Flow(return_flow([grad_key, grad_value]))
    grad_cq = step(grad_cq, flow_cross, ring)
    grad_one, gain_cross = norm_back(dec_one, gain_rows[4], dot_nt(grad_cq, weights[7]))
    grad_one = grad_one + grad_two
    low_one = low(grad_one)
    grad_mixed = low(dot_nt(low_one, weights[6]))
    grad_mixed = step(grad_mixed, flow_cross)
    grad_sq, grad_key, grad_value = attend_back(
        dec_mix[:, :D], self_keys, causal, self_mixed, self_total, grad_mixed
    )
    flow_self = Flow(return_flow([grad_key, grad_value]))
    grad_sq = step(grad_sq, flow_self, flow_dffn)
    grad_sq = step(grad_sq, flow_self)
    grad_sq = step(grad_sq, flow_cross, ring)
    grad_ckv = flow_cross.drain()

    grad_two, gain_efinal = norm_back(enc_two, gain_rows[2], dot_nt(grad_ckv, weights[8]))
    low_etwo = low(grad_two)
    _, pullback = jax.vjp(gated_unit, enc_ffn[1])
    grad_gate = low(pullback(dot_nn(low_etwo, weights[4]))[0])
    grad_gate = step(grad_gate, flow_self, flow_dffn)
    grad_smix = jnp.concatenate([grad_sq, flow_self.drain()], axis=1)
    grad_zero, gain_self = norm_back(dec_zero, gain_rows[3], dot_nt(grad_smix, weights[5]))
    grad_tokens = low(grad_zero + grad_one)
    sent = grad_tokens.reshape(dec_rows, narrow_count, features).transpose(1, 0, 2)
    sent = lax.all_to_all(sent, "narrow", 0, 0).reshape(narrow_count * dec_rows, features)
    flow_dattn = Flow(
        scatter_flow(
            [
                (dec_normed, grad_smix),
                (self_mixed, low_one),
                (cross_normed, grad_cq),
                (encoded, grad_ckv),
                (cross_mixed, low_two),
            ]
        )
    )
    flow_effn = Flow(scatter_flow([(enc_ffn[0], grad_gate), (low_etwo, enc_ffn[2])]))
    grad_gate = step(grad_gate, flow_dattn, flow_effn, ring)
    grad_one, gain_effn = norm_back(enc_one, gain_rows[1], dot_nt(grad_gate, weights[3]))
    grad_one = grad_one + grad_two
    low_eone = low(grad_one)
    grad_mixed = low(dot_nt(low_eone, weights[2]))
    grad_mixed = step(grad_mixed, flow_dattn, flow_effn)
    grad_mixed, sent = step((grad_mixed, sent), flow_dffn)
    sent = lax.all_gather(sent, "wide", axis=0, tiled=True)
    grad_eq, grad_key, grad_value = attend_back(
        enc_mix[:, :D], enc_keys, None, enc_mixed, enc_total, grad_mixed
    )
    flow_enc = Flow(return_flow([grad_key, grad_value]))
    grad_eq = step(grad_eq, flow_enc)
    grad_eq = step(grad_eq, flow_enc)
    grad_eq, sent = step((grad_eq, sent), flow_dattn, flow_effn)
    onehot = (flat_inputs[:, None] == columns[None, :]).astype(jnp.bfloat16)
    looked_grad = dot_tn(onehot, sent)
    grad_eq, looked_grad = step((grad_eq, looked_grad), flow_enc)
    grad_eq = step(grad_eq, flow_dattn, flow_effn)
    grad_emix = jnp.concatenate([grad_eq, flow_enc.drain()], axis=1)
    grad_zero, gain_eattn = norm_back(enc_zero, gain_rows[0], dot_nt(grad_emix, weights[1]))
    grad_zero = grad_zero + grad_one
    low_zero = low(grad_zero)
    gains = [gain_eattn, gain_effn, gain_efinal, gain_self, gain_cross, gain_dffn, gain_final]
    width = -(-SMALL_ROWS // BW) * BW
    gains = jnp.pad(jnp.stack(gains, axis=1), ((0, 0), (2 * POS, width - 2 * POS - 7)))
    marks = (jnp.arange(width) == SMALL_ROWS - 1).astype(jnp.bfloat16)
    small_factor = marks[None, :] + jnp.pad(picked, ((0, 0), (0, width - 2 * POS)))
    flow_eattn = Flow(
        scatter_flow(
            [
                (patches, low_zero),
                (enc_normed, grad_emix),
                (enc_mixed, low_eone),
                (low_zero, small_factor),
            ],
            (5 * D, gains),
        )
    )
    looked_grad = step(looked_grad, flow_eattn)
    head_grad = ring.drain()[:, :vocab_rows].T
    vocab_grad = head_grad + looked_grad
    vocab_square = jnp.sum(vocab_grad * vocab_grad)
    vocab_square = step(vocab_square, flow_eattn)
    vocab_square = step(vocab_square, flow_dattn, flow_effn)
    vocab_square = step(vocab_square, flow_eattn)
    shard_dffn, shard_dattn = flow_dffn.drain(), flow_dattn.drain()
    shard_effn, shard_eattn = flow_effn.drain(), flow_eattn.drain()

    projection = shard_eattn[:, : 5 * D]
    small_shard = shard_eattn[:, 5 * D : 5 * D + SMALL_ROWS].astype(jnp.float32)
    grads = jnp.concatenate([projection, shard_effn, shard_dattn, shard_dffn], axis=1)
    partial_square = (
        jnp.sum(jnp.square(grads.astype(jnp.float32)))
        + vocab_square
        + jnp.sum(small_shard * small_shard)
    )
    scalars = jnp.where(
        jnp.arange(SMALL_ROWS)[None, :] == 0,
        partial_square,
        jnp.where(jnp.arange(SMALL_ROWS)[None, :] == 1, loss_local, 0.0),
    )
    slotted = grads.reshape(piece, BLOCKS, BW).transpose(1, 0, 2).reshape(BLOCKS, piece * BW)
    slotted = low(dot_tn(block_of_slot, slotted)).reshape(devices, own_count, piece, BW)
    small_shard, scalars, slotted = tie(small_shard, scalars, slotted)
    slab = lax.all_to_all(slotted, BOTH, 0, 0).transpose(1, 0, 2, 3).reshape(own_count, D, BW)
    shared = from_narrow(jnp.concatenate([small_shard, scalars], axis=0))
    shared = join_wide(shared.reshape((1,) * wide_bits() + shared.shape), split_orders()[0] + [0])
    shared = shared.reshape(devices, piece + 1, SMALL_ROWS)
    small_grad = shared[:, :piece].reshape(D, SMALL_ROWS).T
    total_square = jnp.sum(shared[:, piece, 0])
    loss_sum = jnp.sum(shared[:, piece, 1])

    grad_norm = jnp.sqrt(total_square)
    factor = jnp.minimum(1.0, clip_limit / (grad_norm + 1e-06))
    kept = (1 - stat_decay) * factor * factor
    slab_grad = slab.astype(jnp.float32) * factor
    left_new = stat_decay * left_stats + kept * jnp.einsum(
        "sik,sjk->sij", slab, slab, preferred_element_type=jnp.float32
    )
    right_new = stat_decay * right_stats + kept * jnp.einsum(
        "ski,skj->sij", slab, slab, preferred_element_type=jnp.float32
    )
    rooted = jnp.einsum("sij,sjk->sik", low(left_roots), slab, preferred_element_type=jnp.float32)
    precond = factor * jnp.einsum(
        "sij,sjk->sik", rooted, right_roots, precision=lax.Precision.HIGHEST
    )
    scale_back = lax.rsqrt(jnp.mean(precond * precond, axis=(1, 2), keepdims=True) + norm_eps)
    master_new = master_slabs - rate_shampoo * precond * scale_back
    vocab_new, vocab_first_new, vocab_second_new = adamw(
        vocab_table, vocab_first, vocab_second, vocab_grad * factor, step_count
    )
    small_new, small_first_new, small_second_new = adamw(
        small_params, small_first, small_second, small_grad * factor, step_count
    )
    return (
        loss_sum,
        tokens_counted,
        master_new,
        master_new.astype(jnp.bfloat16),
        slab_grad,
        left_new,
        right_new,
        vocab_new,
        vocab_new.astype(jnp.bfloat16),
        vocab_first_new,
        vocab_second_new,
        small_new,
        small_first_new,
        small_second_new,
        grad_norm,
    )


def solution(mesh):
    in_specs = (
        P(("wide", "narrow"), None),
        P(("wide", "narrow")),
        P(("wide", "narrow")),
        P(("wide", "narrow")),
        P(("wide", "narrow")),
        P("wide"),
        P("wide", None),
        P(("wide", "narrow"), None, None),
        P(("wide", "narrow"), None, None),
        P(("wide", "narrow"), None, None),
        P(("wide", "narrow"), None, None),
        P(("wide", "narrow"), None, None),
        P(),
        P("wide", "narrow"),
        P("wide", "narrow"),
        P("wide", "narrow"),
        P(),
        P(),
        P(),
        P(),
    )
    out_specs = (
        P(),
        P(),
        P(("wide", "narrow"), None, None),
        P(("wide", "narrow"), None, None),
        P(("wide", "narrow"), None, None),
        P(("wide", "narrow"), None, None),
        P(("wide", "narrow"), None, None),
        P("wide", "narrow"),
        P("wide", "narrow"),
        P("wide", "narrow"),
        P("wide", "narrow"),
        P(),
        P(),
        P(),
        P(),
    )
    return jax.shard_map(shards, mesh=mesh, in_specs=in_specs, out_specs=out_specs, check_vma=False)
```

```python
import jax
import jax.numpy as jnp
from jax import lax
from jax.experimental import pallas as pl
from jax.experimental.pallas import tpu as pltpu
from jax.sharding import PartitionSpec as P

HEAD_DIM = 64
D = 768
attn_scale = 0.125
KERNEL_VMEM = 56 * 1024 * 1024
SMALL_COST = pl.CostEstimate(flops=1 << 20, bytes_accessed=1 << 20, transcendentals=0)


def dot_nt(left, right):
    return lax.dot_general(
        left, right, (((1,), (1,)), ((), ())), preferred_element_type=jnp.float32
    )


def dot_nn(left, right):
    return lax.dot_general(
        left, right, (((1,), (0,)), ((), ())), preferred_element_type=jnp.float32
    )


def dot_tn(left, right):
    return lax.dot_general(
        left, right, (((0,), (0,)), ((), ())), preferred_element_type=jnp.float32
    )


def attend_kernel(masked, parts, row_step, *refs):
    if masked:
        query_pos, key_pos, refs = refs[0], refs[1], refs[2:]
    q_ref, pair_refs, out_ref, lse_ref = refs[0], refs[1 : 1 + parts], refs[-2], refs[-1]
    lane = lax.broadcasted_iota(jnp.int32, (row_step, 128), 1) // HEAD_DIM
    one = jnp.ones((), jnp.bfloat16)
    keys, sides, begins = [], [], [0]
    for pair_ref in pair_refs:
        keys.append(pair_ref[:, :128])
        values = pair_ref[:, 128:]
        key_lane = lax.broadcasted_iota(jnp.int32, values.shape, 1) // HEAD_DIM
        sides.append([jnp.where(key_lane == side, values, one) for side in range(2)])
        begins.append(begins[-1] + values.shape[0])
    for start in range(0, q_ref.shape[0], row_step):
        rows = pl.ds(start, row_step)
        queries = q_ref[rows, :]
        mixed, totals = [], []
        for side in range(2):
            half = jnp.where(lane == side, queries, jnp.zeros((), queries.dtype)) * attn_scale
            scores = [dot_nt(half.astype(jnp.bfloat16), part) for part in keys]
            if masked:
                scores = [
                    jnp.where(
                        key_pos[:, begins[k] : begins[k + 1]] <= query_pos[rows, :],
                        part,
                        -1000000000.0,
                    )
                    for k, part in enumerate(scores)
                ]
            top = jnp.max(scores[0], axis=1, keepdims=True)
            for part in scores[1:]:
                top = jnp.maximum(top, jnp.max(part, axis=1, keepdims=True))
            both = jnp.zeros((row_step, 128), jnp.float32)
            for part, values in zip(scores, sides):
                both += dot_nn(jnp.exp(part - top).astype(jnp.bfloat16), values[side])
            other = (1 - side) * HEAD_DIM
            summed = both[:, other : other + 1]
            mixed.append(both / summed)
            totals.append(top + jnp.log(summed))
        out_ref[rows, :] = jnp.where(lane == 0, mixed[0], mixed[1]).astype(out_ref.dtype)
        lse_ref[rows, :] = jnp.where(lane == 0, totals[0], totals[1])


def attend(queries, pairs, positions):
    rows, keys = queries.shape[0], sum(part.shape[0] for part in pairs)
    row_step = min(rows, 256)
    extra, extra_specs = (), []
    if positions is not None:
        query_pos, key_pos = positions
        extra = (query_pos.reshape(rows, 1), key_pos.reshape(1, keys))
        extra_specs = [
            pl.BlockSpec((rows, 1), lambda j: (0, 0)),
            pl.BlockSpec((1, keys), lambda j: (0, 0)),
        ]
    row_spec = pl.BlockSpec((rows, 128), lambda j: (0, j))
    return pl.pallas_call(
        lambda *refs: attend_kernel(positions is not None, len(pairs), row_step, *refs),
        grid=(D // 128,),
        in_specs=extra_specs
        + [row_spec]
        + [pl.BlockSpec((part.shape[0], 256), lambda j: (0, j)) for part in pairs],
        out_specs=[row_spec, row_spec],
        out_shape=[
            jax.ShapeDtypeStruct((rows, D), jnp.bfloat16),
            jax.ShapeDtypeStruct((rows, D), jnp.float32),
        ],
        compiler_params=pltpu.CompilerParams(vmem_limit_bytes=KERNEL_VMEM),
        cost_estimate=SMALL_COST,
    )(*extra, queries, *pairs)


def attend_back_kernel(masked, parts, *refs):
    if masked:
        query_pos, key_pos, refs = refs[0], refs[1], refs[2:]
    q_ref, pair_refs, refs = refs[0], refs[1 : 1 + parts], refs[1 + parts :]
    out_ref, lse_ref, grad_ref, dq_ref, pair_grad_ref = refs
    queries = q_ref[...]
    grads = grad_ref[...]
    lane = lax.broadcasted_iota(jnp.int32, queries.shape, 1) // HEAD_DIM
    zero = jnp.zeros((), queries.dtype)
    totals = lse_ref[...].T
    weighted = (grads.astype(jnp.float32) * out_ref[...].astype(jnp.float32)).T
    halves, grad_halves, total_rows, delta_rows, grad_queries = [], [], [], [], []
    for side in range(2):
        halves.append((jnp.where(lane == side, queries, zero) * attn_scale).astype(jnp.bfloat16))
        grad_halves.append(jnp.where(lane == side, grads, zero))
        total_rows.append(totals[side * HEAD_DIM : side * HEAD_DIM + 1, :])
        delta_rows.append(
            jnp.sum(weighted[side * HEAD_DIM : (side + 1) * HEAD_DIM, :], axis=0, keepdims=True)
        )
        grad_queries.append(jnp.zeros(queries.shape, jnp.float32))
    base = 0
    for pair_ref in pair_refs:
        key_step = min(pair_ref.shape[0], 512)
        for start in range(0, pair_ref.shape[0], key_step):
            here = pl.ds(start, key_step)
            rows = pl.ds(base + start, key_step)
            keys = pair_ref[here, :128]
            values = pair_ref[here, 128:]
            grad_keys = jnp.zeros(keys.shape, jnp.float32)
            grad_values = jnp.zeros(keys.shape, jnp.float32)
            for side in range(2):
                scores = dot_nt(keys, halves[side])
                probs = jnp.exp(scores - total_rows[side])
                if masked:
                    probs = jnp.where(key_pos[rows, :] <= query_pos[...], probs, 0.0)
                grad_probs = dot_nt(values, grad_halves[side])
                grad_scores = (probs * (grad_probs - delta_rows[side])).astype(jnp.bfloat16)
                grad_values += dot_nn(probs.astype(jnp.bfloat16), grad_halves[side])
                grad_keys += dot_nn(grad_scores, halves[side])
                grad_queries[side] += dot_tn(grad_scores, keys)
            pair_grad_ref[rows, :128] = grad_keys.astype(pair_grad_ref.dtype)
            pair_grad_ref[rows, 128:] = grad_values.astype(pair_grad_ref.dtype)
        base += pair_ref.shape[0]
    dq_ref[...] = (jnp.where(lane == 0, grad_queries[0], grad_queries[1]) * attn_scale).astype(
        dq_ref.dtype
    )


def attend_back(queries, pairs, positions, mixed_rows, log_total, grad_mixed):
    rows, keys = queries.shape[0], sum(part.shape[0] for part in pairs)
    extra, extra_specs = (), []
    if positions is not None:
        query_pos, key_pos = positions
        extra = (query_pos.reshape(1, rows), key_pos.reshape(keys, 1))
        extra_specs = [
            pl.BlockSpec((1, rows), lambda j: (0, 0)),
            pl.BlockSpec((keys, 1), lambda j: (0, 0)),
        ]
    row_spec = pl.BlockSpec((rows, 128), lambda j: (0, j))
    return pl.pallas_call(
        lambda *refs: attend_back_kernel(positions is not None, len(pairs), *refs),
        grid=(D // 128,),
        in_specs=extra_specs
        + [row_spec]
        + [pl.BlockSpec((part.shape[0], 256), lambda j: (0, j)) for part in pairs]
        + [row_spec] * 3,
        out_specs=[row_spec, pl.BlockSpec((keys, 256), lambda j: (0, j))],
        out_shape=[
            jax.ShapeDtypeStruct((rows, D), jnp.bfloat16),
            jax.ShapeDtypeStruct((keys, 2 * D), jnp.bfloat16),
        ],
        compiler_params=pltpu.CompilerParams(vmem_limit_bytes=KERNEL_VMEM),
        cost_estimate=SMALL_COST,
    )(*extra, queries, *pairs, mixed_rows, log_total, grad_mixed)


def head_kernel(vocab, tile, used_ref, rows_ref, table_ref, mixed_ref, exp_ref, stats_ref, logits_ref):
    step = pl.program_id(0)
    padded = table_ref.shape[1]
    shape = (rows_ref.shape[0], 128)
    lane = lax.broadcasted_iota(jnp.int32, shape, 1)

    @pl.when(used_ref[step] == 0)
    def _():
        mixed_ref[...] = jnp.zeros(mixed_ref.shape, mixed_ref.dtype)
        exp_ref[...] = jnp.zeros(exp_ref.shape, exp_ref.dtype)
        stats_ref[...] = jnp.where(lane == 1, 1.0, 0.0)

    @pl.when(used_ref[step] != 0)
    def _():
        rows = rows_ref[...]
        top = jnp.full((rows.shape[0], 1), -jnp.inf, jnp.float32)
        for start in range(0, padded, tile):
            logits = dot_nn(rows, table_ref[:, start : start + tile])
            if start + tile > vocab:
                column = start + lax.broadcasted_iota(jnp.int32, logits.shape, 1)
                logits = jnp.where(column < vocab, logits, -jnp.inf)
            logits_ref[:, start : start + tile] = logits
            top = jnp.maximum(top, jnp.max(logits, axis=1, keepdims=True))
        summed = jnp.zeros((rows.shape[0], 1), jnp.float32)
        mixed = jnp.zeros(mixed_ref.shape, jnp.float32)
        for start in range(0, padded, tile):
            exponent = jnp.exp(logits_ref[:, start : start + tile] - top)
            summed += jnp.sum(exponent, axis=1, keepdims=True)
            low = exponent.astype(jnp.bfloat16)
            exp_ref[:, start : start + tile] = low
            mixed += dot_nt(low, table_ref[:, start : start + tile])
        mixed_ref[...] = mixed
        stats_ref[...] = jnp.where(lane == 0, top, summed)


def head_forward(rows_all, table, used, vocab, block_rows, tile):
    rows, padded = rows_all.shape[0], table.shape[1]
    return pl.pallas_call(
        lambda *refs: head_kernel(vocab, tile, *refs),
        grid_spec=pltpu.PrefetchScalarGridSpec(
            num_scalar_prefetch=1,
            grid=(rows // block_rows,),
            in_specs=[
                pl.BlockSpec((block_rows, D), lambda i, used: (i, 0)),
                pl.BlockSpec((D, padded), lambda i, used: (0, 0), pipeline_mode=pl.Buffered(1)),
            ],
            out_specs=[
                pl.BlockSpec((block_rows, D), lambda i, used: (i, 0)),
                pl.BlockSpec((block_rows, padded), lambda i, used: (i, 0)),
                pl.BlockSpec((block_rows, 128), lambda i, used: (i, 0)),
            ],
            scratch_shapes=[pltpu.VMEM((block_rows, padded), jnp.float32)],
        ),
        out_shape=[
            jax.ShapeDtypeStruct((rows, D), jnp.float32),
            jax.ShapeDtypeStruct((rows, padded), jnp.bfloat16),
            jax.ShapeDtypeStruct((rows, 128), jnp.float32),
        ],
        compiler_params=pltpu.CompilerParams(vmem_limit_bytes=KERNEL_VMEM),
        cost_estimate=SMALL_COST,
    )(used, rows_all, table)


def table_grad_kernel(tile, used_ref, rows_ref, exp_ref, info_ref, grad_ref, total_ref):
    step = pl.program_id(0)

    @pl.when(step == 0)
    def _():
        total_ref[...] = jnp.zeros(total_ref.shape, total_ref.dtype)

    @pl.when(used_ref[step] != 0)
    def _():
        rows = rows_ref[...]
        scale = info_ref[:, 0:1]
        weight = info_ref[:, 1:2]
        target = info_ref[:, 2:3].astype(jnp.int32)
        for start in range(0, exp_ref.shape[1], tile):
            column = start + lax.broadcasted_iota(jnp.int32, (exp_ref.shape[0], tile), 1)
            probs = exp_ref[:, start : start + tile].astype(jnp.float32) * scale
            hits = jnp.where(column == target, weight, 0.0)
            grad_logits = (probs - hits).astype(jnp.bfloat16)
            total_ref[:, start : start + tile] += dot_tn(rows, grad_logits)

    @pl.when(step == pl.num_programs(0) - 1)
    def _():
        grad_ref[...] = total_ref[...].astype(grad_ref.dtype)


def table_grad(rows_all, exps, info, used, block_rows, tile):
    rows, padded = exps.shape
    return pl.pallas_call(
        lambda *refs: table_grad_kernel(tile, *refs),
        grid_spec=pltpu.PrefetchScalarGridSpec(
            num_scalar_prefetch=1,
            grid=(rows // block_rows,),
            in_specs=[
                pl.BlockSpec((block_rows, D), lambda i, used: (i, 0)),
                pl.BlockSpec((block_rows, padded), lambda i, used: (i, 0)),
                pl.BlockSpec((block_rows, 128), lambda i, used: (i, 0)),
            ],
            out_specs=pl.BlockSpec((D, padded), lambda i, used: (0, 0), pipeline_mode=pl.Buffered(1)),
            scratch_shapes=[pltpu.VMEM((D, padded), jnp.float32)],
        ),
        out_shape=jax.ShapeDtypeStruct((D, padded), jnp.bfloat16),
        compiler_params=pltpu.CompilerParams(vmem_limit_bytes=KERNEL_VMEM),
        cost_estimate=SMALL_COST,
    )(used, rows_all, exps, info)


def row_sums_kernel(step_rows, ids_ref, rows_ref, sums_ref):
    width, height = sums_ref.shape
    total = jnp.zeros((height, width), jnp.float32)
    for start in range(0, rows_ref.shape[1], step_rows):
        place = pl.program_id(0) * height + lax.broadcasted_iota(
            jnp.int32, (height, step_rows), 0
        )
        hits = jnp.where(place == ids_ref[:, start : start + step_rows], 1.0, 0.0)
        total += dot_nt(hits.astype(jnp.bfloat16), rows_ref[:, start : start + step_rows])
    sums_ref[...] = total.T


def row_sums(ids, rows, places):
    width, count = rows.shape
    height = 640 if places % 640 == 0 else 256
    return pl.pallas_call(
        lambda *refs: row_sums_kernel(1024, *refs),
        grid=(places // height,),
        in_specs=[
            pl.BlockSpec((1, count), lambda i: (0, 0)),
            pl.BlockSpec((width, count), lambda i: (0, 0), pipeline_mode=pl.Buffered(1)),
        ],
        out_specs=pl.BlockSpec((width, height), lambda i: (0, i)),
        out_shape=jax.ShapeDtypeStruct((width, places), jnp.float32),
        compiler_params=pltpu.CompilerParams(vmem_limit_bytes=KERNEL_VMEM),
        cost_estimate=SMALL_COST,
    )(ids.reshape(1, count), rows)


FF = 2048
POS = 256
TGT = 1024
BW = 128
BLOCKS = 174
EXTENTS = [D, 3 * D, D, 2 * FF, FF, 3 * D, D, D, 2 * D, D, 2 * FF, FF]
GATHERS = [[0, 1], [5, 6, 7, 8], [9, 10, 11]]
PERMUTED = [2, 3, 4]
SMALL_ROWS = 2 * POS + 8

norm_eps = 1e-06
clip_limit = 0.02
stat_decay = 0.5
rate_shampoo = 0.02
rate_adam = 0.5
beta_first = 0.9
beta_second = 0.95
adam_eps = 1e-08
weight_decay = 0.01
BOTH = ("wide", "narrow")


def block_order():
    order, offset = [], 0
    for number, extent in enumerate(EXTENTS):
        blocks = list(range(offset, offset + extent // BW))
        pairs = D // BW
        if number in (1, 5, 8):
            keys, values = blocks[-2 * pairs : -pairs], blocks[-pairs:]
            blocks = blocks[: -2 * pairs] + [b for both in zip(keys, values) for b in both]
        order += blocks
        offset += extent // BW
    return order


def rms_norm(values, gain_vec):
    return (
        values * lax.rsqrt(jnp.mean(values * values, axis=-1, keepdims=True) + norm_eps) * gain_vec
    )


def norm_back(values, gain_vec, grad_out):
    _, pullback = jax.vjp(rms_norm, values, gain_vec)
    return pullback(grad_out)


def low(values):
    return values.astype(jnp.bfloat16)


def gated_unit(gate_up):
    return jax.nn.gelu(gate_up[:, :FF], approximate=True) * gate_up[:, FF:]


def swap(values, bit):
    count = lax.axis_size("wide")
    return lax.ppermute(values, "wide", [(w, w ^ bit) for w in range(count)])


def shift(values, step):
    count = lax.axis_size("narrow")
    return lax.ppermute(values, "narrow", [(i, (i + step) % count) for i in range(count)])


def wide_bits():
    return lax.axis_size("wide").bit_length() - 1


def bit_value(level):
    return (lax.axis_index("wide") >> level) & 1


def gather_wide(values, order):
    bits = wide_bits()
    whole = join_wide(values.reshape((1,) * bits + values.shape), order)
    return whole.reshape((1 << bits,) + values.shape)


def split_orders():
    upper = list(range(1, wide_bits()))
    return upper, upper[::-1]


def gather_wide_fast(values):
    first, second = split_orders()
    half = values.shape[-1] // 2
    return jnp.concatenate(
        [gather_wide(values[..., :half], first + [0]), gather_wide(values[..., half:], second + [0])],
        axis=-1,
    )


def in_three(value):
    parts = []
    for _ in range(3):
        part = lax.reduce_precision(value, 8, 7)
        parts.append(low(part))
        value = value - part
    return parts


def tie(*values):
    return lax.optimization_barrier(values)


def from_narrow(rows):
    count = lax.axis_size("narrow")
    ahead = [rows] + [shift(rows, -step) for step in range(1, count)]
    start = (count - lax.axis_index("narrow")) % count
    return lax.dynamic_slice_in_dim(jnp.stack(ahead + ahead), start, count, axis=0)


def join(whole, other, level):
    axis = wide_bits() - 1 - level
    return jnp.where(
        bit_value(level) == 1,
        jnp.concatenate([other, whole], axis=axis),
        jnp.concatenate([whole, other], axis=axis),
    )


def join_wide(whole, order):
    for level in order:
        whole = join(whole, swap(whole, 1 << level), level)
    return whole


class Flow:
    def __init__(self, stages):
        self.stages, self.result, self.values = stages, None, None
        self.pull(None)

    def pull(self, values):
        try:
            self.values = self.stages.send(values)
        except StopIteration as end:
            self.result, self.values = end.value, None

    def drain(self):
        while self.values is not None:
            self.pull(self.values)
        return self.result


def step(main, *flows):
    for _ in range(2):
        live = [flow for flow in flows if flow.values is not None]
        main, values = lax.optimization_barrier((main, [flow.values for flow in live]))
        for flow, tied in zip(live, values):
            flow.pull(tied)
    return main


def scatter_flow(factors, extra=None):
    bits = wide_bits()
    count = lax.axis_size("narrow")
    here = lax.axis_index("narrow")
    pairs = 1 << (bits - 1)
    low_bit = bit_value(0)

    def products(side, got):
        results, offset = [], 0
        for left, right in factors:
            split = left.reshape(left.shape[0], pairs, 2, -1)
            chosen = lax.dynamic_index_in_dim(split, side, 2, keepdims=False)
            result = dot_tn(chosen.reshape(left.shape[0], -1), right)
            if got is not None:
                result = result + got[:, offset : offset + right.shape[1]].astype(jnp.float32)
            if extra is not None and extra[0] == offset:
                split = extra[1].reshape(pairs, 2, -1, right.shape[1])
                chosen = lax.dynamic_index_in_dim(split, side, 1, keepdims=False)
                result = result + chosen.reshape(result.shape)
            offset += right.shape[1]
            results.append(low(result))
        return jnp.concatenate(results, axis=1)

    yield []
    (sent,) = yield [products(1 - low_bit, None)]
    (got,) = yield [swap(sent, 1)]
    mine = products(low_bit, got)
    middle = mine.shape[1] // 256 * 128
    orders = split_orders()
    wholes = [
        part.reshape((2,) * (bits - 1) + (-1, part.shape[1]))
        for part in (mine[:, :middle], mine[:, middle:])
    ]
    for number in range(bits - 1):
        levels = [order[number] for order in orders]
        theirs = [
            lax.dynamic_index_in_dim(whole, 1 - bit_value(level), bits - 1 - level, keepdims=True)
            for whole, level in zip(wholes, levels)
        ]
        tied = yield wholes + theirs
        wholes, theirs = tied[:2], tied[2:]
        got = yield [swap(part, 1 << level) for part, level in zip(theirs, levels)]
        wholes = [
            low(
                lax.dynamic_index_in_dim(
                    whole, bit_value(level), bits - 1 - level, keepdims=True
                ).astype(jnp.float32)
                + part.astype(jnp.float32)
            )
            for whole, part, level in zip(wholes, got, levels)
        ]
    rows = jnp.concatenate([whole.reshape(count, -1, whole.shape[-1]) for whole in wholes], axis=-1)
    pieces = [
        lax.dynamic_index_in_dim(rows, (here + k) % count, 0, keepdims=False) for k in range(count)
    ]
    pieces = yield pieces
    got = yield [shift(pieces[k], k) for k in range(1, count)]
    total = pieces[0].astype(jnp.float32)
    for piece in got:
        total = total + piece.astype(jnp.float32)
    return low(total)


def ring_flow(parts):
    moving = parts[-1]
    yield []
    for part in parts[-2::-1]:
        (moving,) = yield [low(moving)]
        (moving,) = yield [shift(moving, 1)]
        moving = part.astype(jnp.float32) + moving.astype(jnp.float32)
    return moving


def table_flow(own):
    parts = [own]
    yield []
    for _ in range(lax.axis_size("narrow") - 1):
        (moving,) = yield [parts[-1]]
        (moving,) = yield [shift(moving, -1)]
        parts.append(moving)
    return parts


def keys_flow(rows):
    bit = lax.axis_size("narrow") // 2
    yield []
    while bit:
        (rows,) = yield [rows]
        rows, other = yield [rows, swap(rows, bit)]
        bit //= 2
        if bit:
            rows = jnp.concatenate([rows, other], axis=0)
    return [rows, other]


def return_flow(parts):
    bit = 1
    yield []
    while bit < lax.axis_size("narrow"):
        half = parts[0].shape[0] // 2
        sent = yield [part[half:] for part in parts]
        got = yield [swap(other, bit) for other in sent]
        parts = [
            low(part[:half].astype(jnp.float32) + other.astype(jnp.float32))
            for part, other in zip(parts, got)
        ]
        bit *= 2
    return parts[0]


def gather_flow(rows):
    bits = wide_bits()
    count = lax.axis_size("narrow")
    columns = rows.shape[1]
    middle = columns // 2
    yield []
    (rows,) = yield [rows]
    ahead = yield [rows] + [shift(rows, -k) for k in range(1, count)]
    start = (count - lax.axis_index("narrow")) % count
    stacked = lax.dynamic_slice_in_dim(jnp.stack(ahead + ahead), start, count, axis=0)
    stacked = stacked.reshape((1,) * bits + stacked.shape)
    parts = [stacked[..., :middle], stacked[..., middle:]]
    orders = split_orders()
    for number in range(bits - 1):
        parts = yield parts
        tied = yield parts + [swap(part, 1 << o[number]) for part, o in zip(parts, orders)]
        parts = [join(tied[k], tied[k + 2], orders[k][number]) for k in range(2)]
    (whole,) = yield [jnp.concatenate(parts, axis=-1)]
    whole, other = yield [whole, swap(whole, 1)]
    return join(whole, other, 0).reshape(-1, columns)


def group_offsets():
    offsets, bit = [0], lax.axis_size("narrow") // 2
    while bit:
        offsets = offsets + [o ^ bit for o in offsets]
        bit //= 2
    return offsets


def feed_forward(stream, gain_vec, w_in, w_back):
    normed = low(rms_norm(stream, gain_vec))
    gate_up = dot_nn(normed, w_in)
    hidden = low(gated_unit(gate_up))
    return (dot_nt(hidden, w_back), (normed, gate_up, hidden))


def adamw(param, moment, second, grad, step_count):
    moment = beta_first * moment + (1 - beta_first) * grad
    second = beta_second * second + (1 - beta_second) * grad * grad
    steps = step_count.astype(jnp.float32)
    m_hat = moment / (1 - jnp.power(beta_first, steps))
    v_hat = second / (1 - jnp.power(beta_second, steps))
    return (
        param - rate_adam * (m_hat / (jnp.sqrt(v_hat) + adam_eps) + weight_decay * param),
        moment,
        second,
    )


def shards(
    patches,
    patch_rows,
    patch_cols,
    input_ids,
    target_ids,
    target_lengths,
    loss_mask,
    master_slabs,
    left_stats,
    left_roots,
    right_stats,
    right_roots,
    block_slot,
    vocab_table,
    vocab_first,
    vocab_second,
    small_params,
    small_first,
    small_second,
    step_count,
):
    wide_count = lax.axis_size("wide")
    narrow_count = lax.axis_size("narrow")
    devices = wide_count * narrow_count
    screen_sets = wide_count // narrow_count
    wide_pos = lax.axis_index("wide")
    narrow_pos = lax.axis_index("narrow")
    member = wide_pos % narrow_count
    slot_total = block_slot.shape[0]
    own_count = master_slabs.shape[0]
    piece = D // devices
    slot_ids = block_slot[jnp.array(block_order())]
    enc_rows, dec_rows = patches.shape[0], input_ids.shape[0]
    vocab_rows, features = vocab_table.shape

    block_of_slot = (slot_ids[:, None] == jnp.arange(slot_total)[None, :]).astype(jnp.bfloat16)
    pieces = low(master_slabs).reshape(own_count, devices, piece, BW).transpose(1, 0, 2, 3)
    pieces = lax.all_to_all(pieces, BOTH, 0, 0)

    exchange = []
    for w in range(wide_count):
        for n in range(narrow_count):
            base = w // narrow_count * narrow_count
            exchange.append((w * narrow_count + n, (base + n) * narrow_count + w % narrow_count))
    whole_ids = lax.ppermute(
        jnp.concatenate([patch_rows, patch_cols, input_ids, target_ids]), BOTH, exchange
    )
    rows_ids, cols_ids = whole_ids[:enc_rows], whole_ids[enc_rows : 2 * enc_rows]
    token_ids = whole_ids[2 * enc_rows :].reshape(2, dec_rows)
    every_token = from_narrow(token_ids)
    every_token = every_token.reshape((1,) * wide_bits() + every_token.shape)
    every_token = join_wide(every_token, split_orders()[0] + [0])
    every_token = every_token.reshape(wide_count, narrow_count, 2, dec_rows)
    pieces, patches, every_token = tie(pieces, patches, every_token)
    layer_tokens = lax.dynamic_index_in_dim(every_token, narrow_pos, 1, keepdims=False)
    layer_targets = layer_tokens[:, 1].reshape(-1)
    patches = lax.ppermute(patches, BOTH, exchange)
    ordered = low(dot_nn(block_of_slot, pieces.reshape(slot_total, piece * BW)))
    row_shard = ordered.reshape(BLOCKS, piece, BW).transpose(1, 0, 2).reshape(piece, BLOCKS * BW)
    weights = [None] * len(EXTENTS)

    def shard_of(numbers):
        begin = sum(EXTENTS[: numbers[0]])
        return row_shard[:, begin : begin + sum(EXTENTS[n] for n in numbers)]

    def take(numbers, group):
        offset = 0
        for n in numbers:
            weights[n] = group[:, offset : offset + EXTENTS[n]]
            offset += EXTENTS[n]

    for numbers in GATHERS:
        take(numbers, lax.all_gather(shard_of(numbers), BOTH, axis=0, tiled=True))
    flow_weights = Flow(gather_flow(shard_of(PERMUTED)))

    padded = -(-vocab_rows // 256) * 256
    table_low = low(vocab_table)
    columns = jnp.arange(vocab_rows)
    vocab_start = wide_pos * vocab_rows
    flat_inputs = every_token[:, :, 0].reshape(-1) - vocab_start
    flat_targets = every_token[:, :, 1].reshape(-1) - vocab_start

    def looked_up(ids):
        onehot = (ids[:, None] == columns[None, :]).astype(jnp.bfloat16)
        found = low(dot_nn(onehot, table_low))
        return found.reshape(wide_count, narrow_count * dec_rows, features)

    def delivered(found):
        found = low(jnp.sum(found.astype(jnp.float32), axis=0))
        found = lax.all_to_all(found.reshape(narrow_count, dec_rows, features), "narrow", 0, 0)
        return found.transpose(1, 0, 2).reshape(dec_rows, D).astype(jnp.float32)

    flat_inputs = step(flat_inputs, flow_weights)
    found_inputs = looked_up(flat_inputs)
    found_inputs = step(found_inputs, flow_weights)
    found_inputs = lax.all_to_all(found_inputs, "wide", 0, 0)
    flow_table = Flow(table_flow(jnp.pad(table_low.T, ((0, 0), (0, padded - vocab_rows)))))

    gain_rows = small_params[2 * POS :]
    picked = jnp.concatenate(
        [
            rows_ids[:, None] == jnp.arange(POS)[None, :],
            cols_ids[:, None] == jnp.arange(POS)[None, :],
        ],
        axis=1,
    ).astype(jnp.bfloat16)
    tables = small_params[: 2 * POS]
    tables_high = low(tables)
    tables_rest = low(tables - tables_high.astype(jnp.float32))
    enc_zero = (
        dot_nn(patches, weights[0])
        + gain_rows[7]
        + dot_nn(picked, tables_high)
        + dot_nn(picked, tables_rest)
    )
    enc_zero = step(enc_zero, flow_weights)
    enc_normed = low(rms_norm(enc_zero, gain_rows[0]))
    enc_mix = low(dot_nn(enc_normed, weights[1]))
    enc_query = enc_mix[:, :D]
    flow_keys = Flow(keys_flow(enc_mix[:, D:]))
    enc_query, flat_targets, found_inputs = step(
        (enc_query, flat_targets, found_inputs), flow_keys, flow_table
    )
    found_targets = looked_up(flat_targets)
    dec_zero = delivered(found_inputs)
    enc_query, found_targets, dec_zero = step(
        (enc_query, found_targets, dec_zero), flow_keys, flow_weights, flow_table
    )
    found_targets = lax.all_to_all(found_targets, "wide", 0, 0)
    enc_query = step(enc_query, flow_keys)
    enc_keys = flow_keys.drain()
    enc_mixed, enc_total = attend(enc_query, enc_keys, None)
    enc_mixed = step(enc_mixed, flow_weights)
    take(PERMUTED, flow_weights.drain())
    enc_mixed, target_lengths, loss_mask = tie(enc_mixed, target_lengths, loss_mask)
    screens_info = lax.all_gather(
        jnp.concatenate([target_lengths[:, None], loss_mask], axis=1), "wide", axis=0, tiled=True
    )
    counted = (
        (jnp.arange(TGT)[None, :] < screens_info[:, :1]) & (screens_info[:, 1:] == 1)
    ).astype(jnp.float32)
    tokens_counted = jnp.maximum(jnp.sum(counted), 1.0)
    row_counted = lax.dynamic_index_in_dim(
        counted.reshape(screen_sets, narrow_count, TGT), narrow_pos, 1, keepdims=False
    ).reshape(-1)
    own_counted = lax.dynamic_slice_in_dim(row_counted, wide_pos * dec_rows, dec_rows)

    enc_one = enc_zero + dot_nn(enc_mixed, weights[2])
    enc_fnormed = low(rms_norm(enc_one, gain_rows[1]))
    enc_gate = dot_nn(enc_fnormed, weights[3])
    enc_hidden = low(gated_unit(enc_gate))
    enc_ffn = (enc_fnormed, enc_gate, enc_hidden)

    query_pos = (member * dec_rows + jnp.arange(dec_rows)).astype(jnp.int32)
    key_pos = jnp.concatenate(
        [(member ^ offset) * dec_rows + jnp.arange(dec_rows) for offset in group_offsets()]
    ).astype(jnp.int32)
    causal = (query_pos, key_pos)
    dec_normed = low(rms_norm(dec_zero, gain_rows[3]))
    dec_mix = low(dot_nn(dec_normed, weights[5]))
    flow_keys = Flow(keys_flow(dec_mix[:, D:]))
    enc_hidden, found_targets = step((enc_hidden, found_targets), flow_keys, flow_table)
    enc_two = enc_one + dot_nt(enc_hidden, weights[4])
    encoded = low(rms_norm(enc_two, gain_rows[2]))
    flow_cross = Flow(keys_flow(low(dot_nn(encoded, weights[8]))))
    dec_query = dec_mix[:, :D]
    dec_query, found_targets = step((dec_query, found_targets), flow_keys, flow_cross)
    target_rows = delivered(found_targets)
    dec_query = step(dec_query, flow_keys)
    self_keys = flow_keys.drain()
    self_mixed, self_total = attend(dec_query, self_keys, causal)
    dec_one = dec_zero + dot_nn(self_mixed, weights[6])
    cross_normed = low(rms_norm(dec_one, gain_rows[4]))
    cross_query = low(dot_nn(cross_normed, weights[7]))
    cross_query, target_rows = step((cross_query, target_rows), flow_cross)
    cross_query = step(cross_query, flow_cross)
    cross_keys = flow_cross.drain()
    cross_mixed, cross_total = attend(cross_query, cross_keys, None)
    dec_two = dec_one + dot_nn(cross_mixed, weights[9])
    branch, dec_ffn = feed_forward(dec_two, gain_rows[5], weights[10], weights[11])
    dec_three = dec_two + branch
    final = low(rms_norm(dec_three, gain_rows[6]) * D ** (-0.5))
    table = jnp.concatenate(flow_table.drain(), axis=0)

    rotated = lax.dynamic_slice_in_dim(
        jnp.concatenate([final, final], axis=1), narrow_pos * features, D, axis=1
    )
    rows_all = gather_wide_fast(rotated).reshape(-1, D)
    total_rows = rows_all.shape[0]
    block_rows = 256
    used = jnp.any(row_counted.reshape(-1, block_rows) != 0, axis=1).astype(jnp.int32)
    tile = padded // 5 if padded % 640 == 0 else 256
    mixed, exps, stats = head_forward(rows_all, table, used, vocab_rows, block_rows, tile)
    top_part, summed_part = stats[:, 0], stats[:, 1]
    stats_all = lax.all_gather(jnp.stack([top_part, summed_part]), "wide", axis=0)
    top_logit = jnp.max(stats_all[:, 0], axis=0)
    summed = jnp.sum(stats_all[:, 1] * jnp.exp(stats_all[:, 0] - top_logit), axis=0)
    log_total = top_logit + jnp.log(summed)
    row_weight = row_counted / tokens_counted
    scale = row_weight * jnp.exp(top_part - log_total)
    grad_rows = low(mixed * scale[:, None]).reshape(wide_count, dec_rows, D)
    grad_rows = lax.all_to_all(grad_rows, "wide", 0, 0)
    own_weight = own_counted / tokens_counted
    target_logit = jnp.sum(final.astype(jnp.float32) * target_rows, axis=1)
    own_total = lax.dynamic_slice_in_dim(log_total, wide_pos * dec_rows, dec_rows)
    loss_local = jnp.sum(own_counted * (own_total - target_logit))
    target_cols = (layer_targets - vocab_start).astype(jnp.float32)
    info = jnp.concatenate(
        [
            jnp.stack([scale, row_weight, target_cols], axis=1),
            jnp.zeros((total_rows, 125), jnp.float32),
        ],
        axis=1,
    )
    grad_table = table_grad(rows_all, exps, info, used, block_rows, tile)
    grad_parts = grad_table.reshape(narrow_count, features, padded)
    ring = Flow(ring_flow([grad_parts[k] for k in range(narrow_count)]))
    grad_rows = step(grad_rows, ring)
    grad_back = jnp.sum(grad_rows.astype(jnp.float32), axis=0)
    grad_back = lax.dynamic_slice_in_dim(
        jnp.concatenate([grad_back, grad_back], axis=1), (D - narrow_pos * features) % D, D, axis=1
    )
    grad_final = grad_back - own_weight[:, None] * target_rows

    grad_three, gain_final = norm_back(dec_three, gain_rows[6], grad_final * D ** (-0.5))
    low_three = low(grad_three)
    _, pullback = jax.vjp(gated_unit, dec_ffn[1])
    grad_gate = low(pullback(dot_nn(low_three, weights[11]))[0])
    flow_dffn = Flow(scatter_flow([(dec_ffn[0], grad_gate), (low_three, dec_ffn[2])]))
    grad_gate = step(grad_gate, flow_dffn)
    grad_two, gain_dffn = norm_back(dec_two, gain_rows[5], dot_nt(grad_gate, weights[10]))
    grad_two = grad_two + grad_three
    low_two = low(grad_two)
    grad_mixed = low(dot_nt(low_two, weights[9]))
    grad_mixed = step(grad_mixed, flow_dffn)
    grad_cq, grad_pair = attend_back(
        cross_query, cross_keys, None, cross_mixed, cross_total, grad_mixed
    )
    flow_cross = Flow(return_flow([grad_pair]))
    grad_cq = step(grad_cq, flow_cross, ring)
    grad_one, gain_cross = norm_back(dec_one, gain_rows[4], dot_nt(grad_cq, weights[7]))
    grad_one = grad_one + grad_two
    low_one = low(grad_one)
    grad_mixed = low(dot_nt(low_one, weights[6]))
    grad_mixed = step(grad_mixed, flow_cross)
    grad_sq, grad_pair = attend_back(
        dec_mix[:, :D], self_keys, causal, self_mixed, self_total, grad_mixed
    )
    flow_self = Flow(return_flow([grad_pair]))
    grad_sq = step(grad_sq, flow_self, flow_dffn)
    grad_sq = step(grad_sq, flow_self)
    grad_sq = step(grad_sq, flow_cross, ring)
    grad_ckv = flow_cross.drain()

    grad_two, gain_efinal = norm_back(enc_two, gain_rows[2], dot_nt(grad_ckv, weights[8]))
    low_etwo = low(grad_two)
    _, pullback = jax.vjp(gated_unit, enc_ffn[1])
    grad_gate = low(pullback(dot_nn(low_etwo, weights[4]))[0])
    grad_gate = step(grad_gate, flow_self, flow_dffn)
    grad_smix = jnp.concatenate([grad_sq, flow_self.drain()], axis=1)
    grad_zero, gain_self = norm_back(dec_zero, gain_rows[3], dot_nt(grad_smix, weights[5]))
    grad_tokens = low(grad_zero + grad_one)
    sent = grad_tokens.reshape(dec_rows, narrow_count, features).transpose(1, 0, 2)
    sent = lax.all_to_all(sent, "narrow", 0, 0).reshape(narrow_count * dec_rows, features)
    flow_dattn = Flow(
        scatter_flow(
            [
                (dec_normed, grad_smix),
                (self_mixed, low_one),
                (cross_normed, grad_cq),
                (encoded, grad_ckv),
                (cross_mixed, low_two),
            ]
        )
    )
    flow_effn = Flow(scatter_flow([(enc_ffn[0], grad_gate), (low_etwo, enc_ffn[2])]))
    grad_gate = step(grad_gate, flow_dattn, flow_effn, ring)
    grad_one, gain_effn = norm_back(enc_one, gain_rows[1], dot_nt(grad_gate, weights[3]))
    grad_one = grad_one + grad_two
    low_eone = low(grad_one)
    grad_mixed = low(dot_nt(low_eone, weights[2]))
    grad_mixed = step(grad_mixed, flow_dattn, flow_effn)
    grad_mixed, sent = step((grad_mixed, sent), flow_dffn)
    sent = lax.all_gather(sent, "wide", axis=0, tiled=True)
    grad_eq, grad_pair = attend_back(
        enc_mix[:, :D], enc_keys, None, enc_mixed, enc_total, grad_mixed
    )
    grad_eq = step(grad_eq, flow_dattn, flow_effn)
    flow_enc = Flow(return_flow([grad_pair]))
    grad_eq = step(grad_eq, flow_enc)
    grad_eq, sent = step((grad_eq, sent), flow_enc)
    looked_grad = row_sums(flat_inputs, sent.T, padded)
    grad_eq, looked_grad = step((grad_eq, looked_grad), flow_enc)
    grad_eq, looked_grad = step((grad_eq, looked_grad), flow_dattn, flow_effn)
    grad_emix = jnp.concatenate([grad_eq, flow_enc.drain()], axis=1)
    grad_zero, gain_eattn = norm_back(enc_zero, gain_rows[0], dot_nt(grad_emix, weights[1]))
    grad_zero = grad_zero + grad_one
    low_zero = low(grad_zero)
    gains = [gain_eattn, gain_effn, gain_efinal, gain_self, gain_cross, gain_dffn, gain_final]
    width = -(-SMALL_ROWS // BW) * BW
    gains = jnp.pad(jnp.stack(gains, axis=1), ((0, 0), (2 * POS, width - 2 * POS - 7)))
    marks = (jnp.arange(width) == SMALL_ROWS - 1).astype(jnp.bfloat16)
    small_factor = marks[None, :] + jnp.pad(picked, ((0, 0), (0, width - 2 * POS)))
    flow_eattn = Flow(
        scatter_flow(
            [
                (patches, low_zero),
                (enc_normed, grad_emix),
                (enc_mixed, low_eone),
                (low_zero, small_factor),
            ],
            (5 * D, gains),
        )
    )
    looked_grad = step(looked_grad, flow_eattn)
    vocab_grad = (ring.drain() + looked_grad)[:, :vocab_rows].T
    vocab_square = jnp.sum(vocab_grad * vocab_grad)
    vocab_square = step(vocab_square, flow_eattn)
    vocab_square = step(vocab_square, flow_dattn, flow_effn)
    vocab_square = step(vocab_square, flow_eattn)
    vocab_square = step(vocab_square, flow_eattn)
    shard_dffn, shard_dattn = flow_dffn.drain(), flow_dattn.drain()
    shard_effn, shard_eattn = flow_effn.drain(), flow_eattn.drain()

    projection = shard_eattn[:, : 5 * D]
    small_shard = shard_eattn[:, 5 * D : 5 * D + SMALL_ROWS].astype(jnp.float32)
    grads = jnp.concatenate([projection, shard_effn, shard_dattn, shard_dffn], axis=1)
    partial_square = (
        jnp.sum(jnp.square(grads.astype(jnp.float32)))
        + vocab_square
        + jnp.sum(small_shard * small_shard)
    )
    scalars = jnp.stack(in_three(partial_square) + in_three(loss_local))
    scalars = jnp.pad(scalars[None, :], ((0, 0), (0, SMALL_ROWS - 6)))
    slotted = grads.reshape(piece, BLOCKS, BW).transpose(1, 0, 2).reshape(BLOCKS, piece * BW)
    slotted = low(dot_tn(block_of_slot, slotted)).reshape(devices, own_count, piece, BW)
    small_shard, scalars, slotted = tie(small_shard, scalars, slotted)
    slab = lax.all_to_all(slotted, BOTH, 0, 0).transpose(1, 0, 2, 3).reshape(own_count, D, BW)
    shared = from_narrow(jnp.concatenate([low(small_shard), scalars], axis=0))
    shared = join_wide(shared.reshape((1,) * wide_bits() + shared.shape), split_orders()[0] + [0])
    shared = shared.reshape(devices, piece + 1, SMALL_ROWS).astype(jnp.float32)
    small_grad = shared[:, :piece].reshape(D, SMALL_ROWS).T
    total_square = jnp.sum(shared[:, piece, :3])
    loss_sum = jnp.sum(shared[:, piece, 3:6])

    grad_norm = jnp.sqrt(total_square)
    factor = jnp.minimum(1.0, clip_limit / (grad_norm + 1e-06))
    kept = (1 - stat_decay) * factor * factor
    slab_grad = slab.astype(jnp.float32) * factor
    left_new = stat_decay * left_stats + kept * jnp.einsum(
        "sik,sjk->sij", slab, slab, preferred_element_type=jnp.float32
    )
    right_new = stat_decay * right_stats + kept * jnp.einsum(
        "ski,skj->sij", slab, slab, preferred_element_type=jnp.float32
    )
    rooted = jnp.einsum("sij,sjk->sik", low(left_roots), slab, preferred_element_type=jnp.float32)
    precond = factor * jnp.einsum(
        "sij,sjk->sik", rooted, right_roots, precision=lax.Precision.HIGHEST
    )
    scale_back = lax.rsqrt(jnp.mean(precond * precond, axis=(1, 2), keepdims=True) + norm_eps)
    master_new = master_slabs - rate_shampoo * precond * scale_back
    vocab_new, vocab_first_new, vocab_second_new = adamw(
        vocab_table, vocab_first, vocab_second, vocab_grad * factor, step_count
    )
    small_new, small_first_new, small_second_new = adamw(
        small_params, small_first, small_second, small_grad * factor, step_count
    )
    return (
        loss_sum,
        tokens_counted,
        master_new,
        master_new.astype(jnp.bfloat16),
        slab_grad,
        left_new,
        right_new,
        vocab_new,
        vocab_new.astype(jnp.bfloat16),
        vocab_first_new,
        vocab_second_new,
        small_new,
        small_first_new,
        small_second_new,
        grad_norm,
    )


def solution(mesh):
    in_specs = (
        P(("wide", "narrow"), None),
        P(("wide", "narrow")),
        P(("wide", "narrow")),
        P(("wide", "narrow")),
        P(("wide", "narrow")),
        P("wide"),
        P("wide", None),
        P(("wide", "narrow"), None, None),
        P(("wide", "narrow"), None, None),
        P(("wide", "narrow"), None, None),
        P(("wide", "narrow"), None, None),
        P(("wide", "narrow"), None, None),
        P(),
        P("wide", "narrow"),
        P("wide", "narrow"),
        P("wide", "narrow"),
        P(),
        P(),
        P(),
        P(),
    )
    out_specs = (
        P(),
        P(),
        P(("wide", "narrow"), None, None),
        P(("wide", "narrow"), None, None),
        P(("wide", "narrow"), None, None),
        P(("wide", "narrow"), None, None),
        P(("wide", "narrow"), None, None),
        P("wide", "narrow"),
        P("wide", "narrow"),
        P("wide", "narrow"),
        P("wide", "narrow"),
        P(),
        P(),
        P(),
        P(),
    )
    return jax.shard_map(shards, mesh=mesh, in_specs=in_specs, out_specs=out_specs, check_vma=False)
```

```python
import jax
import jax.numpy as jnp
from jax import lax
from jax.experimental import pallas as pl
from jax.experimental.pallas import tpu as pltpu
from jax.sharding import PartitionSpec as P

HEAD_DIM = 64
D = 768
attn_scale = 0.125
KERNEL_VMEM = 56 * 1024 * 1024
SMALL_COST = pl.CostEstimate(flops=1 << 20, bytes_accessed=1 << 20, transcendentals=0)


def dot_nt(left, right):
    return lax.dot_general(
        left, right, (((1,), (1,)), ((), ())), preferred_element_type=jnp.float32
    )


def dot_nn(left, right):
    return lax.dot_general(
        left, right, (((1,), (0,)), ((), ())), preferred_element_type=jnp.float32
    )


def dot_tn(left, right):
    return lax.dot_general(
        left, right, (((0,), (0,)), ((), ())), preferred_element_type=jnp.float32
    )


def attend_kernel(masked, parts, row_step, *refs):
    if masked:
        query_pos, key_pos, refs = refs[0], refs[1], refs[2:]
    q_ref, pair_refs, out_ref, lse_ref = refs[0], refs[1 : 1 + parts], refs[-2], refs[-1]
    lane = lax.broadcasted_iota(jnp.int32, (row_step, 128), 1) // HEAD_DIM
    one = jnp.ones((), jnp.bfloat16)
    keys, sides, begins = [], [], [0]
    for pair_ref in pair_refs:
        keys.append(pair_ref[:, :128])
        values = pair_ref[:, 128:]
        key_lane = lax.broadcasted_iota(jnp.int32, values.shape, 1) // HEAD_DIM
        sides.append([jnp.where(key_lane == side, values, one) for side in range(2)])
        begins.append(begins[-1] + values.shape[0])
    for start in range(0, q_ref.shape[0], row_step):
        rows = pl.ds(start, row_step)
        queries = q_ref[rows, :]
        mixed, totals = [], []
        for side in range(2):
            half = jnp.where(lane == side, queries, jnp.zeros((), queries.dtype)) * attn_scale
            scores = [dot_nt(half.astype(jnp.bfloat16), part) for part in keys]
            if masked:
                scores = [
                    jnp.where(
                        key_pos[:, begins[k] : begins[k + 1]] <= query_pos[rows, :],
                        part,
                        -1000000000.0,
                    )
                    for k, part in enumerate(scores)
                ]
            top = jnp.max(scores[0], axis=1, keepdims=True)
            for part in scores[1:]:
                top = jnp.maximum(top, jnp.max(part, axis=1, keepdims=True))
            both = jnp.zeros((row_step, 128), jnp.float32)
            for part, values in zip(scores, sides):
                both += dot_nn(jnp.exp(part - top).astype(jnp.bfloat16), values[side])
            other = (1 - side) * HEAD_DIM
            summed = both[:, other : other + 1]
            mixed.append(both / summed)
            totals.append(top + jnp.log(summed))
        out_ref[rows, :] = jnp.where(lane == 0, mixed[0], mixed[1]).astype(out_ref.dtype)
        lse_ref[rows, :] = jnp.where(lane == 0, totals[0], totals[1])


def attend(queries, pairs, positions):
    rows, keys = queries.shape[0], sum(part.shape[0] for part in pairs)
    row_step = min(rows, 256)
    extra, extra_specs = (), []
    if positions is not None:
        query_pos, key_pos = positions
        extra = (query_pos.reshape(rows, 1), key_pos.reshape(1, keys))
        extra_specs = [
            pl.BlockSpec((rows, 1), lambda j: (0, 0)),
            pl.BlockSpec((1, keys), lambda j: (0, 0)),
        ]
    row_spec = pl.BlockSpec((rows, 128), lambda j: (0, j))
    return pl.pallas_call(
        lambda *refs: attend_kernel(positions is not None, len(pairs), row_step, *refs),
        grid=(D // 128,),
        in_specs=extra_specs
        + [row_spec]
        + [pl.BlockSpec((part.shape[0], 256), lambda j: (0, j)) for part in pairs],
        out_specs=[row_spec, row_spec],
        out_shape=[
            jax.ShapeDtypeStruct((rows, D), jnp.bfloat16),
            jax.ShapeDtypeStruct((rows, D), jnp.float32),
        ],
        compiler_params=pltpu.CompilerParams(vmem_limit_bytes=KERNEL_VMEM),
        cost_estimate=SMALL_COST,
    )(*extra, queries, *pairs)


def attend_back_kernel(masked, parts, *refs):
    if masked:
        query_pos, key_pos, refs = refs[0], refs[1], refs[2:]
    q_ref, pair_refs, refs = refs[0], refs[1 : 1 + parts], refs[1 + parts :]
    out_ref, lse_ref, grad_ref, dq_ref, pair_grad_ref = refs
    queries = q_ref[...]
    grads = grad_ref[...]
    lane = lax.broadcasted_iota(jnp.int32, queries.shape, 1) // HEAD_DIM
    zero = jnp.zeros((), queries.dtype)
    totals = lse_ref[...].T
    weighted = (grads.astype(jnp.float32) * out_ref[...].astype(jnp.float32)).T
    halves, grad_halves, total_rows, delta_rows, grad_queries = [], [], [], [], []
    for side in range(2):
        halves.append((jnp.where(lane == side, queries, zero) * attn_scale).astype(jnp.bfloat16))
        grad_halves.append(jnp.where(lane == side, grads, zero))
        total_rows.append(totals[side * HEAD_DIM : side * HEAD_DIM + 1, :])
        delta_rows.append(
            jnp.sum(weighted[side * HEAD_DIM : (side + 1) * HEAD_DIM, :], axis=0, keepdims=True)
        )
        grad_queries.append(jnp.zeros(queries.shape, jnp.float32))
    base = 0
    for pair_ref in pair_refs:
        key_step = min(pair_ref.shape[0], 512)
        for start in range(0, pair_ref.shape[0], key_step):
            here = pl.ds(start, key_step)
            rows = pl.ds(base + start, key_step)
            keys = pair_ref[here, :128]
            values = pair_ref[here, 128:]
            grad_keys = jnp.zeros(keys.shape, jnp.float32)
            grad_values = jnp.zeros(keys.shape, jnp.float32)
            for side in range(2):
                scores = dot_nt(keys, halves[side])
                probs = jnp.exp(scores - total_rows[side])
                if masked:
                    probs = jnp.where(key_pos[rows, :] <= query_pos[...], probs, 0.0)
                grad_probs = dot_nt(values, grad_halves[side])
                grad_scores = (probs * (grad_probs - delta_rows[side])).astype(jnp.bfloat16)
                grad_values += dot_nn(probs.astype(jnp.bfloat16), grad_halves[side])
                grad_keys += dot_nn(grad_scores, halves[side])
                grad_queries[side] += dot_tn(grad_scores, keys)
            pair_grad_ref[rows, :128] = grad_keys.astype(pair_grad_ref.dtype)
            pair_grad_ref[rows, 128:] = grad_values.astype(pair_grad_ref.dtype)
        base += pair_ref.shape[0]
    dq_ref[...] = (jnp.where(lane == 0, grad_queries[0], grad_queries[1]) * attn_scale).astype(
        dq_ref.dtype
    )


def attend_back(queries, pairs, positions, mixed_rows, log_total, grad_mixed):
    rows, keys = queries.shape[0], sum(part.shape[0] for part in pairs)
    extra, extra_specs = (), []
    if positions is not None:
        query_pos, key_pos = positions
        extra = (query_pos.reshape(1, rows), key_pos.reshape(keys, 1))
        extra_specs = [
            pl.BlockSpec((1, rows), lambda j: (0, 0)),
            pl.BlockSpec((keys, 1), lambda j: (0, 0)),
        ]
    row_spec = pl.BlockSpec((rows, 128), lambda j: (0, j))
    return pl.pallas_call(
        lambda *refs: attend_back_kernel(positions is not None, len(pairs), *refs),
        grid=(D // 128,),
        in_specs=extra_specs
        + [row_spec]
        + [pl.BlockSpec((part.shape[0], 256), lambda j: (0, j)) for part in pairs]
        + [row_spec] * 3,
        out_specs=[row_spec, pl.BlockSpec((keys, 256), lambda j: (0, j))],
        out_shape=[
            jax.ShapeDtypeStruct((rows, D), jnp.bfloat16),
            jax.ShapeDtypeStruct((keys, 2 * D), jnp.bfloat16),
        ],
        compiler_params=pltpu.CompilerParams(vmem_limit_bytes=KERNEL_VMEM),
        cost_estimate=SMALL_COST,
    )(*extra, queries, *pairs, mixed_rows, log_total, grad_mixed)


def head_kernel(vocab, tile, used_ref, rows_ref, table_ref, mixed_ref, exp_ref, stats_ref, logits_ref):
    step = pl.program_id(0)
    padded = table_ref.shape[1]
    shape = (rows_ref.shape[0], 128)
    lane = lax.broadcasted_iota(jnp.int32, shape, 1)

    @pl.when(used_ref[step] == 0)
    def _():
        mixed_ref[...] = jnp.zeros(mixed_ref.shape, mixed_ref.dtype)
        exp_ref[...] = jnp.zeros(exp_ref.shape, exp_ref.dtype)
        stats_ref[...] = jnp.where(lane == 1, 1.0, 0.0)

    @pl.when(used_ref[step] != 0)
    def _():
        rows = rows_ref[...]
        top = jnp.full((rows.shape[0], 1), -jnp.inf, jnp.float32)
        for start in range(0, padded, tile):
            logits = dot_nn(rows, table_ref[:, start : start + tile])
            if start + tile > vocab:
                column = start + lax.broadcasted_iota(jnp.int32, logits.shape, 1)
                logits = jnp.where(column < vocab, logits, -jnp.inf)
            logits_ref[:, start : start + tile] = logits
            top = jnp.maximum(top, jnp.max(logits, axis=1, keepdims=True))
        summed = jnp.zeros((rows.shape[0], 1), jnp.float32)
        mixed = jnp.zeros(mixed_ref.shape, jnp.float32)
        for start in range(0, padded, tile):
            exponent = jnp.exp(logits_ref[:, start : start + tile] - top)
            summed += jnp.sum(exponent, axis=1, keepdims=True)
            low = exponent.astype(jnp.bfloat16)
            exp_ref[:, start : start + tile] = low
            mixed += dot_nt(low, table_ref[:, start : start + tile])
        mixed_ref[...] = mixed
        stats_ref[...] = jnp.where(lane == 0, top, summed)


def head_forward(rows_all, table, used, vocab, block_rows, tile):
    rows, padded = rows_all.shape[0], table.shape[1]
    return pl.pallas_call(
        lambda *refs: head_kernel(vocab, tile, *refs),
        grid_spec=pltpu.PrefetchScalarGridSpec(
            num_scalar_prefetch=1,
            grid=(rows // block_rows,),
            in_specs=[
                pl.BlockSpec((block_rows, D), lambda i, used: (i, 0)),
                pl.BlockSpec((D, padded), lambda i, used: (0, 0), pipeline_mode=pl.Buffered(1)),
            ],
            out_specs=[
                pl.BlockSpec((block_rows, D), lambda i, used: (i, 0)),
                pl.BlockSpec((block_rows, padded), lambda i, used: (i, 0)),
                pl.BlockSpec((block_rows, 128), lambda i, used: (i, 0)),
            ],
            scratch_shapes=[pltpu.VMEM((block_rows, padded), jnp.float32)],
        ),
        out_shape=[
            jax.ShapeDtypeStruct((rows, D), jnp.float32),
            jax.ShapeDtypeStruct((rows, padded), jnp.bfloat16),
            jax.ShapeDtypeStruct((rows, 128), jnp.float32),
        ],
        compiler_params=pltpu.CompilerParams(vmem_limit_bytes=KERNEL_VMEM),
        cost_estimate=SMALL_COST,
    )(used, rows_all, table)


def table_grad_kernel(tile, used_ref, rows_ref, exp_ref, info_ref, grad_ref, total_ref):
    step = pl.program_id(0)

    @pl.when(step == 0)
    def _():
        total_ref[...] = jnp.zeros(total_ref.shape, total_ref.dtype)

    @pl.when(used_ref[step] != 0)
    def _():
        rows = rows_ref[...]
        scale = info_ref[:, 0:1]
        weight = info_ref[:, 1:2]
        target = info_ref[:, 2:3].astype(jnp.int32)
        for start in range(0, exp_ref.shape[1], tile):
            column = start + lax.broadcasted_iota(jnp.int32, (exp_ref.shape[0], tile), 1)
            probs = exp_ref[:, start : start + tile].astype(jnp.float32) * scale
            hits = jnp.where(column == target, weight, 0.0)
            grad_logits = (probs - hits).astype(jnp.bfloat16)
            total_ref[:, start : start + tile] += dot_tn(rows, grad_logits)

    @pl.when(step == pl.num_programs(0) - 1)
    def _():
        grad_ref[...] = total_ref[...].astype(grad_ref.dtype)


def table_grad(rows_all, exps, info, used, block_rows, tile):
    rows, padded = exps.shape
    return pl.pallas_call(
        lambda *refs: table_grad_kernel(tile, *refs),
        grid_spec=pltpu.PrefetchScalarGridSpec(
            num_scalar_prefetch=1,
            grid=(rows // block_rows,),
            in_specs=[
                pl.BlockSpec((block_rows, D), lambda i, used: (i, 0)),
                pl.BlockSpec((block_rows, padded), lambda i, used: (i, 0)),
                pl.BlockSpec((block_rows, 128), lambda i, used: (i, 0)),
            ],
            out_specs=pl.BlockSpec((D, padded), lambda i, used: (0, 0), pipeline_mode=pl.Buffered(1)),
            scratch_shapes=[pltpu.VMEM((D, padded), jnp.float32)],
        ),
        out_shape=jax.ShapeDtypeStruct((D, padded), jnp.bfloat16),
        compiler_params=pltpu.CompilerParams(vmem_limit_bytes=KERNEL_VMEM),
        cost_estimate=SMALL_COST,
    )(used, rows_all, exps, info)


def row_sums_kernel(step_rows, ids_ref, rows_ref, sums_ref):
    width, height = sums_ref.shape
    total = jnp.zeros((height, width), jnp.float32)
    for start in range(0, rows_ref.shape[1], step_rows):
        place = pl.program_id(0) * height + lax.broadcasted_iota(
            jnp.int32, (height, step_rows), 0
        )
        hits = jnp.where(place == ids_ref[:, start : start + step_rows], 1.0, 0.0)
        total += dot_nt(hits.astype(jnp.bfloat16), rows_ref[:, start : start + step_rows])
    sums_ref[...] = total.T


def row_sums(ids, rows, places):
    width, count = rows.shape
    height = 640 if places % 640 == 0 else 256
    return pl.pallas_call(
        lambda *refs: row_sums_kernel(1024, *refs),
        grid=(places // height,),
        in_specs=[
            pl.BlockSpec((1, count), lambda i: (0, 0)),
            pl.BlockSpec((width, count), lambda i: (0, 0), pipeline_mode=pl.Buffered(1)),
        ],
        out_specs=pl.BlockSpec((width, height), lambda i: (0, i)),
        out_shape=jax.ShapeDtypeStruct((width, places), jnp.float32),
        compiler_params=pltpu.CompilerParams(vmem_limit_bytes=KERNEL_VMEM),
        cost_estimate=SMALL_COST,
    )(ids.reshape(1, count), rows)


FF = 2048
POS = 256
TGT = 1024
BW = 128
BLOCKS = 174
EXTENTS = [D, 3 * D, D, 2 * FF, FF, 3 * D, D, D, 2 * D, D, 2 * FF, FF]
GATHERS = [[0, 1], [5, 6, 7, 8], [9, 10, 11]]
PERMUTED = [2, 3, 4]
SMALL_ROWS = 2 * POS + 8

norm_eps = 1e-06
clip_limit = 0.02
stat_decay = 0.5
rate_shampoo = 0.02
rate_adam = 0.5
beta_first = 0.9
beta_second = 0.95
adam_eps = 1e-08
weight_decay = 0.01
BOTH = ("wide", "narrow")


def block_order():
    order, offset = [], 0
    for number, extent in enumerate(EXTENTS):
        blocks = list(range(offset, offset + extent // BW))
        pairs = D // BW
        if number in (1, 5, 8):
            keys, values = blocks[-2 * pairs : -pairs], blocks[-pairs:]
            blocks = blocks[: -2 * pairs] + [b for both in zip(keys, values) for b in both]
        order += blocks
        offset += extent // BW
    return order


def rms_norm(values, gain_vec):
    return (
        values * lax.rsqrt(jnp.mean(values * values, axis=-1, keepdims=True) + norm_eps) * gain_vec
    )


def norm_back(values, gain_vec, grad_out):
    _, pullback = jax.vjp(rms_norm, values, gain_vec)
    return pullback(grad_out)


def low(values):
    return values.astype(jnp.bfloat16)


def gated_unit(gate_up):
    return jax.nn.gelu(gate_up[:, :FF], approximate=True) * gate_up[:, FF:]


def swap(values, bit):
    count = lax.axis_size("wide")
    return lax.ppermute(values, "wide", [(w, w ^ bit) for w in range(count)])


def shift(values, step):
    count = lax.axis_size("narrow")
    return lax.ppermute(values, "narrow", [(i, (i + step) % count) for i in range(count)])


def wide_bits():
    return lax.axis_size("wide").bit_length() - 1


def bit_value(level):
    return (lax.axis_index("wide") >> level) & 1


def gather_wide(values, order):
    bits = wide_bits()
    whole = join_wide(values.reshape((1,) * bits + values.shape), order)
    return whole.reshape((1 << bits,) + values.shape)


def split_orders():
    upper = list(range(1, wide_bits()))
    return upper, upper[::-1]


def gather_wide_fast(values):
    first, second = split_orders()
    half = values.shape[-1] // 2
    return jnp.concatenate(
        [gather_wide(values[..., :half], first + [0]), gather_wide(values[..., half:], second + [0])],
        axis=-1,
    )


def in_three(value):
    parts = []
    for _ in range(3):
        part = lax.reduce_precision(value, 8, 7)
        parts.append(low(part))
        value = value - part
    return parts


def tie(*values):
    return lax.optimization_barrier(values)


def from_narrow(rows):
    count = lax.axis_size("narrow")
    ahead = [rows] + [shift(rows, -step) for step in range(1, count)]
    start = (count - lax.axis_index("narrow")) % count
    return lax.dynamic_slice_in_dim(jnp.stack(ahead + ahead), start, count, axis=0)


def join(whole, other, level):
    axis = wide_bits() - 1 - level
    return jnp.where(
        bit_value(level) == 1,
        jnp.concatenate([other, whole], axis=axis),
        jnp.concatenate([whole, other], axis=axis),
    )


def join_wide(whole, order):
    for level in order:
        whole = join(whole, swap(whole, 1 << level), level)
    return whole


class Flow:
    def __init__(self, stages):
        self.stages, self.result, self.values = stages, None, None
        self.pull(None)

    def pull(self, values):
        try:
            self.values = self.stages.send(values)
        except StopIteration as end:
            self.result, self.values = end.value, None

    def drain(self):
        while self.values is not None:
            self.pull(self.values)
        return self.result


def step(main, *flows):
    for _ in range(2):
        live = [flow for flow in flows if flow.values is not None]
        main, values = lax.optimization_barrier((main, [flow.values for flow in live]))
        for flow, tied in zip(live, values):
            flow.pull(tied)
    return main


def scatter_flow(factors, extra=None):
    bits = wide_bits()
    count = lax.axis_size("narrow")
    here = lax.axis_index("narrow")
    pairs = 1 << (bits - 1)
    low_bit = bit_value(0)

    def products(side, got):
        results, offset = [], 0
        for left, right in factors:
            split = left.reshape(left.shape[0], pairs, 2, -1)
            chosen = lax.dynamic_index_in_dim(split, side, 2, keepdims=False)
            result = dot_tn(chosen.reshape(left.shape[0], -1), right)
            if got is not None:
                result = result + got[:, offset : offset + right.shape[1]].astype(jnp.float32)
            if extra is not None and extra[0] == offset:
                split = extra[1].reshape(pairs, 2, -1, right.shape[1])
                chosen = lax.dynamic_index_in_dim(split, side, 1, keepdims=False)
                result = result + chosen.reshape(result.shape)
            offset += right.shape[1]
            results.append(low(result))
        return jnp.concatenate(results, axis=1)

    yield []
    (sent,) = yield [products(1 - low_bit, None)]
    (got,) = yield [swap(sent, 1)]
    mine = products(low_bit, got)
    middle = mine.shape[1] // 256 * 128
    orders = split_orders()
    wholes = [
        part.reshape((2,) * (bits - 1) + (-1, part.shape[1]))
        for part in (mine[:, :middle], mine[:, middle:])
    ]
    for number in range(bits - 1):
        levels = [order[number] for order in orders]
        theirs = [
            lax.dynamic_index_in_dim(whole, 1 - bit_value(level), bits - 1 - level, keepdims=True)
            for whole, level in zip(wholes, levels)
        ]
        tied = yield wholes + theirs
        wholes, theirs = tied[:2], tied[2:]
        got = yield [swap(part, 1 << level) for part, level in zip(theirs, levels)]
        wholes = [
            low(
                lax.dynamic_index_in_dim(
                    whole, bit_value(level), bits - 1 - level, keepdims=True
                ).astype(jnp.float32)
                + part.astype(jnp.float32)
            )
            for whole, part, level in zip(wholes, got, levels)
        ]
    rows = jnp.concatenate([whole.reshape(count, -1, whole.shape[-1]) for whole in wholes], axis=-1)
    pieces = [
        lax.dynamic_index_in_dim(rows, (here + k) % count, 0, keepdims=False) for k in range(count)
    ]
    pieces = yield pieces
    got = yield [shift(pieces[k], k) for k in range(1, count)]
    total = pieces[0].astype(jnp.float32)
    for piece in got:
        total = total + piece.astype(jnp.float32)
    return low(total)


def ring_flow(parts):
    moving = parts[-1]
    yield []
    for part in parts[-2::-1]:
        (moving,) = yield [low(moving)]
        (moving,) = yield [shift(moving, 1)]
        moving = part.astype(jnp.float32) + moving.astype(jnp.float32)
    return moving


def table_flow(own):
    parts = [own]
    yield []
    for _ in range(lax.axis_size("narrow") - 1):
        (moving,) = yield [parts[-1]]
        (moving,) = yield [shift(moving, -1)]
        parts.append(moving)
    return parts


def keys_flow(rows):
    bit = lax.axis_size("narrow") // 2
    yield []
    while bit:
        (rows,) = yield [rows]
        rows, other = yield [rows, swap(rows, bit)]
        bit //= 2
        if bit:
            rows = jnp.concatenate([rows, other], axis=0)
    return [rows, other]


def return_flow(parts):
    bit = 1
    yield []
    while bit < lax.axis_size("narrow"):
        half = parts[0].shape[0] // 2
        sent = yield [part[half:] for part in parts]
        got = yield [swap(other, bit) for other in sent]
        parts = [
            low(part[:half].astype(jnp.float32) + other.astype(jnp.float32))
            for part, other in zip(parts, got)
        ]
        bit *= 2
    return parts[0]


def gather_flow(rows):
    bits = wide_bits()
    count = lax.axis_size("narrow")
    columns = rows.shape[1]
    middle = columns // 2
    yield []
    (rows,) = yield [rows]
    ahead = yield [rows] + [shift(rows, -k) for k in range(1, count)]
    start = (count - lax.axis_index("narrow")) % count
    stacked = lax.dynamic_slice_in_dim(jnp.stack(ahead + ahead), start, count, axis=0)
    stacked = stacked.reshape((1,) * bits + stacked.shape)
    parts = [stacked[..., :middle], stacked[..., middle:]]
    orders = split_orders()
    for number in range(bits - 1):
        parts = yield parts
        tied = yield parts + [swap(part, 1 << o[number]) for part, o in zip(parts, orders)]
        parts = [join(tied[k], tied[k + 2], orders[k][number]) for k in range(2)]
    (whole,) = yield [jnp.concatenate(parts, axis=-1)]
    whole, other = yield [whole, swap(whole, 1)]
    return join(whole, other, 0).reshape(-1, columns)


def group_offsets():
    offsets, bit = [0], lax.axis_size("narrow") // 2
    while bit:
        offsets = offsets + [o ^ bit for o in offsets]
        bit //= 2
    return offsets


def feed_forward(stream, gain_vec, w_in, w_back):
    normed = low(rms_norm(stream, gain_vec))
    gate_up = dot_nn(normed, w_in)
    hidden = low(gated_unit(gate_up))
    return (dot_nt(hidden, w_back), (normed, gate_up, hidden))


def adamw(param, moment, second, grad, step_count):
    moment = beta_first * moment + (1 - beta_first) * grad
    second = beta_second * second + (1 - beta_second) * grad * grad
    steps = step_count.astype(jnp.float32)
    m_hat = moment / (1 - jnp.power(beta_first, steps))
    v_hat = second / (1 - jnp.power(beta_second, steps))
    return (
        param - rate_adam * (m_hat / (jnp.sqrt(v_hat) + adam_eps) + weight_decay * param),
        moment,
        second,
    )


def shards(
    patches,
    patch_rows,
    patch_cols,
    input_ids,
    target_ids,
    target_lengths,
    loss_mask,
    master_slabs,
    left_stats,
    left_roots,
    right_stats,
    right_roots,
    block_slot,
    vocab_table,
    vocab_first,
    vocab_second,
    small_params,
    small_first,
    small_second,
    step_count,
):
    wide_count = lax.axis_size("wide")
    narrow_count = lax.axis_size("narrow")
    devices = wide_count * narrow_count
    screen_sets = wide_count // narrow_count
    wide_pos = lax.axis_index("wide")
    narrow_pos = lax.axis_index("narrow")
    member = wide_pos % narrow_count
    slot_total = block_slot.shape[0]
    own_count = master_slabs.shape[0]
    piece = D // devices
    slot_ids = block_slot[jnp.array(block_order())]
    enc_rows, dec_rows = patches.shape[0], input_ids.shape[0]
    vocab_rows, features = vocab_table.shape

    block_of_slot = (slot_ids[:, None] == jnp.arange(slot_total)[None, :]).astype(jnp.bfloat16)
    pieces = low(master_slabs).reshape(own_count, devices, piece, BW).transpose(1, 0, 2, 3)
    pieces = lax.all_to_all(pieces, BOTH, 0, 0)

    exchange = []
    for w in range(wide_count):
        for n in range(narrow_count):
            base = w // narrow_count * narrow_count
            exchange.append((w * narrow_count + n, (base + n) * narrow_count + w % narrow_count))
    slots = narrow_pos * dec_rows + jnp.arange(dec_rows)
    slot_mask = lax.dynamic_slice_in_dim(loss_mask[0], narrow_pos * dec_rows, dec_rows)
    slot_counted = ((slots < target_lengths[0]) & (slot_mask == 1)).astype(jnp.int32)
    whole_ids = lax.ppermute(
        jnp.concatenate([patch_rows, patch_cols, input_ids, target_ids, slot_counted]),
        BOTH,
        exchange,
    )
    rows_ids, cols_ids = whole_ids[:enc_rows], whole_ids[enc_rows : 2 * enc_rows]
    token_ids = whole_ids[2 * enc_rows :].reshape(3, dec_rows)
    every_token = from_narrow(token_ids)
    every_token = every_token.reshape((1,) * wide_bits() + every_token.shape)
    every_token = join_wide(every_token, split_orders()[0] + [0])
    every_token = every_token.reshape(wide_count, narrow_count, 3, dec_rows)
    pieces, patches, every_token = tie(pieces, patches, every_token)
    layer_tokens = lax.dynamic_index_in_dim(every_token, narrow_pos, 1, keepdims=False)
    layer_targets = layer_tokens[:, 1].reshape(-1)
    patches = lax.ppermute(patches, BOTH, exchange)
    ordered = low(dot_nn(block_of_slot, pieces.reshape(slot_total, piece * BW)))
    row_shard = ordered.reshape(BLOCKS, piece, BW).transpose(1, 0, 2).reshape(piece, BLOCKS * BW)
    weights = [None] * len(EXTENTS)

    def shard_of(numbers):
        begin = sum(EXTENTS[: numbers[0]])
        return row_shard[:, begin : begin + sum(EXTENTS[n] for n in numbers)]

    def take(numbers, group):
        offset = 0
        for n in numbers:
            weights[n] = group[:, offset : offset + EXTENTS[n]]
            offset += EXTENTS[n]

    for numbers in GATHERS:
        take(numbers, lax.all_gather(shard_of(numbers), BOTH, axis=0, tiled=True))
    flow_weights = Flow(gather_flow(shard_of(PERMUTED)))

    padded = -(-vocab_rows // 256) * 256
    table_low = low(vocab_table)
    columns = jnp.arange(vocab_rows)
    vocab_start = wide_pos * vocab_rows
    flat_inputs = every_token[:, :, 0].reshape(-1) - vocab_start
    flat_targets = every_token[:, :, 1].reshape(-1) - vocab_start

    def looked_up(ids):
        onehot = (ids[:, None] == columns[None, :]).astype(jnp.bfloat16)
        found = low(dot_nn(onehot, table_low))
        return found.reshape(wide_count, narrow_count * dec_rows, features)

    def delivered(found):
        found = low(jnp.sum(found.astype(jnp.float32), axis=0))
        found = lax.all_to_all(found.reshape(narrow_count, dec_rows, features), "narrow", 0, 0)
        return found.transpose(1, 0, 2).reshape(dec_rows, D).astype(jnp.float32)

    flat_inputs = step(flat_inputs, flow_weights)
    found_inputs = looked_up(flat_inputs)
    found_inputs = step(found_inputs, flow_weights)
    found_inputs = lax.all_to_all(found_inputs, "wide", 0, 0)
    flow_table = Flow(table_flow(jnp.pad(table_low.T, ((0, 0), (0, padded - vocab_rows)))))

    gain_rows = small_params[2 * POS :]
    picked = jnp.concatenate(
        [
            rows_ids[:, None] == jnp.arange(POS)[None, :],
            cols_ids[:, None] == jnp.arange(POS)[None, :],
        ],
        axis=1,
    ).astype(jnp.bfloat16)
    tables = small_params[: 2 * POS]
    tables_high = low(tables)
    tables_rest = low(tables - tables_high.astype(jnp.float32))
    enc_zero = (
        dot_nn(patches, weights[0])
        + gain_rows[7]
        + dot_nn(picked, tables_high)
        + dot_nn(picked, tables_rest)
    )
    enc_zero = step(enc_zero, flow_weights)
    enc_normed = low(rms_norm(enc_zero, gain_rows[0]))
    enc_mix = low(dot_nn(enc_normed, weights[1]))
    enc_query = enc_mix[:, :D]
    flow_keys = Flow(keys_flow(enc_mix[:, D:]))
    enc_query, flat_targets, found_inputs = step(
        (enc_query, flat_targets, found_inputs), flow_keys, flow_table
    )
    found_targets = looked_up(flat_targets)
    dec_zero = delivered(found_inputs)
    enc_query, found_targets, dec_zero = step(
        (enc_query, found_targets, dec_zero), flow_keys, flow_weights, flow_table
    )
    found_targets = lax.all_to_all(found_targets, "wide", 0, 0)
    enc_query = step(enc_query, flow_keys)
    enc_keys = flow_keys.drain()
    enc_mixed, enc_total = attend(enc_query, enc_keys, None)
    enc_mixed = step(enc_mixed, flow_weights)
    take(PERMUTED, flow_weights.drain())
    counted = every_token[:, :, 2].astype(jnp.float32)
    tokens_counted = jnp.maximum(jnp.sum(counted), 1.0)
    row_counted = layer_tokens[:, 2].reshape(-1).astype(jnp.float32)
    own_counted = lax.dynamic_slice_in_dim(row_counted, wide_pos * dec_rows, dec_rows)

    enc_one = enc_zero + dot_nn(enc_mixed, weights[2])
    enc_fnormed = low(rms_norm(enc_one, gain_rows[1]))
    enc_gate = dot_nn(enc_fnormed, weights[3])
    enc_hidden = low(gated_unit(enc_gate))
    enc_ffn = (enc_fnormed, enc_gate, enc_hidden)

    query_pos = (member * dec_rows + jnp.arange(dec_rows)).astype(jnp.int32)
    key_pos = jnp.concatenate(
        [(member ^ offset) * dec_rows + jnp.arange(dec_rows) for offset in group_offsets()]
    ).astype(jnp.int32)
    causal = (query_pos, key_pos)
    dec_normed = low(rms_norm(dec_zero, gain_rows[3]))
    dec_mix = low(dot_nn(dec_normed, weights[5]))
    flow_keys = Flow(keys_flow(dec_mix[:, D:]))
    enc_hidden, found_targets = step((enc_hidden, found_targets), flow_keys, flow_table)
    enc_two = enc_one + dot_nt(enc_hidden, weights[4])
    encoded = low(rms_norm(enc_two, gain_rows[2]))
    flow_cross = Flow(keys_flow(low(dot_nn(encoded, weights[8]))))
    dec_query = dec_mix[:, :D]
    dec_query, found_targets = step((dec_query, found_targets), flow_keys, flow_cross)
    target_rows = delivered(found_targets)
    dec_query = step(dec_query, flow_keys)
    self_keys = flow_keys.drain()
    self_mixed, self_total = attend(dec_query, self_keys, causal)
    dec_one = dec_zero + dot_nn(self_mixed, weights[6])
    cross_normed = low(rms_norm(dec_one, gain_rows[4]))
    cross_query = low(dot_nn(cross_normed, weights[7]))
    cross_query, target_rows = step((cross_query, target_rows), flow_cross)
    cross_query = step(cross_query, flow_cross)
    cross_keys = flow_cross.drain()
    cross_mixed, cross_total = attend(cross_query, cross_keys, None)
    dec_two = dec_one + dot_nn(cross_mixed, weights[9])
    branch, dec_ffn = feed_forward(dec_two, gain_rows[5], weights[10], weights[11])
    dec_three = dec_two + branch
    final = low(rms_norm(dec_three, gain_rows[6]) * D ** (-0.5))
    table = jnp.concatenate(flow_table.drain(), axis=0)

    rotated = lax.dynamic_slice_in_dim(
        jnp.concatenate([final, final], axis=1), narrow_pos * features, D, axis=1
    )
    rows_all = gather_wide_fast(rotated).reshape(-1, D)
    total_rows = rows_all.shape[0]
    block_rows = 256
    used = jnp.any(row_counted.reshape(-1, block_rows) != 0, axis=1).astype(jnp.int32)
    tile = padded // 5 if padded % 640 == 0 else 256
    mixed, exps, stats = head_forward(rows_all, table, used, vocab_rows, block_rows, tile)
    top_part, summed_part = stats[:, 0], stats[:, 1]
    stats_all = lax.all_gather(jnp.stack([top_part, summed_part]), "wide", axis=0)
    top_logit = jnp.max(stats_all[:, 0], axis=0)
    summed = jnp.sum(stats_all[:, 1] * jnp.exp(stats_all[:, 0] - top_logit), axis=0)
    log_total = top_logit + jnp.log(summed)
    row_weight = row_counted / tokens_counted
    scale = row_weight * jnp.exp(top_part - log_total)
    grad_rows = low(mixed * scale[:, None]).reshape(wide_count, dec_rows, D)
    grad_rows = lax.all_to_all(grad_rows, "wide", 0, 0)
    own_weight = own_counted / tokens_counted
    target_logit = jnp.sum(final.astype(jnp.float32) * target_rows, axis=1)
    own_total = lax.dynamic_slice_in_dim(log_total, wide_pos * dec_rows, dec_rows)
    loss_local = jnp.sum(own_counted * (own_total - target_logit))
    target_cols = (layer_targets - vocab_start).astype(jnp.float32)
    info = jnp.concatenate(
        [
            jnp.stack([scale, row_weight, target_cols], axis=1),
            jnp.zeros((total_rows, 125), jnp.float32),
        ],
        axis=1,
    )
    grad_table = table_grad(rows_all, exps, info, used, block_rows, tile)
    grad_parts = grad_table.reshape(narrow_count, features, padded)
    ring = Flow(ring_flow([grad_parts[k] for k in range(narrow_count)]))
    grad_rows = step(grad_rows, ring)
    grad_back = jnp.sum(grad_rows.astype(jnp.float32), axis=0)
    grad_back = lax.dynamic_slice_in_dim(
        jnp.concatenate([grad_back, grad_back], axis=1), (D - narrow_pos * features) % D, D, axis=1
    )
    grad_final = grad_back - own_weight[:, None] * target_rows

    grad_three, gain_final = norm_back(dec_three, gain_rows[6], grad_final * D ** (-0.5))
    low_three = low(grad_three)
    _, pullback = jax.vjp(gated_unit, dec_ffn[1])
    grad_gate = low(pullback(dot_nn(low_three, weights[11]))[0])
    flow_dffn = Flow(scatter_flow([(dec_ffn[0], grad_gate), (low_three, dec_ffn[2])]))
    grad_gate = step(grad_gate, flow_dffn)
    grad_two, gain_dffn = norm_back(dec_two, gain_rows[5], dot_nt(grad_gate, weights[10]))
    grad_two = grad_two + grad_three
    low_two = low(grad_two)
    grad_mixed = low(dot_nt(low_two, weights[9]))
    grad_mixed = step(grad_mixed, flow_dffn)
    grad_cq, grad_pair = attend_back(
        cross_query, cross_keys, None, cross_mixed, cross_total, grad_mixed
    )
    flow_cross = Flow(return_flow([grad_pair]))
    grad_cq = step(grad_cq, flow_cross, ring)
    grad_one, gain_cross = norm_back(dec_one, gain_rows[4], dot_nt(grad_cq, weights[7]))
    grad_one = grad_one + grad_two
    low_one = low(grad_one)
    grad_mixed = low(dot_nt(low_one, weights[6]))
    grad_mixed = step(grad_mixed, flow_cross)
    grad_sq, grad_pair = attend_back(
        dec_mix[:, :D], self_keys, causal, self_mixed, self_total, grad_mixed
    )
    flow_self = Flow(return_flow([grad_pair]))
    grad_sq = step(grad_sq, flow_self, flow_dffn)
    grad_sq = step(grad_sq, flow_self)
    grad_sq = step(grad_sq, flow_cross, ring)
    grad_ckv = flow_cross.drain()

    grad_two, gain_efinal = norm_back(enc_two, gain_rows[2], dot_nt(grad_ckv, weights[8]))
    low_etwo = low(grad_two)
    _, pullback = jax.vjp(gated_unit, enc_ffn[1])
    grad_gate = low(pullback(dot_nn(low_etwo, weights[4]))[0])
    grad_gate = step(grad_gate, flow_self, flow_dffn)
    grad_smix = jnp.concatenate([grad_sq, flow_self.drain()], axis=1)
    grad_zero, gain_self = norm_back(dec_zero, gain_rows[3], dot_nt(grad_smix, weights[5]))
    grad_tokens = low(grad_zero + grad_one)
    sent = grad_tokens.reshape(dec_rows, narrow_count, features).transpose(1, 0, 2)
    sent = lax.all_to_all(sent, "narrow", 0, 0).reshape(narrow_count * dec_rows, features)
    flow_dattn = Flow(
        scatter_flow(
            [
                (dec_normed, grad_smix),
                (self_mixed, low_one),
                (cross_normed, grad_cq),
                (encoded, grad_ckv),
                (cross_mixed, low_two),
            ]
        )
    )
    flow_effn = Flow(scatter_flow([(enc_ffn[0], grad_gate), (low_etwo, enc_ffn[2])]))
    grad_gate = step(grad_gate, flow_dattn, flow_effn, ring)
    grad_one, gain_effn = norm_back(enc_one, gain_rows[1], dot_nt(grad_gate, weights[3]))
    grad_one = grad_one + grad_two
    low_eone = low(grad_one)
    grad_mixed = low(dot_nt(low_eone, weights[2]))
    grad_mixed = step(grad_mixed, flow_dattn, flow_effn)
    grad_mixed, sent = step((grad_mixed, sent), flow_dffn)
    sent = lax.all_gather(sent, "wide", axis=0, tiled=True)
    grad_eq, grad_pair = attend_back(
        enc_mix[:, :D], enc_keys, None, enc_mixed, enc_total, grad_mixed
    )
    grad_eq = step(grad_eq, flow_dattn, flow_effn)
    flow_enc = Flow(return_flow([grad_pair]))
    grad_eq = step(grad_eq, flow_enc)
    grad_eq, sent = step((grad_eq, sent), flow_enc)
    looked_grad = row_sums(flat_inputs, sent.T, padded)
    grad_eq, looked_grad = step((grad_eq, looked_grad), flow_enc)
    grad_eq, looked_grad = step((grad_eq, looked_grad), flow_dattn, flow_effn)
    grad_emix = jnp.concatenate([grad_eq, flow_enc.drain()], axis=1)
    grad_zero, gain_eattn = norm_back(enc_zero, gain_rows[0], dot_nt(grad_emix, weights[1]))
    grad_zero = grad_zero + grad_one
    low_zero = low(grad_zero)
    gains = [gain_eattn, gain_effn, gain_efinal, gain_self, gain_cross, gain_dffn, gain_final]
    width = -(-SMALL_ROWS // BW) * BW
    gains = jnp.pad(jnp.stack(gains, axis=1), ((0, 0), (2 * POS, width - 2 * POS - 7)))
    marks = (jnp.arange(width) == SMALL_ROWS - 1).astype(jnp.bfloat16)
    small_factor = marks[None, :] + jnp.pad(picked, ((0, 0), (0, width - 2 * POS)))
    flow_eattn = Flow(
        scatter_flow(
            [
                (patches, low_zero),
                (enc_normed, grad_emix),
                (enc_mixed, low_eone),
                (low_zero, small_factor),
            ],
            (5 * D, gains),
        )
    )
    looked_grad = step(looked_grad, flow_eattn)
    vocab_grad = (ring.drain() + looked_grad)[:, :vocab_rows].T
    vocab_square = jnp.sum(vocab_grad * vocab_grad)
    vocab_square = step(vocab_square, flow_eattn)
    vocab_square = step(vocab_square, flow_dattn, flow_effn)
    vocab_square = step(vocab_square, flow_eattn)
    vocab_square = step(vocab_square, flow_eattn)
    shard_dffn, shard_dattn = flow_dffn.drain(), flow_dattn.drain()
    shard_effn, shard_eattn = flow_effn.drain(), flow_eattn.drain()

    projection = shard_eattn[:, : 5 * D]
    small_shard = shard_eattn[:, 5 * D : 5 * D + SMALL_ROWS].astype(jnp.float32)
    grads = jnp.concatenate([projection, shard_effn, shard_dattn, shard_dffn], axis=1)
    partial_square = (
        jnp.sum(jnp.square(grads.astype(jnp.float32)))
        + vocab_square
        + jnp.sum(small_shard * small_shard)
    )
    scalars = jnp.stack(in_three(partial_square) + in_three(loss_local))
    scalars = jnp.pad(scalars[None, :], ((0, 0), (0, SMALL_ROWS - 6)))
    slotted = grads.reshape(piece, BLOCKS, BW).transpose(1, 0, 2).reshape(BLOCKS, piece * BW)
    slotted = low(dot_tn(block_of_slot, slotted)).reshape(devices, own_count, piece, BW)
    small_shard, scalars, slotted = tie(small_shard, scalars, slotted)
    slab = lax.all_to_all(slotted, BOTH, 0, 0).transpose(1, 0, 2, 3).reshape(own_count, D, BW)
    shared = from_narrow(jnp.concatenate([low(small_shard), scalars], axis=0))
    shared = join_wide(shared.reshape((1,) * wide_bits() + shared.shape), split_orders()[0] + [0])
    shared = shared.reshape(devices, piece + 1, SMALL_ROWS).astype(jnp.float32)
    small_grad = shared[:, :piece].reshape(D, SMALL_ROWS).T
    total_square = jnp.sum(shared[:, piece, :3])
    loss_sum = jnp.sum(shared[:, piece, 3:6])

    grad_norm = jnp.sqrt(total_square)
    factor = jnp.minimum(1.0, clip_limit / (grad_norm + 1e-06))
    kept = (1 - stat_decay) * factor * factor
    slab_grad = slab.astype(jnp.float32) * factor
    left_new = stat_decay * left_stats + kept * jnp.einsum(
        "sik,sjk->sij", slab, slab, preferred_element_type=jnp.float32
    )
    right_new = stat_decay * right_stats + kept * jnp.einsum(
        "ski,skj->sij", slab, slab, preferred_element_type=jnp.float32
    )
    rooted = jnp.einsum("sij,sjk->sik", low(left_roots), slab, preferred_element_type=jnp.float32)
    precond = factor * jnp.einsum(
        "sij,sjk->sik", rooted, right_roots, precision=lax.Precision.HIGHEST
    )
    scale_back = lax.rsqrt(jnp.mean(precond * precond, axis=(1, 2), keepdims=True) + norm_eps)
    master_new = master_slabs - rate_shampoo * precond * scale_back
    vocab_new, vocab_first_new, vocab_second_new = adamw(
        vocab_table, vocab_first, vocab_second, vocab_grad * factor, step_count
    )
    small_new, small_first_new, small_second_new = adamw(
        small_params, small_first, small_second, small_grad * factor, step_count
    )
    return (
        loss_sum,
        tokens_counted,
        master_new,
        master_new.astype(jnp.bfloat16),
        slab_grad,
        left_new,
        right_new,
        vocab_new,
        vocab_new.astype(jnp.bfloat16),
        vocab_first_new,
        vocab_second_new,
        small_new,
        small_first_new,
        small_second_new,
        grad_norm,
    )


def solution(mesh):
    in_specs = (
        P(("wide", "narrow"), None),
        P(("wide", "narrow")),
        P(("wide", "narrow")),
        P(("wide", "narrow")),
        P(("wide", "narrow")),
        P("wide"),
        P("wide", None),
        P(("wide", "narrow"), None, None),
        P(("wide", "narrow"), None, None),
        P(("wide", "narrow"), None, None),
        P(("wide", "narrow"), None, None),
        P(("wide", "narrow"), None, None),
        P(),
        P("wide", "narrow"),
        P("wide", "narrow"),
        P("wide", "narrow"),
        P(),
        P(),
        P(),
        P(),
    )
    out_specs = (
        P(),
        P(),
        P(("wide", "narrow"), None, None),
        P(("wide", "narrow"), None, None),
        P(("wide", "narrow"), None, None),
        P(("wide", "narrow"), None, None),
        P(("wide", "narrow"), None, None),
        P("wide", "narrow"),
        P("wide", "narrow"),
        P("wide", "narrow"),
        P("wide", "narrow"),
        P(),
        P(),
        P(),
        P(),
    )
    return jax.shard_map(shards, mesh=mesh, in_specs=in_specs, out_specs=out_specs, check_vma=False)
```
